32 devices in a mesh: dp: 8 (over y, x, core), tp: 4 (over z).
Axes of the slice: x: 2, y: 2, z: 4, core: 2. Of those that a mesh axis runs over, the one named last changes fastest.
Arguments:
- tokens: bfloat16 [25088, 768], P(('dp', 'tp')), may hold values from -6 to 6
- heights: int32 [8], P('dp'), may hold values from 43 to 56, as said below
- widths: int32 [8], P('dp'), may hold values from 15 to 56
- norm_gain: bfloat16 [2, 768], replicated, may hold values from 0.25 to 1.75
- norm_bias: bfloat16 [2, 768], replicated, may hold values from -1.796875 to 1.796875
- w_qkv: bfloat16 [3, 768, 768], P(None, None, 'tp'), may hold values from -0.21875 to 0.21875
- b_qv: bfloat16 [2, 768], P(None, 'tp'), may hold values from -1.796875 to 1.796875
- rel_pos: bfloat16 [2, 27, 64], replicated, may hold values from -0.8984375 to 0.8984375
- w_proj: bfloat16 [768, 768], P('tp'), may hold values from -1.75 to 1.75
- b_proj: bfloat16 [768], replicated, may hold values from -1.796875 to 1.796875
- w_fc1: bfloat16 [768, 3072], P(None, 'tp'), may hold values from -0.21875 to 0.21875
- b_fc1: bfloat16 [3072], P('tp'), may hold values from -1.796875 to 1.796875
- w_fc2: bfloat16 [3072, 768], P('tp'), may hold values from -0.21875 to 0.21875
- b_fc2: bfloat16 [768], replicated, may hold values from -1.796875 to 1.796875
- cotangent: bfloat16 [25088, 768], P(('dp', 'tp')), may hold values from -6 to 6
Outputs:
- out: bfloat16 [25088, 768], P(('dp', 'tp'))
- grad_tokens: float32 [25088, 768], P(('dp', 'tp'))
- grad_norm_gain: float32 [2, 768], replicated
- grad_norm_bias: float32 [2, 768], replicated
- grad_qkv: float32 [3, 768, 768], P(None, None, 'tp')
- grad_b_qv: float32 [2, 768], P(None, 'tp')
- grad_rel_pos: float32 [2, 27, 64], replicated
- grad_proj: float32 [768, 768], P('tp')
- grad_b_proj: float32 [768], replicated
- grad_fc1: float32 [768, 3072], P(None, 'tp')
- grad_b_fc1: float32 [3072], P('tp')
- grad_fc2: float32 [3072, 768], P('tp')
- grad_b_fc2: float32 [768], replicated
The draws below stay inside these ranges and needn't reach their ends.
Inputs may be any that keep to these rules, and one draw needn't show every extreme that they name: `heights`: patch rows of each image; the last row of windows always holds patches.
All inputs are finite; a program needn't handle non-finite values.
Results may differ from the reference program's by a relative error of at most 0.018.
Values may be sent and summed in bfloat16 or wider, within the bound.
A program may use at most 192 MiB of HBM per device.

```python
import math
import jax
import jax.numpy as jnp
from jax import lax

D = 768
HEADS = 12
HEAD_DIM = 64
FF = 3072
WIN = 14
GRID = 4
IMAGES = 8
ROWS = 25088


def bounded_sizes(key, low_end, high_end):
    drawn = jax.random.randint(key, (IMAGES,), low_end, high_end + 1)
    ranking = jax.random.permutation(jax.random.fold_in(key, 7), IMAGES)
    drawn = drawn.at[ranking[0]].set(high_end)
    drawn = drawn.at[ranking[1]].set(low_end)
    return drawn.astype(jnp.int32)


def draw_heights(key, part):
    key = jax.random.fold_in(key, 11)
    return bounded_sizes(key, (GRID - 1) * WIN + 1, GRID * WIN)


def draw_widths(key, part):
    key = jax.random.fold_in(key, 12)
    return bounded_sizes(key, WIN + 1, GRID * WIN)


def level_of(own_key, extent, cuts, least, largest):
    gain, own = 1.0, jax.random.fold_in(own_key, 6)
    for dim, parts in cuts:
        steps = jnp.exp(jax.random.uniform(jax.random.fold_in(own, dim), (parts,), jnp.float32, least / len(cuts), largest / len(cuts)))
        gain = gain * jnp.repeat(steps, extent[dim] // parts).reshape([-1 if axis == dim else 1 for axis in range(len(extent))])
    return gain


def noise(rng, dims, deviation, most, cuts=(), kind=jnp.bfloat16):
    values = jax.random.normal(rng, dims, jnp.float32) * deviation
    if len(cuts) > 0:
        values = level_of(rng, dims, cuts, -0.22, 0.18) * values
    return jnp.clip(values, min=-most, max=most).astype(kind)


def setup_inputs(seed: int = 0) -> dict:
    streams_of = jax.random.split(jax.random.key(seed), 16)
    tokens = noise(streams_of[0], (ROWS, D), 1.0, 6.0, ((0, 32),))
    heights = draw_heights(jax.random.fold_in(streams_of[15], 71), 0)
    widths = draw_widths(jax.random.fold_in(streams_of[15], 71), 0)
    norm_gain = jnp.clip(1.0 + 0.15 * jax.random.normal(streams_of[3], (2, D), jnp.float32), 0.25, 1.75).astype(jnp.bfloat16)
    norm_bias = noise(streams_of[4], (2, D), 0.3, 1.796875)
    w_qkv = noise(streams_of[5], (3, D, D), D ** -0.5, 0.21875, ((2, 4),))
    b_qv = noise(streams_of[6], (2, D), 0.3, 1.796875, ((1, 4),))
    rel_pos = noise(streams_of[7], (2, 2 * WIN - 1, HEAD_DIM), 0.15, 0.8984375)
    w_proj = noise(streams_of[8], (D, D), (D // 64) ** -0.5, 1.75, ((0, 4),))
    b_proj = noise(streams_of[9], (D,), 0.3, 1.796875)
    w_fc1 = noise(streams_of[10], (D, FF), D ** -0.5, 0.21875, ((1, 4),))
    b_fc1 = noise(streams_of[11], (FF,), 0.3, 1.796875, ((0, 4),))
    w_fc2 = noise(streams_of[12], (FF, D), (FF // 4) ** -0.5, 0.21875, ((0, 4),))
    b_fc2 = noise(streams_of[13], (D,), 0.3, 1.796875)
    cotangent = noise(streams_of[14], (ROWS, D), 1.0, 6.0, ((0, 32),))
    return dict(tokens=tokens, heights=heights, widths=widths, norm_gain=norm_gain, norm_bias=norm_bias, w_qkv=w_qkv, b_qv=b_qv, rel_pos=rel_pos, w_proj=w_proj, b_proj=b_proj, w_fc1=w_fc1, b_fc1=b_fc1, w_fc2=w_fc2, b_fc2=b_fc2, cotangent=cotangent)


@jax.custom_vjp
def low(v):
    return lax.optimization_barrier(v.astype(jnp.bfloat16)).astype(jnp.float32)

@jax.custom_vjp
def low_back(v):
    return v

def low_keep(v):
    return (low(v), None)

def low_pass(kept, grad):
    return (grad,)

def back_keep(v):
    return (v, None)

def back_low(kept, grad):
    return (low(grad),)
low.defvjp(low_keep, low_pass)
low_back.defvjp(back_keep, back_low)
highest = lax.Precision.HIGHEST
neg_fill = -30000.0

def layer_norm(values, norm_gains, shifts):
    centre = lax.optimization_barrier(jnp.mean(values, axis=-1, keepdims=True))
    centred = values - centre
    spread = lax.optimization_barrier(jnp.mean(centred * centred, axis=-1, keepdims=True))
    return centred * lax.rsqrt(spread + 1e-06) * norm_gains + shifts

def valid_slots(height, breadth, start, slot_count):
    index = start + jnp.arange(slot_count, dtype=jnp.int32)
    window = index // (WIN * WIN)
    inside = index % (WIN * WIN)
    row_at = window // GRID * WIN + inside // WIN
    column_at = window % GRID * WIN + inside % WIN
    return (row_at < height) & (column_at < breadth)

def offset_onehot():
    offsets = jnp.arange(WIN, dtype=jnp.int32)[:, None] - jnp.arange(WIN, dtype=jnp.int32)[None, :] + (WIN - 1)
    return (offsets[:, :, None] == jnp.arange(2 * WIN - 1, dtype=jnp.int32)[None, None, :]).astype(jnp.float32)

def relative_tables(rel_table):
    return jnp.einsum('ykj,tjc->tykc', offset_onehot(), rel_table, precision=highest)

def window_block(windows):
    return 4 if windows % 4 == 0 else 2 if windows % 2 == 0 else 1

def window_scores(queries, key_rows, tables):
    leading = queries.shape[:2]
    grid_q = queries.reshape(leading + (WIN, WIN, HEAD_DIM))
    direct = jnp.einsum('nhqc,nhkc->nhqk', queries, key_rows, precision=highest) / math.sqrt(HEAD_DIM)
    along_h = jnp.einsum('nhyxc,ykc->nhyxk', grid_q, tables[0], precision=highest)
    along_w = jnp.einsum('nhyxc,xkc->nhyxk', grid_q, tables[1], precision=highest)
    combined = direct.reshape(leading + (WIN, WIN, WIN, WIN)) + along_h[..., :, None] + along_w[..., None, :]
    return combined.reshape(leading + (WIN * WIN, WIN * WIN))

def block_forward(params, patches, valid):
    norm_gains, shifts, qkv_weight, qv_bias, rel_table, proj_weight, proj_bias, fc1_weight, fc1_bias, fc2_weight, fc2_bias = params
    slot_count = patches.shape[0]
    normed = low(layer_norm(patches, norm_gains[0], shifts[0]))
    projected = jnp.einsum('rd,tde->tre', normed, qkv_weight, precision=highest)
    queries = low_back(low(projected[0] + qv_bias[0]))
    key_rows = low_back(low(projected[1]))
    values = low_back(low(projected[2] + qv_bias[1]))
    tables = relative_tables(rel_table)
    windows = slot_count // (WIN * WIN)
    per_block = window_block(windows)
    blocks = windows // per_block

    def to_heads(flat):
        return flat.reshape(blocks, per_block, WIN * WIN, HEADS, HEAD_DIM).transpose(0, 1, 3, 2, 4)

    def attend(pieces):
        q_block, k_block, v_block, keep_block = pieces
        scores = low_back(window_scores(q_block, k_block, tables))
        scores = jnp.where(keep_block[:, None, None, :], scores, neg_fill)
        attention = low(jax.nn.softmax(scores, axis=-1))
        return jnp.einsum('nhqk,nhkc->nhqc', attention, v_block, precision=highest)
    mixture = lax.map(jax.checkpoint(attend), (to_heads(queries), to_heads(key_rows), to_heads(values), valid.reshape(blocks, per_block, WIN * WIN)))
    mixture = low_back(low(mixture.transpose(0, 1, 3, 2, 4).reshape(slot_count, D)))
    branch = low_back(jnp.dot(mixture, proj_weight, precision=highest))
    masking = valid[:, None].astype(jnp.float32)
    middle = patches + masking * (branch + proj_bias)
    normed_two = low(layer_norm(middle, norm_gains[1], shifts[1]))
    before = low_back(jnp.dot(normed_two, fc1_weight, precision=highest) + fc1_bias)
    hidden = low(jax.nn.gelu(before, approximate=False))
    branch_two = low_back(jnp.dot(hidden, fc2_weight, precision=highest))
    return middle + masking * (branch_two + fc2_bias)

def reference(tokens, heights, widths, norm_gain, norm_bias, w_qkv, b_qv, rel_pos, w_proj, b_proj, w_fc1, b_fc1, w_fc2, b_fc2, cotangent):
    slot_count = GRID * GRID * WIN * WIN
    params = tuple((item.astype(jnp.float32) for item in (norm_gain, norm_bias, w_qkv, b_qv, rel_pos, w_proj, b_proj, w_fc1, b_fc1, w_fc2, b_fc2)))
    images = tokens.astype(jnp.float32).reshape(-1, slot_count, D)
    cotangents = cotangent.astype(jnp.float32).reshape(-1, slot_count, D)

    def one_image(totals, inputs):
        patches, image_cot, height, breadth = inputs
        valid = valid_slots(height, breadth, 0, slot_count)
        result, pullback = jax.vjp(lambda weights, rows: block_forward(weights, rows, valid), params, patches)
        grad_params, grad_patches = pullback(image_cot)
        totals = jax.tree.map(lambda first, second: first + second, totals, grad_params)
        return (totals, (result.astype(jnp.bfloat16), grad_patches))
    zeros = jax.tree.map(jnp.zeros_like, params)
    totals, (results, grad_rows) = lax.scan(one_image, zeros, (images, cotangents, heights, widths))
    return (results.reshape(-1, D), grad_rows.reshape(-1, D), totals[0], totals[1], totals[2], totals[3], totals[4], totals[5], totals[6], totals[7], totals[8], totals[9], totals[10])
```

```python
import jax
import jax.numpy as jnp
from jax import lax
from jax.experimental import pallas as pl
from jax.experimental.pallas import tpu as pltpu
from jax.sharding import PartitionSpec as P

HEAD_DIM = 64
WIN = 14
GRID = 4
SLOTS = WIN * WIN
PAD = 208
LANES = 128
HALF = 64

bf16 = jnp.bfloat16
f32 = jnp.float32
neg_fill = -30000.0
pad_fill = -1e30


def dot(a, b, dims=((1,), (0,))):
    return lax.dot_general(a, b, (dims, ((), ())), preferred_element_type=f32)


def window_constants():
    slot = jnp.arange(PAD, dtype=jnp.int32)[:, None]
    lane = jnp.arange(LANES, dtype=jnp.int32)[None, :]
    real = slot < SLOTS
    y, x = slot // WIN, slot % WIN
    shift = jnp.where(real, (WIN - 1) - jnp.where(lane < HALF, y, x), 0)
    bits = jnp.stack([(shift >> b) & 1 for b in range(4)]).astype(jnp.int32)
    inner = lane % HALF
    place = jnp.where(lane < HALF, y, x)
    hot = real & ((inner == place) | (inner - 32 == place)) & ((inner < WIN) | ((inner >= 32) & (inner < 32 + WIN)))
    return bits, hot.astype(bf16)


def position_matrix(rel_pos):
    flipped = rel_pos[:, ::-1, :]
    rows = jnp.pad(flipped, ((0, 0), (0, HALF - flipped.shape[1]), (0, 0))).reshape(LANES, HEAD_DIM)
    return jnp.concatenate([rows, rows], axis=1)


def shift_lanes(values, bits_ref, left):
    for b in range(4):
        amount = LANES - (1 << b) if left else (1 << b)
        moved = pltpu.roll(values, amount, 1)
        mask = bits_ref[b] != 0
        values = jnp.where(jnp.concatenate([mask, mask], axis=0), moved, values)
    return values


def split_heads(pair):
    lane = lax.broadcasted_iota(jnp.int32, pair.shape, 1)
    zero = jnp.zeros_like(pair)
    return jnp.concatenate(
        [jnp.where(lane < HALF, pair, zero), jnp.where(lane < HALF, zero, pair)], axis=0
    )


def merge_heads(stacked):
    top, bottom = stacked[:PAD], stacked[PAD:]
    lane = lax.broadcasted_iota(jnp.int32, top.shape, 1)
    return jnp.where(lane < HALF, top, bottom)


def attend_forward_kernel(q_ref, k_ref, v_ref, fill_ref, rel_ref, hot_ref, bits_ref, mix_ref, p_ref):
    pairs = q_ref.shape[1] // LANES
    fill = fill_ref[0]
    for pair in range(pairs):
        columns = slice(pair * LANES, (pair + 1) * LANES)
        queries = split_heads(q_ref[:, columns])
        bias = shift_lanes(dot(queries, rel_ref[...], ((1,), (1,))), bits_ref, True)
        high = bias.astype(bf16).astype(f32)
        low = pltpu.roll(bias - high, 32, 1)
        lane = lax.broadcasted_iota(jnp.int32, bias.shape, 1)
        bias = jnp.where((lane & 32) == 0, high, low).astype(bf16)
        wide_q = jnp.concatenate([queries * jnp.asarray(0.125, bf16), bias], axis=1)
        wide_k = jnp.concatenate([k_ref[:, columns], hot_ref[...]], axis=1)
        scores = dot(wide_q, wide_k, ((1,), (1,)))
        scores = jnp.where(fill == 0.0, scores, fill)
        summit = jnp.max(scores, axis=1, keepdims=True)
        weights = jnp.exp(scores - summit)
        total = jnp.sum(weights, axis=1, keepdims=True)
        attention = (weights * (1.0 / total)).astype(bf16)
        p_ref[0, pair] = attention
        mix_ref[:, columns] = merge_heads(dot(attention, v_ref[:, columns])).astype(bf16)


def attend_backward_kernel(
    q_ref, k_ref, v_ref, p_ref, d_ref, rel_ref, hot_ref, bits_ref, dq_ref, dk_ref, dv_ref, table_ref
):
    pairs = q_ref.shape[1] // LANES

    @pl.when(pl.program_id(0) == 0)
    def _():
        table_ref[...] = jnp.zeros_like(table_ref)

    for pair in range(pairs):
        columns = slice(pair * LANES, (pair + 1) * LANES)
        attention = p_ref[0, pair]
        d_mix = split_heads(d_ref[:, columns])
        queries = split_heads(q_ref[:, columns])
        eighth = jnp.asarray(0.125, bf16)
        d_attn = dot(d_mix, v_ref[:, columns], ((1,), (1,)))
        soft = attention.astype(f32)
        weighted = d_attn * soft
        inner = jnp.sum(weighted, axis=1, keepdims=True)
        d_scores = (weighted - soft * inner).astype(bf16)
        dv_ref[:, columns] = dot(attention, d_mix, ((0,), (0,))).astype(bf16)
        dk_ref[:, columns] = dot(d_scores, queries * eighth, ((0,), (0,))).astype(bf16)
        wide_k = jnp.concatenate([k_ref[:, columns] * eighth, hot_ref[...]], axis=1)
        both = dot(d_scores, wide_k)
        d_offsets = shift_lanes(both[:, LANES:], bits_ref, False)
        high = d_offsets.astype(bf16)
        low = (d_offsets - high.astype(f32)).astype(bf16)
        parts = jnp.concatenate([high, low], axis=1)
        rel = jnp.concatenate([rel_ref[...], rel_ref[...]], axis=0)
        dq_ref[:, columns] = merge_heads(both[:, :LANES] + dot(parts, rel)).astype(bf16)
        table_ref[...] += dot(parts, queries, ((0,), (0,)))


def attend_forward(q, k, v, fill, rel, hot, bits):
    rows, width = q.shape
    windows = rows // PAD
    pairs = width // LANES
    block = pl.BlockSpec((PAD, width), lambda i: (i, 0))
    whole = lambda a: pl.BlockSpec(a.shape, lambda i: (0,) * a.ndim)
    return pl.pallas_call(
        attend_forward_kernel,
        grid=(windows,),
        in_specs=[block, block, block, pl.BlockSpec((1, 1, PAD), lambda i: (i, 0, 0)), whole(rel), whole(hot), whole(bits)],
        out_specs=[block, pl.BlockSpec((1, pairs, 2 * PAD, PAD), lambda i: (i, 0, 0, 0))],
        out_shape=[
            jax.ShapeDtypeStruct((rows, width), bf16),
            jax.ShapeDtypeStruct((windows, pairs, 2 * PAD, PAD), bf16),
        ],
        compiler_params=pltpu.CompilerParams(vmem_limit_bytes=50 << 20),
    )(q, k, v, fill, rel, hot, bits)


def attend_backward(q, k, v, p, d_mixture, rel, hot, bits):
    rows, width = q.shape
    windows = rows // PAD
    pairs = width // LANES
    block = pl.BlockSpec((PAD, width), lambda i: (i, 0))
    whole = lambda a: pl.BlockSpec(a.shape, lambda i: (0,) * a.ndim)
    return pl.pallas_call(
        attend_backward_kernel,
        grid=(windows,),
        in_specs=[
            block,
            block,
            block,
            pl.BlockSpec((1, pairs, 2 * PAD, PAD), lambda i: (i, 0, 0, 0)),
            block,
            whole(rel),
            whole(hot),
            whole(bits),
        ],
        out_specs=[block, block, block, pl.BlockSpec((2 * LANES, LANES), lambda i: (0, 0))],
        out_shape=[jax.ShapeDtypeStruct((rows, width), bf16)] * 3
        + [jax.ShapeDtypeStruct((2 * LANES, LANES), f32)],
        compiler_params=pltpu.CompilerParams(vmem_limit_bytes=50 << 20),
    )(q, k, v, p, d_mixture, rel, hot, bits)


def normalize(values):
    centre = jnp.mean(values, axis=-1, keepdims=True)
    centred = values - centre
    scale = lax.rsqrt(jnp.mean(centred * centred, axis=-1, keepdims=True) + 1e-06)
    return centred * scale, scale


def normalize_back(gradient, normal, scale, gain):
    e = gradient * gain
    return scale * (
        e - jnp.mean(e, axis=-1, keepdims=True) - normal * jnp.mean(e * normal, axis=-1, keepdims=True)
    )


def gather_shards(weight, split):
    dp = lax.axis_size("dp")
    size = weight.shape[split] // dp
    piece = lax.dynamic_slice_in_dim(weight, lax.axis_index("dp") * size, size, split)
    pieces = lax.all_gather(piece, ("dp", "tp"), axis=0, tiled=False)
    pieces = pieces.reshape((dp, -1) + piece.shape)
    return jnp.moveaxis(pieces, 0, split + 1).reshape((-1,) + weight.shape)


def spread_sum(gradient, split):
    dp = lax.axis_size("dp")
    tp = gradient.shape[0]
    shape = gradient.shape[1:]
    cut = gradient.reshape((tp,) + shape[:split] + (dp, shape[split] // dp) + shape[split + 1 :])
    cut = jnp.moveaxis(cut, split + 1, 0).astype(bf16)
    mine = lax.psum_scatter(cut.reshape((dp * tp,) + cut.shape[2:]), ("dp", "tp"), scatter_dimension=0, tiled=True)
    return lax.all_gather(mine[0], "dp", axis=split, tiled=True).astype(f32)


def pad_windows(rows):
    windows = rows.shape[0] // SLOTS
    cut = rows.reshape((windows, SLOTS) + rows.shape[1:])
    return jnp.pad(cut, ((0, 0), (0, PAD - SLOTS), (0, 0))).reshape((windows * PAD,) + rows.shape[1:])


def cut_windows(rows):
    windows = rows.shape[0] // PAD
    return rows.reshape((windows, PAD) + rows.shape[1:])[:, :SLOTS].reshape((windows * SLOTS,) + rows.shape[1:])


def keep_slots(height, breadth, windows):
    first = lax.axis_index("tp") * windows
    window = (first + jnp.arange(windows, dtype=jnp.int32))[:, None]
    inside = jnp.arange(PAD, dtype=jnp.int32)[None, :]
    row_at = window // GRID * WIN + inside // WIN
    column_at = window % GRID * WIN + inside % WIN
    real = inside < SLOTS
    return (row_at < height) & (column_at < breadth) & real, real


def body(
    tokens,
    heights,
    widths,
    norm_gain,
    norm_bias,
    w_qkv,
    b_qv,
    rel_pos,
    w_proj,
    b_proj,
    w_fc1,
    b_fc1,
    w_fc2,
    b_fc2,
    cotangent,
):
    tp = lax.axis_size("tp")
    width = tokens.shape[1]
    windows = tokens.shape[0] // SLOTS
    heads_part = w_qkv.shape[2]

    full_qkv = gather_shards(w_qkv, 1).transpose(1, 2, 0, 3).reshape(3, width, width)
    full_proj = gather_shards(w_proj, 0).reshape(width, width)
    full_fc1 = gather_shards(w_fc1, 0).transpose(1, 0, 2).reshape(width, -1)
    full_fc2 = gather_shards(w_fc2, 0).reshape(-1, width)
    full_b_qv = lax.all_gather(b_qv, "tp", axis=1, tiled=True).astype(f32)
    full_b_fc1 = lax.all_gather(b_fc1, "tp", axis=0, tiled=True).astype(f32)

    keep, real = keep_slots(heights[0], widths[0], windows)
    fill = jnp.where(keep, 0.0, jnp.where(real, neg_fill, pad_fill)).astype(f32)[:, None, :]
    masking = keep.reshape(-1, 1).astype(f32)
    gains = norm_gain.astype(f32)
    shifts = norm_bias.astype(f32)
    bits, hot = window_constants()
    rel = position_matrix(rel_pos)

    inputs = pad_windows(tokens).astype(f32)
    d_output = pad_windows(cotangent).astype(f32)
    normal_one, scale_one = normalize(inputs)
    normed = (normal_one * gains[0] + shifts[0]).astype(bf16)
    queries = (dot(normed, full_qkv[0]) + full_b_qv[0]).astype(bf16)
    key_rows = dot(normed, full_qkv[1]).astype(bf16)
    values = (dot(normed, full_qkv[2]) + full_b_qv[1]).astype(bf16)
    mixture, attention = attend_forward(queries, key_rows, values, fill, rel, hot, bits)
    middle = inputs + masking * (dot(mixture, full_proj) + b_proj.astype(f32))
    normal_two, scale_two = normalize(middle)
    normed_two = (normal_two * gains[1] + shifts[1]).astype(bf16)
    before = dot(normed_two, full_fc1) + full_b_fc1
    phi = 0.5 * (1.0 + lax.erf(before * 0.7071067811865476))
    hidden = (before * phi).astype(bf16)
    slope = phi + before * (jnp.exp(-0.5 * before * before) * 0.3989422804014327)
    result = (middle + masking * (dot(hidden, full_fc2) + b_fc2.astype(f32))).astype(bf16)

    masked_out = masking * d_output
    grad_bias_two = jnp.sum(masked_out, axis=0)
    d_second = masked_out.astype(bf16)
    grad_second = dot(hidden, d_second, ((0,), (0,)))
    d_hidden = dot(d_second, full_fc2, ((1,), (1,)))
    d_before = (slope * d_hidden).astype(bf16)
    grad_bias_one = jnp.sum(d_before.astype(f32), axis=0)
    grad_first = dot(normed_two, d_before, ((0,), (0,)))
    d_normed_two = dot(d_before, full_fc1, ((1,), (1,)))
    d_middle = d_output + normalize_back(d_normed_two, normal_two, scale_two, gains[1])
    masked_mid = masking * d_middle
    grad_bias_proj = jnp.sum(masked_mid, axis=0)
    d_first = masked_mid.astype(bf16)
    grad_projection = dot(mixture, d_first, ((0,), (0,)))
    d_mixture = dot(d_first, full_proj, ((1,), (1,))).astype(bf16)
    d_queries, d_keys, d_values, table = attend_backward(
        queries, key_rows, values, attention, d_mixture, rel, hot, bits
    )
    grad_qkv = jnp.stack(
        [dot(normed, part, ((0,), (0,))) for part in (d_queries, d_keys, d_values)]
    )
    grad_qv_bias = jnp.stack(
        [jnp.sum(d_queries.astype(f32), axis=0), jnp.sum(d_values.astype(f32), axis=0)]
    )
    d_normed = (
        dot(d_queries, full_qkv[0], ((1,), (1,)))
        + dot(d_keys, full_qkv[1], ((1,), (1,)))
        + dot(d_values, full_qkv[2], ((1,), (1,)))
    )
    grad_inputs = d_middle + normalize_back(d_normed, normal_one, scale_one, gains[0])

    offsets = 2 * WIN - 1
    table = table[:LANES] + table[LANES:]
    table = table[:, :HALF] + table[:, HALF:]
    grad_table = jnp.stack([table[:offsets], table[HALF : HALF + offsets]])[:, ::-1, :]

    small = lax.psum(
        (
            jnp.stack([jnp.sum(d_normed * normal_one, axis=0), jnp.sum(d_normed_two * normal_two, axis=0)]),
            jnp.stack([jnp.sum(d_normed, axis=0), jnp.sum(d_normed_two, axis=0)]),
            grad_table,
            grad_bias_proj,
            grad_bias_two,
            grad_qv_bias,
            grad_bias_one,
        ),
        ("dp", "tp"),
    )
    me = lax.axis_index("tp")
    grad_qkv = spread_sum(grad_qkv.reshape(3, width, tp, heads_part).transpose(2, 0, 1, 3), 1)
    grad_projection = spread_sum(grad_projection.reshape(tp, heads_part, width), 0)
    grad_first = spread_sum(grad_first.reshape(width, tp, -1).transpose(1, 0, 2), 0)
    grad_second = spread_sum(grad_second.reshape(tp, -1, width), 0)
    return (
        cut_windows(result),
        cut_windows(grad_inputs),
        small[0],
        small[1],
        grad_qkv,
        lax.dynamic_slice_in_dim(small[5], me * heads_part, heads_part, 1),
        small[2],
        grad_projection,
        small[3],
        grad_first,
        lax.dynamic_slice_in_dim(small[6], me * w_fc1.shape[1], w_fc1.shape[1], 0),
        grad_second,
        small[4],
    )


def solution(mesh):
    rows = P(("dp", "tp"), None)
    return jax.shard_map(
        body,
        mesh=mesh,
        in_specs=(
            rows,
            P("dp"),
            P("dp"),
            P(),
            P(),
            P(None, None, "tp"),
            P(None, "tp"),
            P(),
            P("tp", None),
            P(),
            P(None, "tp"),
            P("tp"),
            P("tp", None),
            P(),
            rows,
        ),
        out_specs=(
            rows,
            rows,
            P(),
            P(),
            P(None, None, "tp"),
            P(None, "tp"),
            P(),
            P("tp", None),
            P(),
            P(None, "tp"),
            P("tp"),
            P("tp", None),
            P(),
        ),
        check_vma=False,
    )
```

```python
import jax
import jax.numpy as jnp
from jax import lax
from jax.experimental import pallas as pl
from jax.experimental.pallas import tpu as pltpu
from jax.sharding import PartitionSpec as P

HEAD_DIM = 64
WIN = 14
GRID = 4
SLOTS = WIN * WIN
PAD = 208
LANES = 128
HALF = 64

bf16 = jnp.bfloat16
f32 = jnp.float32
neg_fill = -30000.0
pad_fill = -1e30


def dot(a, b, dims=((1,), (0,))):
    return lax.dot_general(a, b, (dims, ((), ())), preferred_element_type=f32)


def window_constants():
    slot = jnp.arange(PAD, dtype=jnp.int32)[:, None]
    lane = jnp.arange(LANES, dtype=jnp.int32)[None, :]
    real = slot < SLOTS
    y, x = slot // WIN, slot % WIN
    shift = jnp.where(real, (WIN - 1) - jnp.where(lane < HALF, y, x), 0)
    bits = jnp.stack([(shift >> b) & 1 for b in range(4)]).astype(jnp.int32)
    inner = lane % HALF
    place = jnp.where(lane < HALF, y, x)
    hot = real & ((inner == place) | (inner - 32 == place)) & ((inner < WIN) | ((inner >= 32) & (inner < 32 + WIN)))
    return bits, hot.astype(bf16)


def position_matrix(rel_pos):
    flipped = rel_pos[:, ::-1, :]
    rows = jnp.pad(flipped, ((0, 0), (0, HALF - flipped.shape[1]), (0, 0))).reshape(LANES, HEAD_DIM)
    return jnp.concatenate([rows, rows], axis=1)


def shift_lanes(values, bits_ref, left):
    for b in range(4):
        amount = LANES - (1 << b) if left else (1 << b)
        moved = pltpu.roll(values, amount, 1)
        mask = bits_ref[b] != 0
        values = jnp.where(jnp.concatenate([mask, mask], axis=0), moved, values)
    return values


def split_heads(pair):
    lane = lax.broadcasted_iota(jnp.int32, pair.shape, 1)
    zero = jnp.zeros_like(pair)
    return jnp.concatenate(
        [jnp.where(lane < HALF, pair, zero), jnp.where(lane < HALF, zero, pair)], axis=0
    )


def merge_heads(stacked):
    top, bottom = stacked[:PAD], stacked[PAD:]
    lane = lax.broadcasted_iota(jnp.int32, top.shape, 1)
    return jnp.where(lane < HALF, top, bottom)


def attend_forward_kernel(q_ref, k_ref, v_ref, fill_ref, rel_ref, hot_ref, bits_ref, mix_ref, p_ref):
    pairs = q_ref.shape[1] // LANES
    fill = fill_ref[0]
    for pair in range(pairs):
        columns = slice(pair * LANES, (pair + 1) * LANES)
        queries = split_heads(q_ref[:, columns])
        bias = shift_lanes(dot(queries, rel_ref[...], ((1,), (1,))), bits_ref, True)
        high = bias.astype(bf16).astype(f32)
        low = pltpu.roll(bias - high, 32, 1)
        lane = lax.broadcasted_iota(jnp.int32, bias.shape, 1)
        bias = jnp.where((lane & 32) == 0, high, low).astype(bf16)
        wide_q = jnp.concatenate([queries * jnp.asarray(0.125, bf16), bias], axis=1)
        wide_k = jnp.concatenate([k_ref[:, columns], hot_ref[...]], axis=1)
        scores = dot(wide_q, wide_k, ((1,), (1,)))
        scores = jnp.where(fill == 0.0, scores, fill)
        summit = jnp.max(scores, axis=1, keepdims=True)
        weights = jnp.exp(scores - summit)
        total = jnp.sum(weights, axis=1, keepdims=True)
        attention = (weights * (1.0 / total)).astype(bf16)
        p_ref[0, pair] = attention
        mix_ref[:, columns] = merge_heads(dot(attention, v_ref[:, columns])).astype(bf16)


def attend_backward_kernel(
    q_ref, k_ref, v_ref, p_ref, d_ref, rel_ref, hot_ref, bits_ref, dq_ref, dk_ref, dv_ref, table_ref
):
    pairs = q_ref.shape[1] // LANES

    @pl.when(pl.program_id(0) == 0)
    def _():
        table_ref[...] = jnp.zeros_like(table_ref)

    for pair in range(pairs):
        columns = slice(pair * LANES, (pair + 1) * LANES)
        attention = p_ref[0, pair]
        d_mix = split_heads(d_ref[:, columns])
        queries = split_heads(q_ref[:, columns])
        eighth = jnp.asarray(0.125, bf16)
        d_attn = dot(d_mix, v_ref[:, columns], ((1,), (1,)))
        soft = attention.astype(f32)
        weighted = d_attn * soft
        inner = jnp.sum(weighted, axis=1, keepdims=True)
        d_scores = (weighted - soft * inner).astype(bf16)
        dv_ref[:, columns] = dot(attention, d_mix, ((0,), (0,))).astype(bf16)
        dk_ref[:, columns] = dot(d_scores, queries * eighth, ((0,), (0,))).astype(bf16)
        wide_k = jnp.concatenate([k_ref[:, columns] * eighth, hot_ref[...]], axis=1)
        both = dot(d_scores, wide_k)
        d_offsets = shift_lanes(both[:, LANES:], bits_ref, False)
        high = d_offsets.astype(bf16)
        low = (d_offsets - high.astype(f32)).astype(bf16)
        parts = jnp.concatenate([high, low], axis=1)
        rel = jnp.concatenate([rel_ref[...], rel_ref[...]], axis=0)
        dq_ref[:, columns] = merge_heads(both[:, :LANES] + dot(parts, rel)).astype(bf16)
        table_ref[...] += dot(parts, queries, ((0,), (0,)))


def attend_forward(q, k, v, fill, rel, hot, bits):
    rows, width = q.shape
    windows = rows // PAD
    pairs = width // LANES
    block = pl.BlockSpec((PAD, width), lambda i: (i, 0))
    whole = lambda a: pl.BlockSpec(a.shape, lambda i: (0,) * a.ndim)
    return pl.pallas_call(
        attend_forward_kernel,
        grid=(windows,),
        in_specs=[block, block, block, pl.BlockSpec((1, 1, PAD), lambda i: (i, 0, 0)), whole(rel), whole(hot), whole(bits)],
        out_specs=[block, pl.BlockSpec((1, pairs, 2 * PAD, PAD), lambda i: (i, 0, 0, 0))],
        out_shape=[
            jax.ShapeDtypeStruct((rows, width), bf16),
            jax.ShapeDtypeStruct((windows, pairs, 2 * PAD, PAD), bf16),
        ],
        compiler_params=pltpu.CompilerParams(vmem_limit_bytes=50 << 20),
    )(q, k, v, fill, rel, hot, bits)


def attend_backward(q, k, v, p, d_mixture, rel, hot, bits):
    rows, width = q.shape
    windows = rows // PAD
    pairs = width // LANES
    block = pl.BlockSpec((PAD, width), lambda i: (i, 0))
    whole = lambda a: pl.BlockSpec(a.shape, lambda i: (0,) * a.ndim)
    return pl.pallas_call(
        attend_backward_kernel,
        grid=(windows,),
        in_specs=[
            block,
            block,
            block,
            pl.BlockSpec((1, pairs, 2 * PAD, PAD), lambda i: (i, 0, 0, 0)),
            block,
            whole(rel),
            whole(hot),
            whole(bits),
        ],
        out_specs=[block, block, block, pl.BlockSpec((2 * LANES, LANES), lambda i: (0, 0))],
        out_shape=[jax.ShapeDtypeStruct((rows, width), bf16)] * 3
        + [jax.ShapeDtypeStruct((2 * LANES, LANES), f32)],
        compiler_params=pltpu.CompilerParams(vmem_limit_bytes=50 << 20),
    )(q, k, v, p, d_mixture, rel, hot, bits)


def normalize(values):
    centre = jnp.mean(values, axis=-1, keepdims=True)
    centred = values - centre
    scale = lax.rsqrt(jnp.mean(centred * centred, axis=-1, keepdims=True) + 1e-06)
    return centred * scale, scale


def normalize_back(gradient, normal, scale, gain):
    e = gradient * gain
    return scale * (
        e - jnp.mean(e, axis=-1, keepdims=True) - normal * jnp.mean(e * normal, axis=-1, keepdims=True)
    )


MESH = pl.DeviceIdType.MESH


class Place:
    def __init__(self, tp, dp):
        self.tp, self.dp = tp, dp
        self.d, self.me = lax.axis_index("dp"), lax.axis_index("tp")
        c, x, y = self.d % 2, (self.d // 2) % 2, (self.d // 4) % 2
        self.c = c
        self.core = self.d + 1 - 2 * c
        peer_x, peer_y = self.d + 2 - 4 * x, self.d + 4 - 8 * y
        self.x, self.y = peer_x, peer_y
        self.first = peer_x * (1 - c) + peer_y * c
        self.second = peer_y * (1 - c) + peer_x * c
        self.bit_one = x * (1 - c) + y * c
        self.bit_two = y * (1 - c) + x * c
        self.extra = []
        for bit in range(3, dp.bit_length() - 1):
            step = 1 << bit
            self.extra.append(self.d + step * (1 - 2 * ((self.d // step) % 2)))

    def block(self, one, two, c=None):
        c = self.c if c is None else c
        y = two * (1 - c) + one * c
        x = one * (1 - c) + two * c
        return 2 * y + x

    def flips(self):
        a, b = self.bit_one, self.bit_two
        return [self.block(a, b), self.block(1 - a, b), self.block(a, 1 - b), self.block(1 - a, 1 - b)]

    def other(self, step):
        return (self.me + step) % self.tp

    def greet(self):
        barrier = pltpu.get_barrier_semaphore()
        peers = [self.core, self.x, self.y] + self.extra
        for peer in peers:
            pl.semaphore_signal(barrier, inc=1, device_id=(peer, self.me), device_id_type=MESH)

        def signal(step, carry):
            pl.semaphore_signal(barrier, inc=1, device_id=(self.d, self.other(step)), device_id_type=MESH)
            return carry

        lax.fori_loop(1, self.tp, signal, 0)
        pl.semaphore_wait(barrier, len(peers) + self.tp - 1)


def piece(ref, block, c):
    rows, columns = ref.shape[-2] // 4, ref.shape[-1] // 2
    lead = (slice(None),) * (len(ref.shape) - 2)
    return ref.at[
        lead + (pl.ds(pl.multiple_of(block * rows, rows), rows), pl.ds(pl.multiple_of(c * columns, columns), columns))
    ]


def remote(src, dst, send, recv, device):
    return pltpu.make_async_remote_copy(
        src_ref=src, dst_ref=dst, send_sem=send, recv_sem=recv, device_id=device, device_id_type=MESH
    )


class Spread:
    def __init__(self, place, ref, send, recv, at):
        self.place, self.ref, self.send, self.recv, self.at = place, ref, send, recv, at

    def copy(self, k, arriving):
        place = self.place
        flips = place.flips()
        me = place.me
        if k == 0:
            device, block, came = place.first, flips[0], flips[1]
            half = came_half = place.c
        elif k < 3:
            device, block, came = place.second, flips[k - 1], flips[k + 1]
            half = came_half = place.c
        else:
            device, block = place.core, flips[k - 3]
            came = flips[(0, 2, 1, 3)[k - 3]]
            half, came_half = place.c, 1 - place.c
        where, side = (came, came_half) if arriving else (block, half)
        view = piece(self.ref, where, side)
        index = tuple(self.at) + (k,)
        return remote(view, view, self.send.at[index], self.recv.at[index], (device, me))

    def start_own(self):
        for k in (0, 1, 3):
            self.copy(k, False).start()

    def after_first(self):
        self.copy(0, True).wait_recv()
        for k in (2, 4):
            self.copy(k, False).start()

    def after_second(self):
        for k in (1, 2):
            self.copy(k, True).wait_recv()
            self.copy(k + 4, False).start()

    def finish(self):
        for k in range(3, 7):
            self.copy(k, True).wait_recv()
        for k in range(7):
            self.copy(k, False).wait_send()


def gather_kernel(
    tp, dp, a_ref, f_ref, g_ref, small_ref, ga_ref, gf_ref, gg_ref, gs_ref, z_send, z_recv, p_send, p_recv, local, s_send, s_recv
):
    place = Place(tp, dp)
    pairs = [(a_ref, ga_ref), (f_ref, gf_ref), (g_ref, gg_ref)]
    place.greet()

    def around(fn):
        def step(j, carry):
            fn(place.other(j))
            return carry

        lax.fori_loop(1, tp, step, 0)

    def z_copy(w, other, arriving):
        src, dst = pairs[w]
        owner = other if arriving else place.me
        block = place.flips()[0]
        return remote(
            piece(src, block, place.c),
            piece(dst.at[owner], block, place.c),
            z_send.at[w, other],
            z_recv.at[w, owner],
            (place.d, other),
        )

    def small_copy(other, arriving):
        owner = other if arriving else place.me
        return remote(small_ref, gs_ref.at[owner], s_send.at[other], s_recv.at[owner], (place.d, other))

    def spread(w, s):
        return Spread(place, pairs[w][1].at[s], p_send, p_recv, (w, s))

    around(lambda s: small_copy(s, False).start())
    around(lambda s: z_copy(0, s, False).start())
    mine = pltpu.make_async_copy(small_ref, gs_ref.at[place.me], local.at[0])
    mine.start()

    def first(w):
        def one(s):
            z_copy(w, s, True).wait_recv()
            spread(w, s).start_own()

        around(one)

    second = lambda w: around(lambda s: spread(w, s).after_first())
    third = lambda w: around(lambda s: spread(w, s).after_second())
    send = lambda w: around(lambda s: z_copy(w, s, False).start())
    first(0)
    send(1)
    second(0)
    first(1)
    third(0)
    send(2)
    second(1)
    first(2)
    third(1)
    second(2)
    third(2)
    for w in range(3):
        around(lambda s: spread(w, s).finish())
        around(lambda s: z_copy(w, s, False).wait_send())
    mine.wait()
    around(lambda s: small_copy(s, True).wait_recv())
    around(lambda s: small_copy(s, False).wait_send())


def gather_weights(tp, dp, a, f, g, small):
    any_space = pl.BlockSpec(memory_space=pl.ANY)
    dma = pltpu.SemaphoreType.DMA
    return pl.pallas_call(
        lambda *refs: gather_kernel(tp, dp, *refs),
        in_specs=[any_space] * 4,
        out_specs=[any_space] * 4,
        out_shape=[jax.ShapeDtypeStruct((tp,) + w.shape, w.dtype) for w in (a, f, g, small)],
        scratch_shapes=[
            dma((3, tp)),
            dma((3, tp)),
            dma((3, tp, 7)),
            dma((3, tp, 7)),
            dma((1,)),
            dma((tp,)),
            dma((tp,)),
        ],
        compiler_params=pltpu.CompilerParams(collective_id=1, has_side_effects=True),
    )(a, f, g, small)


def reduce_kernel(tp, dp, *refs):
    count = 3
    grads, small_ref = refs[:count], refs[count]
    outs, small_out = refs[count + 1 : 2 * count + 1], refs[2 * count + 1]
    scratch = list(refs[2 * count + 2 :])
    take = lambda n: [scratch.pop(0) for _ in range(n)]
    own, halves, quarters, eighths, arrived, final = (take(count) for _ in range(6))
    extra_buffers = take(count) if dp > 8 else None
    small_sum, small_in, small_z = take(3)
    local, core_send, core_recv, one_send, one_recv, two_send, two_recv, z_send, z_recv, p_send, p_recv, s_send, s_recv, sz_send, sz_recv = take(15)
    place = Place(tp, dp)
    a, b, c = place.bit_one, place.bit_two, place.c
    me = place.me

    def rows_of(ref, block, size):
        return pl.ds(pl.multiple_of(block * size, size), size)

    def half_of(w, side):
        columns = grads[w].shape[-1] // 2
        return grads[w].at[:, :, :, pl.ds(pl.multiple_of(side * columns, columns), columns)]

    own_copy = [pltpu.make_async_copy(half_of(w, c), own[w], local.at[w]) for w in range(count)]
    core_copy = [
        remote(half_of(w, 1 - c), halves[w], core_send.at[w], core_recv.at[w], (place.core, me)) for w in range(count)
    ]

    def quarter_copy(w, two):
        size = quarters[w].shape[2] // 2
        return remote(
            halves[w].at[:, :, rows_of(halves[w], place.block(1 - a, two), size)],
            quarters[w].at[:, :, two * size : (two + 1) * size],
            one_send.at[w, two],
            one_recv.at[w, two],
            (place.first, me),
        )

    def eighth_copy(w):
        size = eighths[w].shape[2]
        return remote(
            quarters[w].at[:, :, rows_of(quarters[w], 1 - b, size)],
            eighths[w],
            two_send.at[w],
            two_recv.at[w],
            (place.second, me),
        )

    def around(fn):
        def step(j, carry):
            fn(place.other(j))
            return carry

        lax.fori_loop(1, tp, step, 0)

    def shard_copy(w, other, arriving):
        owner = other if arriving else me
        return remote(
            eighths[w].at[other], arrived[w].at[owner], z_send.at[w, other], z_recv.at[w, owner], (place.d, other)
        )

    def each_shard(fn):
        def step(s, carry):
            fn(s)
            return carry

        lax.fori_loop(0, tp, step, 0)

    def add_half(w, block):
        size = eighths[w].shape[2]
        rows = rows_of(halves[w], block, size)

        def one(s):
            halves[w][s, :, rows] += own[w][s, :, rows]

        each_shard(one)

    def add_quarter(w, two):
        size = eighths[w].shape[2]
        rows, block = rows_of(quarters[w], two, size), rows_of(halves[w], place.block(a, two), size)

        def one(s):
            quarters[w][s, :, rows] += halves[w][s, :, block]

        each_shard(one)

    def step_one(w):
        own_copy[w].wait()
        core_copy[w].wait_recv()
        for two in range(2):
            add_half(w, place.block(1 - a, two))
            quarter_copy(w, two).start()
        for two in range(2):
            add_half(w, place.block(a, two))

    def step_two(w):
        for two in range(2):
            quarter_copy(w, two).wait_recv()
        add_quarter(w, 1 - b)
        eighth_copy(w).start()
        add_quarter(w, b)

    def step_three(w):
        eighth_copy(w).wait_recv()
        size = eighths[w].shape[2]
        rows = rows_of(quarters[w], b, size)

        def one(s):
            eighths[w][s] += quarters[w][s, :, rows]

        each_shard(one)
        around(lambda s: shard_copy(w, s, False).start())

    def step_four(w):
        around(lambda s: shard_copy(w, s, True).wait_recv())
        arrived[w][me] = eighths[w][me]
        total = arrived[w][0].astype(f32)
        for s in range(1, tp):
            total += arrived[w][s].astype(f32)
        final[w][...] = total.astype(bf16)
        for k, peer in enumerate(place.extra):
            copy = remote(final[w], extra_buffers[w].at[k], sz_send.at[tp + w, k], sz_recv.at[tp + w, k], (peer, me))
            copy.start()
            copy.wait()
            final[w][...] += extra_buffers[w][k]
        put = pltpu.make_async_copy(final[w], piece(outs[w], place.flips()[0], c), local.at[w])
        put.start()
        put.wait()
        spread(w).start_own()

    def spread(w):
        return Spread(place, outs[w], p_send, p_recv, (w,))

    levels = [place.core, place.x, place.y] + place.extra

    def small_copy(k):
        return remote(small_sum, small_in.at[k], s_send.at[k], s_recv.at[k], (levels[k], me))

    def small_level(k):
        small_copy(k).wait()
        small_sum[...] += small_in[k]
        if k + 1 < len(levels):
            small_copy(k + 1).start()

    def small_shard(other, arriving):
        owner = other if arriving else me
        return remote(small_sum, small_z.at[owner], sz_send.at[other, 0], sz_recv.at[owner, 0], (place.d, other))

    place.greet()
    order = (2, 1, 0)
    for w in order:
        own_copy[w].start()
        core_copy[w].start()
    small_sum[...] = small_ref[...]
    small_copy(0).start()
    u, v, t = order
    step_one(u)
    small_level(0)
    step_one(v)
    small_level(1)
    step_two(u)
    small_level(2)
    step_one(t)
    step_two(v)
    step_three(u)
    for k in range(3, len(levels)):
        small_level(k)
    around(lambda s: small_shard(s, False).start())
    step_two(t)
    step_three(v)
    step_four(u)
    step_three(t)
    step_four(v)
    spread(u).after_first()
    around(lambda s: small_shard(s, True).wait_recv())
    small_z[me] = small_sum[...]
    total = small_z[0]
    for s in range(1, tp):
        total += small_z[s]
    small_out[...] = total
    step_four(t)
    spread(u).after_second()
    spread(v).after_first()
    spread(t).after_first()
    spread(v).after_second()
    spread(t).after_second()
    for w in order:
        spread(w).finish()
    for w in range(count):
        core_copy[w].wait_send()
        for two in range(2):
            quarter_copy(w, two).wait_send()
        eighth_copy(w).wait_send()
        around(lambda s: shard_copy(w, s, False).wait_send())
    around(lambda s: small_shard(s, False).wait_send())


def reduce_gradients(tp, dp, grads, small):
    count = len(grads)
    any_space = pl.BlockSpec(memory_space=pl.ANY)
    vmem = pl.BlockSpec(memory_space=pltpu.VMEM)
    dma = pltpu.SemaphoreType.DMA
    more = dp.bit_length() - 4
    half = lambda g, part, lead: pltpu.VMEM(lead + (g.shape[1], g.shape[2] // part, g.shape[3] // 2), bf16)
    scratch = []
    for part, lead in ((1, (tp,)), (1, (tp,)), (2, (tp,)), (4, (tp,)), (4, (tp,)), (4, ())):
        scratch += [half(g, part, lead) for g in grads]
    if more:
        scratch += [half(g, 4, (more,)) for g in grads]
    scratch += [
        pltpu.VMEM(small.shape, f32),
        pltpu.VMEM((3 + more,) + small.shape, f32),
        pltpu.VMEM((tp,) + small.shape, f32),
    ]
    scratch += [dma((count,)), dma((count,)), dma((count,)), dma((count, 2)), dma((count, 2)), dma((count,)), dma((count,))]
    scratch += [dma((count, tp)), dma((count, tp)), dma((count, 7)), dma((count, 7)), dma((3 + more,)), dma((3 + more,))]
    scratch += [dma((tp + count, max(more, 1))), dma((tp + count, max(more, 1)))]
    return pl.pallas_call(
        lambda *refs: reduce_kernel(tp, dp, *refs),
        in_specs=[any_space] * count + [vmem],
        out_specs=[any_space] * count + [vmem],
        out_shape=[jax.ShapeDtypeStruct(g.shape[1:], bf16) for g in grads] + [jax.ShapeDtypeStruct(small.shape, f32)],
        scratch_shapes=scratch,
        compiler_params=pltpu.CompilerParams(collective_id=2, has_side_effects=True, vmem_limit_bytes=56 << 20),
    )(*grads, small)


def pack_small(parts):
    flat = jnp.concatenate([part.reshape(-1) for part in parts])
    rows = -(-flat.shape[0] // (8 * LANES)) * 8
    return jnp.pad(flat, (0, rows * LANES - flat.shape[0])).reshape(rows, LANES)


def unpack_small(packed, shapes):
    flat, at, parts = packed.reshape(-1), 0, []
    for shape in shapes:
        size = 1
        for extent in shape:
            size *= extent
        parts.append(flat[at : at + size].reshape(shape))
        at += size
    return parts


def pad_windows(rows):
    windows = rows.shape[0] // SLOTS
    cut = rows.reshape((windows, SLOTS) + rows.shape[1:])
    return jnp.pad(cut, ((0, 0), (0, PAD - SLOTS), (0, 0))).reshape((windows * PAD,) + rows.shape[1:])


def cut_windows(rows):
    windows = rows.shape[0] // PAD
    return rows.reshape((windows, PAD) + rows.shape[1:])[:, :SLOTS].reshape((windows * SLOTS,) + rows.shape[1:])


def keep_slots(height, breadth, windows):
    first = lax.axis_index("tp") * windows
    window = (first + jnp.arange(windows, dtype=jnp.int32))[:, None]
    inside = jnp.arange(PAD, dtype=jnp.int32)[None, :]
    row_at = window // GRID * WIN + inside // WIN
    column_at = window % GRID * WIN + inside % WIN
    real = inside < SLOTS
    return (row_at < height) & (column_at < breadth) & real, real


def body(
    tokens,
    heights,
    widths,
    norm_gain,
    norm_bias,
    w_qkv,
    b_qv,
    rel_pos,
    w_proj,
    b_proj,
    w_fc1,
    b_fc1,
    w_fc2,
    b_fc2,
    cotangent,
):
    tp, dp = lax.axis_size("tp"), lax.axis_size("dp")
    width = tokens.shape[1]
    windows = tokens.shape[0] // SLOTS
    heads_part = w_qkv.shape[2]

    turned = jnp.concatenate([w_qkv.transpose(0, 2, 1), w_proj[None]], axis=0)
    small = pack_small([b_qv.astype(f32), b_fc1.astype(f32)])
    full_a, full_f, full_g, full_small = gather_weights(tp, dp, turned, w_fc1[None], w_fc2[None], small)
    me = lax.axis_index("tp")
    full_a, full_f, full_g = [
        lax.dynamic_update_index_in_dim(whole, part, me, 0)
        for whole, part in ((full_a, turned), (full_f, w_fc1[None]), (full_g, w_fc2[None]))
    ]
    full_qkv = [full_a[:, t].reshape(width, width) for t in range(3)]
    full_proj = full_a[:, 3].reshape(width, width)
    full_fc1 = full_f[:, 0].transpose(1, 0, 2).reshape(width, -1)
    full_fc2 = full_g.reshape(-1, width)
    biases = [unpack_small(full_small[s], (b_qv.shape, b_fc1.shape)) for s in range(tp)]
    full_b_qv = jnp.concatenate([pair[0] for pair in biases], axis=1)
    full_b_fc1 = jnp.concatenate([pair[1] for pair in biases])

    keep, real = keep_slots(heights[0], widths[0], windows)
    fill = jnp.where(keep, 0.0, jnp.where(real, neg_fill, pad_fill)).astype(f32)[:, None, :]
    masking = keep.reshape(-1, 1).astype(f32)
    gains = norm_gain.astype(f32)
    shifts = norm_bias.astype(f32)
    bits, hot = window_constants()
    rel = position_matrix(rel_pos)

    inputs = pad_windows(tokens).astype(f32)
    d_output = pad_windows(cotangent).astype(f32)
    normal_one, scale_one = normalize(inputs)
    normed = (normal_one * gains[0] + shifts[0]).astype(bf16)
    queries = (dot(normed, full_qkv[0], ((1,), (1,))) + full_b_qv[0]).astype(bf16)
    key_rows = dot(normed, full_qkv[1], ((1,), (1,))).astype(bf16)
    values = (dot(normed, full_qkv[2], ((1,), (1,))) + full_b_qv[1]).astype(bf16)
    mixture, attention = attend_forward(queries, key_rows, values, fill, rel, hot, bits)
    middle = inputs + masking * (dot(mixture, full_proj) + b_proj.astype(f32))
    normal_two, scale_two = normalize(middle)
    normed_two = (normal_two * gains[1] + shifts[1]).astype(bf16)
    before = dot(normed_two, full_fc1) + full_b_fc1
    phi = 0.5 * (1.0 + lax.erf(before * 0.7071067811865476))
    hidden = (before * phi).astype(bf16)
    slope = phi + before * (jnp.exp(-0.5 * before * before) * 0.3989422804014327)
    result = (middle + masking * (dot(hidden, full_fc2) + b_fc2.astype(f32))).astype(bf16)

    masked_out = masking * d_output
    grad_bias_two = jnp.sum(masked_out, axis=0)
    d_second = masked_out.astype(bf16)
    grad_second = dot(hidden, d_second, ((0,), (0,)))
    d_hidden = dot(d_second, full_fc2, ((1,), (1,)))
    d_before = (slope * d_hidden).astype(bf16)
    grad_bias_one = jnp.sum(d_before.astype(f32), axis=0)
    grad_first = dot(normed_two, d_before, ((0,), (0,)))
    d_normed_two = dot(d_before, full_fc1, ((1,), (1,)))
    d_middle = d_output + normalize_back(d_normed_two, normal_two, scale_two, gains[1])
    masked_mid = masking * d_middle
    grad_bias_proj = jnp.sum(masked_mid, axis=0)
    d_first = masked_mid.astype(bf16)
    grad_projection = dot(mixture, d_first, ((0,), (0,)))
    d_mixture = dot(d_first, full_proj, ((1,), (1,))).astype(bf16)
    d_queries, d_keys, d_values, table = attend_backward(
        queries, key_rows, values, attention, d_mixture, rel, hot, bits
    )
    grad_qkv = [dot(part, normed, ((0,), (0,))).astype(bf16) for part in (d_queries, d_keys, d_values)]
    grad_qv_bias = jnp.stack(
        [jnp.sum(d_queries.astype(f32), axis=0), jnp.sum(d_values.astype(f32), axis=0)]
    )
    d_normed = (
        dot(d_queries, full_qkv[0])
        + dot(d_keys, full_qkv[1])
        + dot(d_values, full_qkv[2])
    )
    grad_inputs = d_middle + normalize_back(d_normed, normal_one, scale_one, gains[0])

    offsets = 2 * WIN - 1
    table = table[:LANES] + table[LANES:]
    table = table[:, :HALF] + table[:, HALF:]
    grad_table = jnp.stack([table[:offsets], table[HALF : HALF + offsets]])[:, ::-1, :]

    shard = lambda grad, count: grad.astype(bf16).reshape((tp, count, grad.shape[0] // (tp * count), width))
    grads = [
        jnp.stack([part.reshape(tp, heads_part, width) for part in grad_qkv + [grad_projection.astype(bf16)]], axis=1),
        grad_first.astype(bf16).reshape(width, tp, 1, -1).transpose(1, 2, 0, 3),
        shard(grad_second, 1),
    ]
    parts = [
        jnp.stack([jnp.sum(d_normed * normal_one, axis=0), jnp.sum(d_normed_two * normal_two, axis=0)]),
        jnp.stack([jnp.sum(d_normed, axis=0), jnp.sum(d_normed_two, axis=0)]),
        grad_table,
        grad_bias_proj,
        grad_bias_two,
        grad_qv_bias,
        grad_bias_one,
    ]
    out_a, out_f, out_g, out_small = reduce_gradients(tp, dp, grads, pack_small(parts))
    small = unpack_small(out_small, [part.shape for part in parts])
    me = lax.axis_index("tp")
    return (
        cut_windows(result),
        cut_windows(grad_inputs),
        small[0],
        small[1],
        out_a[:3].transpose(0, 2, 1).astype(f32),
        lax.dynamic_slice_in_dim(small[5], me * heads_part, heads_part, 1),
        small[2],
        out_a[3].astype(f32),
        small[3],
        out_f[0].astype(f32),
        lax.dynamic_slice_in_dim(small[6], me * w_fc1.shape[1], w_fc1.shape[1], 0),
        out_g[0].astype(f32),
        small[4],
    )


def solution(mesh):
    rows = P(("dp", "tp"), None)
    return jax.shard_map(
        body,
        mesh=mesh,
        in_specs=(
            rows,
            P("dp"),
            P("dp"),
            P(),
            P(),
            P(None, None, "tp"),
            P(None, "tp"),
            P(),
            P("tp", None),
            P(),
            P(None, "tp"),
            P("tp"),
            P("tp", None),
            P(),
            rows,
        ),
        out_specs=(
            rows,
            rows,
            P(),
            P(),
            P(None, None, "tp"),
            P(None, "tp"),
            P(),
            P("tp", None),
            P(),
            P(None, "tp"),
            P("tp"),
            P("tp", None),
            P(),
        ),
        check_vma=False,
    )
```

```python
import jax
import jax.numpy as jnp
from jax import lax
from jax.experimental import pallas as pl
from jax.experimental.pallas import tpu as pltpu
from jax.sharding import PartitionSpec as P

HEAD_DIM = 64
WIN = 14
GRID = 4
SLOTS = WIN * WIN
PAD = 208
LANES = 128
HALF = 64
CHUNK = 64
TILE = 256

bf16 = jnp.bfloat16
f32 = jnp.float32
neg_fill = -30000.0
pad_fill = -1e30
root_half = 0.7071067811865476
bell = 0.3989422804014327
VMEM_LIMIT = 64 << 20
MESH = pl.DeviceIdType.MESH


def dot(a, b, dims=((1,), (0,))):
    return lax.dot_general(a, b, (dims, ((), ())), preferred_element_type=f32)


NT = ((1,), (1,))
TN = ((0,), (0,))


def window_constants():
    slot = jnp.arange(PAD, dtype=jnp.int32)[:, None]
    lane = jnp.arange(HALF, dtype=jnp.int32)[None, :]
    place = jnp.where(lane % 32 < 16, slot // WIN, slot % WIN)
    hot = ((slot < SLOTS) & (lane % 16 == place)).astype(bf16)
    zero = jnp.zeros_like(hot)
    return jnp.concatenate([jnp.concatenate([hot, zero], 1), jnp.concatenate([zero, hot], 1)], 0), hot[:, :32].T


def position_matrices(rel_pos):
    flipped = rel_pos[:, ::-1, :]
    rows = jnp.pad(flipped, ((0, 0), (0, 32 - flipped.shape[1]), (0, 0))).reshape(HALF, HEAD_DIM)
    zero = jnp.zeros_like(rows)
    both = jnp.concatenate([jnp.concatenate([rows, zero], 1), jnp.concatenate([zero, rows], 1)], 0)
    return both * jnp.asarray(8.0, bf16), both.T


def stack_heads(pair, heads):
    if heads == 1:
        return pair
    lane = lax.broadcasted_iota(jnp.int32, pair.shape, 1)
    zero = jnp.zeros_like(pair)
    return jnp.concatenate([jnp.where(lane < HALF, pair, zero), jnp.where(lane < HALF, zero, pair)], axis=0)


def merge_heads(stacked, heads):
    if heads == 1:
        return stacked
    top, bottom = stacked[:PAD], stacked[PAD:]
    lane = lax.broadcasted_iota(jnp.int32, top.shape, 1)
    return jnp.where(lane < HALF, top, bottom)


def place_of_lane():
    lane = lax.broadcasted_iota(jnp.int32, (1, PAD), 1)
    row = lax.div(lane, WIN)
    return row, lane - row * WIN


def attend_forward_unit(q_ref, k_ref, v_ref, mix_ref, p_ref, fill_ref, rel_ref, hot_ref, scr_ref, blocks):
    places = place_of_lane()
    eighth = jnp.asarray(0.125, bf16)
    firsts, scores, biases = [], [], []
    count = 0
    for window, start, heads in blocks:
        firsts.append(count)
        lanes, rows = slice(start, start + LANES), slice(window * PAD, (window + 1) * PAD)
        left = jnp.concatenate([rel_ref[: heads * HALF], stack_heads(k_ref[rows, lanes], heads)], axis=0)
        both = dot(left, q_ref[rows, lanes] * eighth, NT)
        for head in range(heads):
            scr_ref[count + head] = both[head * HALF : (head + 1) * HALF]
        scores.append(both[heads * HALF :])
        count += heads
    for b, (window, start, heads) in enumerate(blocks):
        parts = []
        for head in range(heads):
            along = []
            for base, place in ((0, places[0]), (32, places[1])):
                picked = scr_ref[firsts[b] + head, base : base + 16, :]
                for at in range(WIN - 1):
                    first = base + WIN - 1 - at
                    picked = jnp.where(place == at, scr_ref[firsts[b] + head, first : first + 16, :], picked)
                along.append(picked)
            bias = jnp.concatenate(along, axis=0)
            high = bias.astype(bf16)
            parts += [high, (bias - high.astype(f32)).astype(bf16)]
        biases.append(jnp.concatenate(parts, axis=0))
    for b, (window, start, heads) in enumerate(blocks):
        scores[b] = scores[b] + dot(hot_ref[: heads * PAD, : heads * HALF], biases[b])
    for b, (window, start, heads) in enumerate(blocks):
        fill = fill_ref[window * PAD : (window + 1) * PAD]
        fill = jnp.concatenate([fill, fill[:, : PAD - LANES]], axis=1)
        for head in range(heads):
            one = scores[b][head * PAD : (head + 1) * PAD]
            one = jnp.where(fill == 0.0, one, fill)
            weights = jnp.exp(one - jnp.max(one, axis=0, keepdims=True))
            total = jnp.sum(weights, axis=0, keepdims=True)
            p_ref[firsts[b] + head] = (weights * (1.0 / total)).astype(bf16)
    for b, (window, start, heads) in enumerate(blocks):
        lanes, rows = slice(start, start + LANES), slice(window * PAD, (window + 1) * PAD)
        turned = v_ref[rows, lanes].T
        parts = [
            dot(turned[head * HALF : (head + 1) * HALF], p_ref[firsts[b] + head]).astype(bf16) for head in range(heads)
        ]
        if heads == 1:
            parts.append(jnp.zeros_like(parts[0]))
        mix_ref[rows, lanes] = jnp.concatenate(parts, axis=0).T


def attend_backward_unit(
    q_ref, k_ref, v_ref, d_ref, p_ref, dq_ref, dk_ref, dv_ref, table_ref, relt_ref, hott_ref, scr_ref, blocks
):
    places = place_of_lane()
    eighth = jnp.asarray(0.125, bf16)
    firsts, d_attn, d_scores, sums, offsets = [], [], [], [], []
    count = 0
    for window, start, heads in blocks:
        firsts.append(count)
        lanes, rows = slice(start, start + LANES), slice(window * PAD, (window + 1) * PAD)
        d_attn.append(dot(stack_heads(v_ref[rows, lanes], heads), d_ref[rows, lanes], NT))
        count += heads
    for b, (window, start, heads) in enumerate(blocks):
        lanes, rows = slice(start, start + LANES), slice(window * PAD, (window + 1) * PAD)
        soft = p_ref[firsts[b] : firsts[b] + heads].reshape(heads * PAD, PAD)
        dv_ref[rows, lanes] = merge_heads(dot(soft, d_ref[rows, lanes]), heads).astype(bf16)
    for b, (window, start, heads) in enumerate(blocks):
        parts = []
        for head in range(heads):
            soft = p_ref[firsts[b] + head].astype(f32)
            weighted = d_attn[b][head * PAD : (head + 1) * PAD] * soft
            inner = jnp.sum(weighted, axis=0, keepdims=True)
            parts.append((weighted - soft * inner).astype(bf16))
        d_scores.append(parts)
    for b, (window, start, heads) in enumerate(blocks):
        lanes, rows = slice(start, start + LANES), slice(window * PAD, (window + 1) * PAD)
        turned_k = k_ref[rows, lanes].T * eighth
        parts = []
        for head in range(heads):
            left = jnp.concatenate([turned_k[head * HALF : (head + 1) * HALF], hott_ref[...]], axis=0)
            both = dot(left, d_scores[b][head])
            for axis in range(2):
                scr_ref[firsts[b] + head, axis, 16:32, :] = both[HALF + 16 * axis : HALF + 16 * axis + 16]
            parts.append(both[:HALF])
        sums.append(parts)
    for b, (window, start, heads) in enumerate(blocks):
        spread = []
        for head in range(heads):
            for axis in range(2):
                picked = scr_ref[firsts[b] + head, axis, 16:48, :]
                for at in range(WIN - 1):
                    picked = jnp.where(places[axis] == at, scr_ref[firsts[b] + head, axis, 3 + at : 35 + at, :], picked)
                spread.append(picked)
        offsets.append(jnp.concatenate(spread, axis=0).astype(bf16))
    for b, (window, start, heads) in enumerate(blocks):
        lanes, rows = slice(start, start + LANES), slice(window * PAD, (window + 1) * PAD)
        right = dot(jnp.concatenate(d_scores[b] + [offsets[b]], axis=0), q_ref[rows, lanes])
        dk_ref[rows, lanes] = (merge_heads(right[: heads * PAD], heads) * 0.125).astype(bf16)
        table_ref[: heads * HALF] += right[heads * PAD :]
        extra = dot(relt_ref[:, : heads * HALF], offsets[b])
        turned = jnp.concatenate(sums[b] if heads == 2 else sums[b] + [jnp.zeros_like(sums[b][0])], axis=0) + extra
        turned = turned.astype(bf16)
        dq_ref[rows, lanes] = turned.T


class Place:
    def __init__(self, tp, dp):
        self.tp, self.dp = tp, dp
        self.d, self.me = lax.axis_index("dp"), lax.axis_index("tp")
        c, x, y = self.d % 2, (self.d // 2) % 2, (self.d // 4) % 2
        self.c = c
        self.core = self.d + 1 - 2 * c
        peer_x, peer_y = self.d + 2 - 4 * x, self.d + 4 - 8 * y
        self.x, self.y = peer_x, peer_y
        self.first = peer_x * (1 - c) + peer_y * c
        self.second = peer_y * (1 - c) + peer_x * c
        self.bit_one = x * (1 - c) + y * c
        self.bit_two = y * (1 - c) + x * c
        self.extra = []
        for bit in range(3, dp.bit_length() - 1):
            step = 1 << bit
            self.extra.append(self.d + step * (1 - 2 * ((self.d // step) % 2)))

    def block(self, one, two, c=None):
        c = self.c if c is None else c
        y = two * (1 - c) + one * c
        x = one * (1 - c) + two * c
        return 2 * y + x

    def flips(self):
        a, b = self.bit_one, self.bit_two
        return [self.block(a, b), self.block(1 - a, b), self.block(a, 1 - b), self.block(1 - a, 1 - b)]

    def other(self, step):
        return (self.me + step) % self.tp

    def greet_start(self):
        barrier = pltpu.get_barrier_semaphore()
        for peer in [self.core, self.x, self.y] + self.extra:
            pl.semaphore_signal(barrier, inc=1, device_id=(peer, self.me), device_id_type=MESH)

        def signal(step, carry):
            pl.semaphore_signal(barrier, inc=1, device_id=(self.d, self.other(step)), device_id_type=MESH)
            return carry

        lax.fori_loop(1, self.tp, signal, 0)

    def greet_wait(self):
        pl.semaphore_wait(pltpu.get_barrier_semaphore(), 3 + len(self.extra) + self.tp - 1)


def piece(ref, block, c):
    rows, columns = ref.shape[-2] // 4, ref.shape[-1] // 2
    lead = (slice(None),) * (len(ref.shape) - 2)
    return ref.at[
        lead + (pl.ds(pl.multiple_of(block * rows, rows), rows), pl.ds(pl.multiple_of(c * columns, columns), columns))
    ]


def remote(src, dst, send, recv, device):
    return pltpu.make_async_remote_copy(
        src_ref=src, dst_ref=dst, send_sem=send, recv_sem=recv, device_id=device, device_id_type=MESH
    )


class Spread:
    def __init__(self, place, ref, send, recv, at):
        self.place, self.ref, self.send, self.recv, self.at = place, ref, send, recv, at

    def copy(self, k, arriving):
        place = self.place
        flips = place.flips()
        me = place.me
        if k == 0:
            device, block, came = place.first, flips[0], flips[1]
            half = came_half = place.c
        elif k < 3:
            device, block, came = place.second, flips[k - 1], flips[k + 1]
            half = came_half = place.c
        else:
            device, block = place.core, flips[k - 3]
            came = flips[(0, 2, 1, 3)[k - 3]]
            half, came_half = place.c, 1 - place.c
        where, side = (came, came_half) if arriving else (block, half)
        view = piece(self.ref, where, side)
        index = tuple(self.at) + (k,)
        return remote(view, view, self.send.at[index], self.recv.at[index], (device, me))

    def start_own(self):
        for k in (0, 1, 3):
            self.copy(k, False).start()

    def after_first(self):
        self.copy(0, True).wait_recv()
        for k in (2, 4):
            self.copy(k, False).start()

    def after_second(self):
        for k in (1, 2):
            self.copy(k, True).wait_recv()
            self.copy(k + 4, False).start()

    def ready(self):
        for k in range(3, 7):
            self.copy(k, True).wait_recv()

    def sent(self):
        for k in range(7):
            self.copy(k, False).wait_send()


def repeat(count, fn, first=0):
    def step(i, carry):
        fn(i)
        return carry

    lax.fori_loop(first, count, step, 0)


def normal_rows(values):
    centre = jnp.mean(values, axis=-1, keepdims=True)
    centred = values - centre
    scale = lax.rsqrt(jnp.mean(centred * centred, axis=-1, keepdims=True) + 1e-06)
    return centred * scale, scale


def normal_back(gradient, normal, scale, gain):
    e = gradient * gain
    return scale * (
        e - jnp.mean(e, axis=-1, keepdims=True) - normal * jnp.mean(e * normal, axis=-1, keepdims=True)
    )


def block_kernel(tp, dp, names, *refs):
    r = dict(zip(names, refs))
    place = Place(tp, dp)
    me, c, one_bit, two_bit = place.me, place.c, place.bit_one, place.bit_two
    x, cot, fill, vec = r["x"], r["cot"], r["fill"], r["vec"]
    a, f, g, ga = r["a"], r["f"], r["g"], r["ga"]
    normed, q, k, v, mix = r["normed"], r["q"], r["k"], r["v"], r["mix"]
    middle, total, slide = r["middle"], r["total"], r["slide"]
    normed_two, turned_two, hid, dbs = r["normed_two"], r["turned_two"], r["hid"], r["dbs"]
    sums, bias = r["sums"], r["bias"]
    rows_all, width = x.shape
    part = a.shape[2]
    units = f.shape[3]
    windows = rows_all // PAD
    half_rows = rows_all // 2
    columns = width // TILE
    halves_of_rows = [slice(0, half_rows), slice(half_rows, rows_all)]
    blocks = []
    for window in range(windows // 2):
        for start in range(0, part, LANES):
            blocks.append((window, start, min(2, (part - start) // HALF)))

    weights = [
        (r["own_a"].at[0:3], lambda s: a.at[s, 0:3]),
        (r["own_a"].at[3:4], lambda s: a.at[s, 3:4]),
        (r["own_f"], lambda s: f.at[s]),
        (r["own_g"], lambda s: g.at[s]),
    ]
    own_copy = [
        pltpu.make_async_copy(src, dst, r["local"].at[i])
        for i, (src, dst) in enumerate(
            [(r["own_a"], a.at[me]), (r["own_f"], f.at[me]), (r["own_g"], g.at[me]), (r["own_bias"], bias.at[me])]
        )
    ]

    def z_copy(w, other, arriving):
        src, dst = weights[w]
        owner = other if arriving else me
        block = place.flips()[0]
        return remote(
            piece(src, block, c),
            piece(dst(owner), block, c),
            r["z_send"].at[w, other],
            r["z_recv"].at[w, owner],
            (place.d, other),
        )

    def bias_copy(other, arriving):
        owner = other if arriving else me
        return remote(r["own_bias"], bias.at[owner], r["b_send"].at[other], r["b_recv"].at[owner], (place.d, other))

    def spread(w, s):
        return Spread(place, weights[w][1](s), r["p_send"], r["p_recv"], (w, s))

    def send(w):
        repeat(tp, lambda j: z_copy(w, place.other(tp - j), False).start(), 1)

    def first(w, j):
        z_copy(w, place.other(j), True).wait_recv()
        spread(w, place.other(j)).start_own()

    def second(w, j):
        spread(w, place.other(j)).after_first()

    def third(w, j):
        spread(w, place.other(j)).after_second()

    def ready(w, j):
        spread(w, place.other(j)).ready()

    def sent(w, j):
        spread(w, place.other(j)).sent()
        z_copy(w, place.other(j), False).wait_send()

    grads = [ga, f, g]
    halves, quarters, eighths, arrived, final = ([r[name + str(w)] for w in range(3)] for name in ("h", "u", "e", "t", "o"))
    outs = [r["out_a"], r["out_f"], r["out_g"]]

    def rows_of(block, size):
        return pl.ds(pl.multiple_of(block * size, size), size)

    def lanes_of(w, side):
        count = grads[w].shape[-1] // 2
        return pl.ds(pl.multiple_of(side * count, count), count)

    def core_copy(w, s):
        return remote(
            grads[w].at[s, :, :, lanes_of(w, 1 - c)],
            halves[w].at[s],
            r["core_send"].at[w, s],
            r["core_recv"].at[w, s],
            (place.core, me),
        )

    def quarter_copy(w, s, two):
        size = eighths[w].shape[2]
        return remote(
            halves[w].at[s, :, rows_of(place.block(1 - one_bit, two), size)],
            quarters[w].at[s, :, two * size : (two + 1) * size],
            r["one_send"].at[w, s, two],
            r["one_recv"].at[w, s, two],
            (place.first, me),
        )

    def eighth_copy(w, s):
        size = eighths[w].shape[2]
        return remote(
            quarters[w].at[s, :, rows_of(1 - two_bit, size)],
            eighths[w].at[s],
            r["two_send"].at[w, s],
            r["two_recv"].at[w, s],
            (place.second, me),
        )

    def shard_copy(w, other, arriving):
        owner = other if arriving else me
        return remote(
            eighths[w].at[other], arrived[w].at[owner], r["s_send"].at[w, other], r["s_recv"].at[w, owner], (place.d, other)
        )

    def reduce_one(w, s):
        core_copy(w, s).start()

    def reduce_two(w, s):
        core_copy(w, s).wait_recv()
        size = eighths[w].shape[2]

        def add(block):
            rows = rows_of(block, size)
            halves[w][s, :, rows] += grads[w][s, :, rows, lanes_of(w, c)]

        for two in range(2):
            add(place.block(1 - one_bit, two))
            quarter_copy(w, s, two).start()
        for two in range(2):
            add(place.block(one_bit, two))

    def reduce_three(w, s):
        size = eighths[w].shape[2]
        for two in range(2):
            quarter_copy(w, s, two).wait_recv()

        def add(two):
            rows = rows_of(two, size)
            quarters[w][s, :, rows] += halves[w][s, :, rows_of(place.block(one_bit, two), size)]

        add(1 - two_bit)
        eighth_copy(w, s).start()
        add(two_bit)

    def reduce_four(w, j):
        s = place.other(j)
        eighth_copy(w, s).wait_recv()
        eighths[w][s] += quarters[w][s, :, rows_of(two_bit, eighths[w].shape[2])]
        if j > 0:
            shard_copy(w, s, False).start()

    def out_spread(w):
        return Spread(place, outs[w], r["q_send"], r["q_recv"], (w,))

    def reduce_five(w):
        repeat(tp, lambda j: shard_copy(w, place.other(j), True).wait_recv(), 1)
        arrived[w][me] = eighths[w][me]
        value = arrived[w][0].astype(f32)
        for s in range(1, tp):
            value += arrived[w][s].astype(f32)
        final[w][...] = value.astype(bf16)
        for i, peer in enumerate(place.extra):
            copy = remote(final[w], r["x" + str(w)].at[i], r["x_send"].at[w, i], r["x_recv"].at[w, i], (peer, me))
            copy.start()
            copy.wait()
            final[w][...] += r["x" + str(w)][i]
        put = pltpu.make_async_copy(final[w], piece(outs[w], place.flips()[0], c), r["put"].at[w])
        put.start()
        put.wait()
        out_spread(w).start_own()

    def reduce_done(w):
        out_spread(w).ready()
        out_spread(w).sent()

        def one(j):
            s = place.other(j)
            core_copy(w, s).wait_send()
            for two in range(2):
                quarter_copy(w, s, two).wait_send()
            eighth_copy(w, s).wait_send()

        repeat(tp, one)
        repeat(tp, lambda j: shard_copy(w, place.other(j), False).wait_send(), 1)

    levels = [place.core, place.x, place.y] + place.extra
    table = r["table"]
    small = [(sums, r["sums_in"], r["sums_z"], r["sums_out"]), (r["fold"], r["fold_in"], r["fold_z"], r["fold_out"])]

    def small_copy(i, level):
        return remote(
            small[i][0], small[i][1].at[level], r["v_send"].at[i, level], r["v_recv"].at[i, level], (levels[level], me)
        )

    def small_start(level):
        for i in range(2):
            small_copy(i, level).start()

    def small_level(level):
        for i in range(2):
            small_copy(i, level).wait()
            small[i][0][...] += small[i][1][level]
        if level + 1 < len(levels):
            small_start(level + 1)

    def small_shard(i, other, arriving):
        owner = other if arriving else me
        return remote(small[i][0], small[i][2].at[owner], r["vz_send"].at[i, other], r["vz_recv"].at[i, owner], (place.d, other))

    def small_across():
        for i in range(2):
            repeat(tp, lambda j: small_shard(i, place.other(j), False).start(), 1)

    def small_finish():
        for i in range(2):
            repeat(tp, lambda j: small_shard(i, place.other(j), True).wait_recv(), 1)
            small[i][2][me] = small[i][0][...]
            value = small[i][2][0]
            for s in range(1, tp):
                value += small[i][2][s]
            small[i][3][...] = value
            repeat(tp, lambda j: small_shard(i, place.other(j), False).wait_send(), 1)

    def chunk(i):
        return pl.ds(pl.multiple_of(i * CHUNK, CHUNK), CHUNK)

    chunks = rows_all // CHUNK

    def keep_rows(rows, count):
        keep = (fill[rows] == 0.0).astype(f32)
        return jnp.concatenate([keep] * (count // LANES), axis=1)

    def norm_one(i):
        rows = chunk(i)
        normal, _ = normal_rows(x[rows].astype(f32))
        normed[rows] = (normal * vec[0:1] + vec[1:2]).astype(bf16)

    def project(s):
        for t, target in enumerate((q, k, v)):
            for rows in halves_of_rows:
                value = dot(normed[rows], a[s, t], NT)
                if t != 1:
                    value = value + bias[s, 1 + t // 2 : 2 + t // 2, :part]
                target[s, rows, :part] = value.astype(bf16)

    def unit_view(ref, s, at):
        return ref.at[s, pl.ds(pl.multiple_of(at * half_rows, half_rows), half_rows)]

    def p_out(i):
        return pltpu.make_async_copy(r["p"].at[i % 2], r["p_hbm"].at[i], r["p_sem"].at[i % 2])

    def p_in(i):
        return pltpu.make_async_copy(r["p_hbm"].at[i], r["p"].at[i % 2], r["p_sem"].at[i % 2])

    def attend(i, s, at):
        attend_forward_unit(
            unit_view(q, s, at),
            unit_view(k, s, at),
            unit_view(v, s, at),
            unit_view(mix, s, at),
            r["p"].at[i % 2],
            fill.at[pl.ds(pl.multiple_of(at * half_rows, half_rows), half_rows)],
            r["rel"],
            r["hot"],
            r["scr_a"],
            blocks,
        )

    def attend_back(i, s, at):
        views = [unit_view(ref, s, at) for ref in (q, k, v)]
        attend_backward_unit(
            *views, unit_view(mix, s, at), r["p"].at[i % 2], *views, table, r["relt"], r["hott"], r["scr_b"], blocks
        )

    def mix_out(n):
        tile = pl.ds(pl.multiple_of(n * TILE, TILE), TILE)
        for rows in halves_of_rows:
            value = dot(mix[0, rows, :part], a[0, 3, :, tile])
            for s in range(1, tp):
                value = value + dot(mix[s, rows, :part], a[s, 3, :, tile])
            middle[rows, tile] = x[rows, tile].astype(f32) + keep_rows(rows, TILE) * (value + vec[4:5, tile])

    def norm_two(i):
        rows = chunk(i)
        value = middle[rows]
        normal, _ = normal_rows(value)
        normed_two[rows] = (normal * vec[2:3] + vec[3:4]).astype(bf16)
        total[rows] = value + keep_rows(rows, width) * vec[5:6]
        slide[rows] = jnp.zeros_like(value)

    def layers(s):
        def one(n):
            tile = pl.ds(pl.multiple_of(n * TILE, TILE), TILE)
            column = None
            for rows in halves_of_rows:
                before = dot(normed_two[rows], f[s, 0, :, tile]) + bias[s, 0:1, tile]
                keep = keep_rows(rows, TILE)
                phi = 0.5 * (1.0 + lax.erf(before * root_half))
                hid[rows, tile] = (before * phi * keep).astype(bf16)
                slope = phi + before * (jnp.exp(-0.5 * before * before) * bell)
                down = (slope * (dot(cot[rows], g[s, 0, tile, :], NT) * keep)).astype(bf16)
                dbs[rows, tile] = down
                part_sum = jnp.sum(down.astype(f32), axis=0, keepdims=True)
                column = part_sum if column is None else column + part_sum
            r["layer_sum"][s, 0:1, tile] = column

        repeat(units // TILE, one)

    def layers_add(s):
        def one(n):
            tile = pl.ds(pl.multiple_of(n * TILE, TILE), TILE)
            for rows in halves_of_rows:
                total[rows, tile] += dot(hid[rows], g[s, 0, :, tile])
                slide[rows, tile] += dot(dbs[rows], f[s, 0, tile, :], NT)

        repeat(columns, one)

    def layers_grad(s):
        def one(n):
            tile = pl.ds(pl.multiple_of(n * TILE, TILE), TILE)
            g[s, 0, tile, :] = dot(hid[:, tile], cot[...], TN).astype(bf16)
            f[s, 0, :, tile] = dot(turned_two[...], dbs[:, tile]).astype(bf16)

        repeat(units // TILE, one)

    def middle_back(i):
        rows = chunk(i)
        hid[rows, :width] = total[rows].astype(bf16)
        keep = keep_rows(rows, width)
        gradient = slide[rows]
        normal, scale = normal_rows(middle[rows])
        outer = cot[rows].astype(f32)
        down = outer + normal_back(gradient, normal, scale, vec[2:3])
        slide[rows] = down
        masked = down * keep
        dbs[rows, :width] = masked.astype(bf16)
        total[rows] = jnp.zeros_like(down)
        add = lambda at, value: sums.__setitem__(
            (slice(at, at + 1), slice(None)), sums[at : at + 1] + jnp.sum(value, axis=0, keepdims=True)
        )
        add(1, gradient * normal)
        add(3, gradient)
        add(4, masked)
        add(5, outer * keep)

    def mix_back(s):
        ga[s, 3] = dot(mix[s, :, :part], dbs[:, :width], TN).astype(bf16)
        for rows in halves_of_rows:
            mix[s, rows, :part] = dot(dbs[rows, :width], a[s, 3], NT).astype(bf16)

    def project_back(s):
        for t, source in enumerate((q, k, v)):
            ga[s, t] = dot(source[s, :, :part], normed[...], TN).astype(bf16)
        for i, source in ((0, q), (1, v)):
            value = jnp.sum(source[s, :, :part].astype(f32), axis=0, keepdims=True)
            r["head_sum"][s, i : i + 1, :part] = value

        def one(n):
            tile = pl.ds(pl.multiple_of(n * TILE, TILE), TILE)
            for rows in halves_of_rows:
                total[rows, tile] += (
                    dot(q[s, rows, :part], a[s, 0, :, tile])
                    + dot(k[s, rows, :part], a[s, 1, :, tile])
                    + dot(v[s, rows, :part], a[s, 2, :, tile])
                )

        repeat(columns, one)

    def input_back(i):
        rows = chunk(i)
        gradient = total[rows]
        normal, scale = normal_rows(x[rows].astype(f32))
        middle[rows] = slide[rows] + normal_back(gradient, normal, scale, vec[0:1])
        sums[0:1] = sums[0:1] + jnp.sum(gradient * normal, axis=0, keepdims=True)
        sums[2:3] = sums[2:3] + jnp.sum(gradient, axis=0, keepdims=True)

    def run(events, index):
        for at, steps in events.items():

            @pl.when(index == at)
            def _(steps=steps):
                for fn, *args in steps:
                    fn(*args)

    everyone = list(range(1, tp))
    last = tp - 1
    each = lambda fn, w: [(fn, w, j) for j in everyone]

    for copy in own_copy:
        copy.start()
    place.greet_start()
    repeat(chunks, norm_one)
    lead = part - part % LANES
    if lead < part:
        for ref in (q, k, v, mix):
            for s in range(tp):
                ref[s, :, lead:] = jnp.zeros((rows_all, LANES), bf16)
    sums[...] = jnp.zeros_like(sums)
    table[...] = jnp.zeros_like(table)
    r["scr_b"][...] = jnp.zeros_like(r["scr_b"])
    place.greet_wait()
    send(0)
    repeat(tp, lambda j: bias_copy(place.other(tp - j), False).start(), 1)
    send(1)
    own_copy[0].wait()
    own_copy[3].wait()

    before_project, before_unit = gather_events(
        tp, dict(send=send, first=first, second=second, third=third, ready=ready, bias=lambda: repeat(tp, lambda j: bias_copy(place.other(j), True).wait_recv(), 1))
    )

    def forward_unit(i):
        j, at = i // 2, i % 2
        s = place.other(j)

        @pl.when(at == 0)
        def _():
            run(before_project, j)
            project(s)

        run(before_unit, i)

        @pl.when(i >= 2)
        def _():
            p_out(i - 2).wait()

        attend(i, s, at)
        p_out(i).start()

    unit_count = 2 * tp
    repeat(unit_count, forward_unit)
    p_out(unit_count - 2).wait()
    p_out(unit_count - 1).wait()
    for j in everyone:
        ready(1, j)
    repeat(columns, mix_out)
    repeat(chunks, norm_two)
    turned_two[...] = normed_two[...].T
    own_copy[1].wait()
    own_copy[2].wait()

    stages = layer_events(tp, dict(send=send, first=first, second=second, third=third, ready=ready, sent=sent, one=reduce_one, two=reduce_two, three=reduce_three, four=reduce_four, other=place.other))

    def layer_step(j):
        s = place.other(j)
        run(stages[0], j)
        layers(s)
        run(stages[1], j)
        layers_add(s)
        run(stages[2], j)
        layers_grad(s)
        run(stages[3], j)

    repeat(tp, layer_step)

    repeat(chunks, middle_back)
    put_out = pltpu.make_async_copy(hid.at[:, :width], r["out"], r["local"].at[1])
    put_out.start()
    back = back_events(tp, dict(sent=sent, one=reduce_one, two=reduce_two, three=reduce_three, four=reduce_four, five=reduce_five, after_first=lambda w: out_spread(w).after_first(), after_second=lambda w: out_spread(w).after_second(), other=place.other))
    run({0: back["start"]}, 0)
    p_in(0).start()
    repeat(tp, lambda j: mix_back(place.other(j)))

    def backward_unit(i):
        j, at = i // 2, i % 2
        s = place.other(j)
        run(back["unit"], i)

        @pl.when(i + 1 < unit_count)
        def _():
            p_in(i + 1).start()

        p_in(i).wait()
        attend_back(i, s, at)

        @pl.when(at == 1)
        def _():
            project_back(s)
            run(back["shard"], j)

    repeat(unit_count, backward_unit)
    repeat(chunks, input_back)
    put_in = pltpu.make_async_copy(middle, r["grad_x"], r["local"].at[2])
    put_in.start()
    for s in range(tp):
        for n in range(units // width):
            at = 8 + s * (units // width) + n
            sums[at : at + 1] = r["layer_sum"][s, 0:1, n * width : (n + 1) * width]
        sums[16 + s : 17 + s, :part] = r["head_sum"][s, 0:1, :part]
        sums[16 + s : 17 + s, width // 2 : width // 2 + part] = r["head_sum"][s, 1:2, :part]
    r["fold"][...] = table[:HALF, :HALF] + table[HALF:, HALF:]
    small_start(0)
    two, three, four = reduce_two, reduce_three, reduce_four
    s = place.other(last)
    two(0, s)
    small_level(0)
    three(0, s)
    small_level(1)
    four(0, last)
    for level in range(2, len(levels)):
        small_level(level)
    small_across()
    reduce_five(0)
    out_spread(0).after_first()
    small_finish()
    out_spread(0).after_second()
    for w in (2, 1, 0):
        reduce_done(w)
    for j in everyone:
        sent(0, j)
        sent(1, j)
    repeat(tp, lambda j: bias_copy(place.other(tp - j), False).wait_send(), 1)
    put_out.wait()
    put_in.wait()


def gather_events(tp, do):
    every = list(range(1, tp))
    project, unit = {}, {}
    at = lambda table, key, *step: table.setdefault(key, []).append(step)
    unit_of = lambda i: min(i, 2 * tp - 1)
    at(unit, 0, do["first"], 0, 1)
    at(unit, 1, do["second"], 0, 1)
    for j in every[1:]:
        at(unit, 1, do["first"], 0, j)
    at(project, 1, do["third"], 0, 1)
    for j in every[1:]:
        at(project, 1, do["second"], 0, j)
    at(project, 1, do["bias"])
    at(project, 1, do["ready"], 0, 1)
    for j in every[1:]:
        at(unit, unit_of(2), do["third"], 0, j)
    at(unit, unit_of(2), do["send"], 2)
    for j in every:
        at(unit, unit_of(3), do["first"], 1, j)
    for j in every[1:]:
        at(project, j, do["ready"], 0, j)
    for j in every:
        at(unit, unit_of(4), do["second"], 1, j)
    at(unit, unit_of(4), do["send"], 3)
    for j in every:
        at(unit, unit_of(5), do["third"], 1, j)
        at(unit, unit_of(5), do["first"], 2, j)
    for j in every:
        at(unit, unit_of(6), do["second"], 2, j)
    for j in every:
        at(unit, unit_of(7), do["third"], 2, j)
        at(unit, unit_of(7), do["first"], 3, j)
    return project, unit


def layer_events(tp, do):
    every = list(range(1, tp))
    stages = [{}, {}, {}, {}]
    at = lambda stage, key, *step: stages[stage].setdefault(key, []).append(step)
    for j in every:
        at(0, 0, do["second"], 3, j)
    for j in every:
        at(1, 0, do["third"], 3, j)
    for j in every:
        at(0, j, do["ready"], 2, j)
        at(0, j, do["ready"], 3, j)
        at(2, j, do["sent"], 2, j)
        at(2, j, do["sent"], 3, j)
    for j in range(tp):
        for w in (2, 1):
            at(3, j, do["one"], w, do["other"](j))
    for j in every:
        for w in (2, 1):
            at(1, j, do["two"], w, do["other"](j - 1))
        for w in (2, 1):
            at(3, j, do["three"], w, do["other"](j - 1))
    for j in every[1:]:
        for w in (2, 1):
            at(2, j, do["four"], w, j - 2)
    return stages


def back_events(tp, do):
    unit, shard, start = {}, {}, []
    at = lambda table, key, *step: table.setdefault(key, []).append(step)
    last = tp - 1
    for w in (2, 1):
        start.append((do["two"], w, do["other"](last)))
    for w in (2, 1):
        if last > 0:
            at(unit, 0, do["four"], w, last - 1)
    for w in (2, 1):
        at(unit, 0, do["three"], w, do["other"](last))
    for w in (2, 1):
        at(unit, 1, do["four"], w, last)
    for w in (2, 1):
        at(unit, 2, do["five"], w)
    for w in (2, 1):
        at(unit, 3, do["after_first"], w)
    for w in (2, 1):
        at(unit, 3, do["after_second"], w)
    for j in range(tp):
        at(shard, j, do["one"], 0, do["other"](j))
        if j > 0:
            at(unit, 2 * j, do["two"], 0, do["other"](j - 1))
            at(unit, 2 * j + 1, do["three"], 0, do["other"](j - 1))
            at(shard, j, do["four"], 0, j - 1)
    return dict(unit=unit, shard=shard, start=start)


def whole_block(tp, dp, x, cot, fill, vec, own_a, own_f, own_g, own_bias, rel, relt, hot, hott):
    rows, width = x.shape
    part = own_a.shape[1]
    units = own_f.shape[2]
    heads = (rows // PAD // 2) * (part // HEAD_DIM)
    wide = -(-part // LANES) * LANES
    unit_count = 2 * tp
    any_space = pl.BlockSpec(memory_space=pl.ANY)
    vmem = pl.BlockSpec(memory_space=pltpu.VMEM)
    dma = pltpu.SemaphoreType.DMA
    inputs = [
        ("x", x, vmem),
        ("cot", cot, vmem),
        ("fill", fill, vmem),
        ("vec", vec, vmem),
        ("own_a", own_a, any_space),
        ("own_f", own_f, any_space),
        ("own_g", own_g, any_space),
        ("own_bias", own_bias, any_space),
        ("rel", rel, vmem),
        ("relt", relt, vmem),
        ("hot", hot, vmem),
        ("hott", hott, vmem),
    ]
    shape = jax.ShapeDtypeStruct
    outputs = [
        ("out", shape((rows, width), bf16), any_space),
        ("grad_x", shape((rows, width), f32), any_space),
        ("out_a", shape(own_a.shape, bf16), any_space),
        ("out_f", shape(own_f.shape, bf16), any_space),
        ("out_g", shape(own_g.shape, bf16), any_space),
        ("sums_out", shape((24, width), f32), vmem),
        ("fold_out", shape((HALF, HALF), f32), vmem),
        ("p_hbm", shape((unit_count, heads, PAD, PAD), bf16), any_space),
    ]
    buffer = lambda dims, kind: pltpu.VMEM(tuple(dims), kind)
    scratch = [
        ("a", buffer((tp,) + own_a.shape, bf16)),
        ("f", buffer((tp,) + own_f.shape, bf16)),
        ("g", buffer((tp,) + own_g.shape, bf16)),
        ("ga", buffer((tp,) + own_a.shape, bf16)),
        ("bias", buffer((tp,) + own_bias.shape, f32)),
        ("normed", buffer((rows, width), bf16)),
    ]
    scratch += [(name, buffer((tp, rows, wide), bf16)) for name in ("q", "k", "v", "mix")]
    scratch += [("p", buffer((2, heads, PAD, PAD), bf16))]
    scratch += [(name, buffer((rows, width), f32)) for name in ("middle", "total", "slide")]
    scratch += [("normed_two", buffer((rows, width), bf16)), ("turned_two", buffer((width, rows), bf16))]
    scratch += [(name, buffer((rows, units), bf16)) for name in ("hid", "dbs")]
    scratch += [
        ("sums", buffer((24, width), f32)),
        ("table", buffer((LANES, LANES), f32)),
        ("fold", buffer((HALF, HALF), f32)),
        ("layer_sum", buffer((tp, 8, units), f32)),
        ("head_sum", buffer((tp, 8, wide), f32)),
        ("scr_a", buffer((heads, HALF, PAD), f32)),
        ("scr_b", buffer((heads, 2, 48, PAD), f32)),
    ]
    levels = dp.bit_length() - 1
    more = levels - 3
    for w, own in enumerate((own_a, own_f, own_g)):
        n, count, lanes = own.shape[0], own.shape[1], own.shape[2] // 2
        scratch += [
            ("h" + str(w), buffer((tp, n, count, lanes), bf16)),
            ("u" + str(w), buffer((tp, n, count // 2, lanes), bf16)),
            ("e" + str(w), buffer((tp, n, count // 4, lanes), bf16)),
            ("t" + str(w), buffer((tp, n, count // 4, lanes), bf16)),
            ("o" + str(w), buffer((n, count // 4, lanes), bf16)),
        ]
        if more:
            scratch += [("x" + str(w), buffer((more, n, count // 4, lanes), bf16))]
    for name, dims in (("sums", (24, width)), ("fold", (HALF, HALF))):
        scratch += [(name + "_in", buffer((levels,) + dims, f32)), (name + "_z", buffer((tp,) + dims, f32))]
    semaphores = dict(local=(4,), p_sem=(2,), put=(3,))
    for name, dims in dict(
        z=(4, tp), p=(4, tp, 7), b=(tp,), core=(3, tp), one=(3, tp, 2), two=(3, tp), s=(3, tp), q=(3, 7), x=(3, max(more, 1)), v=(2, levels), vz=(2, tp)
    ).items():
        semaphores[name + "_send"] = semaphores[name + "_recv"] = dims
    scratch += [(name, dma(dims)) for name, dims in semaphores.items()]
    names = [entry[0] for entry in inputs + outputs + scratch]
    return pl.pallas_call(
        lambda *refs: block_kernel(tp, dp, names, *refs),
        in_specs=[entry[2] for entry in inputs],
        out_specs=[entry[2] for entry in outputs],
        out_shape=[entry[1] for entry in outputs],
        scratch_shapes=[entry[1] for entry in scratch],
        compiler_params=pltpu.CompilerParams(collective_id=1, has_side_effects=True, vmem_limit_bytes=VMEM_LIMIT),
    )(*[entry[1] for entry in inputs])


def pad_windows(rows):
    windows = rows.shape[0] // SLOTS
    cut = rows.reshape((windows, SLOTS) + rows.shape[1:])
    return jnp.pad(cut, ((0, 0), (0, PAD - SLOTS), (0, 0))).reshape((windows * PAD,) + rows.shape[1:])


def cut_windows(rows):
    windows = rows.shape[0] // PAD
    return rows.reshape((windows, PAD) + rows.shape[1:])[:, :SLOTS].reshape((windows * SLOTS,) + rows.shape[1:])


def keep_slots(height, breadth, windows):
    first = lax.axis_index("tp") * windows
    window = (first + jnp.arange(windows, dtype=jnp.int32))[:, None]
    inside = jnp.arange(PAD, dtype=jnp.int32)[None, :]
    row_at = window // GRID * WIN + inside // WIN
    column_at = window % GRID * WIN + inside % WIN
    real = inside < SLOTS
    return (row_at < height) & (column_at < breadth) & real, real


def body(
    tokens,
    heights,
    widths,
    norm_gain,
    norm_bias,
    w_qkv,
    b_qv,
    rel_pos,
    w_proj,
    b_proj,
    w_fc1,
    b_fc1,
    w_fc2,
    b_fc2,
    cotangent,
):
    tp, dp = lax.axis_size("tp"), lax.axis_size("dp")
    width = tokens.shape[1]
    windows = tokens.shape[0] // SLOTS
    part, units = w_qkv.shape[2], w_fc1.shape[1]
    keep, real = keep_slots(heights[0], widths[0], windows)
    fill = jnp.where(keep, 0.0, jnp.where(real, neg_fill, pad_fill)).astype(f32)
    fill = jnp.broadcast_to(fill.reshape(-1, 1), (windows * PAD, LANES))
    vec = jnp.concatenate([norm_gain[0:1], norm_bias[0:1], norm_gain[1:2], norm_bias[1:2], b_proj[None], b_fc2[None]])
    vec = jnp.pad(vec.astype(f32), ((0, 2), (0, 0)))
    biases = jnp.concatenate([b_fc1[None].astype(f32), jnp.pad(b_qv.astype(f32), ((0, 0), (0, units - part)))])
    biases = jnp.pad(biases, ((0, 5), (0, 0)))
    turned = jnp.concatenate([w_qkv.transpose(0, 2, 1), w_proj[None]], axis=0)
    rel, relt = position_matrices(rel_pos)
    hot, hott = window_constants()
    out, grad_x, out_a, out_f, out_g, sums, fold, _ = whole_block(
        tp, dp, pad_windows(tokens), pad_windows(cotangent), fill, vec, turned, w_fc1[None], w_fc2[None], biases, rel, relt, hot, hott
    )
    me = lax.axis_index("tp")
    offsets = 2 * WIN - 1
    grad_rel = jnp.stack([fold[:offsets], fold[32 : 32 + offsets]])[:, ::-1, :]
    per = units // width
    mine = lax.dynamic_slice_in_dim(sums, 16 + me, 1, 0)
    return (
        cut_windows(out),
        cut_windows(grad_x),
        sums[0:2],
        sums[2:4],
        out_a[:3].transpose(0, 2, 1).astype(f32),
        jnp.concatenate([mine[:, :part], mine[:, width // 2 : width // 2 + part]]),
        grad_rel,
        out_a[3].astype(f32),
        sums[4],
        out_f[0].astype(f32),
        lax.dynamic_slice_in_dim(sums, 8 + me * per, per, 0).reshape(-1),
        out_g[0].astype(f32),
        sums[5],
    )


def solution(mesh):
    rows = P(("dp", "tp"), None)
    return jax.shard_map(
        body,
        mesh=mesh,
        in_specs=(
            rows,
            P("dp"),
            P("dp"),
            P(),
            P(),
            P(None, None, "tp"),
            P(None, "tp"),
            P(),
            P("tp", None),
            P(),
            P(None, "tp"),
            P("tp"),
            P("tp", None),
            P(),
            rows,
        ),
        out_specs=(
            rows,
            rows,
            P(),
            P(),
            P(None, None, "tp"),
            P(None, "tp"),
            P(),
            P("tp", None),
            P(),
            P(None, "tp"),
            P("tp"),
            P("tp", None),
            P(),
        ),
        check_vma=False,
    )
```

```python
import jax
import jax.numpy as jnp
import ml_dtypes
import numpy as np
from jax import lax
from jax.experimental import pallas as pl
from jax.experimental.pallas import tpu as pltpu
from jax.sharding import PartitionSpec as P

HEAD_DIM = 64
WIN = 14
GRID = 4
SLOTS = WIN * WIN
PAD = 208
LANES = 128
HALF = 64
CHUNK = 64
ENDS = 16
PLACES = [
    ("start", 0, ("send", 0, 1), ("send", 0, 2), ("first", 0, 1), ("send", 0, 3)),
    ("project", 0, ("second", 0, 1), ("send", 1, 1)),
    ("unit", 0, ("first", 0, 2), ("third", 0, 1), ("first", 0, 3)),
    ("unit", 1, ("ready", 0, 1), ("send", 1, 3)),
    ("project", 1, ("bias_ready",), ("second", 0, 2)),
    ("unit", 2, ("second", 0, 3)),
    ("unit", 3, ("third", 0, 2), ("first", 1, 1)),
    ("project", 2, ("send", 1, 2), ("ready", 0, 2), ("third", 0, 3)),
    ("unit", 5, ("ready", 0, 3), ("first", 1, 3)),
    ("mid1", 0, ("second", 1, 1)),
    ("layers", 2, ("first", 1, 2)),
    ("add", 0, ("third", 1, 1)),
    ("grad", 0, ("second", 1, 3), ("z_sent", 1)),
    ("layers", 3, ("ready", 1, 1)),
    ("layers", 5, ("one", 1, 0), ("second", 1, 2)),
    ("add", 5, ("third", 1, 3)),
    ("grad", 3, ("two", 1, 0), ("third", 1, 2), ("sent", 1, 1)),
    ("layer3", 1, ("ready", 1, 3)),
    ("layers", 6, ("one", 1, 1), ("ready", 1, 2)),
    ("grad", 6, ("three", 1, 0), ("two", 1, 1), ("sent", 1, 2)),
    ("layers", 11, ("one", 1, 2)),
    ("add", 11, ("two", 1, 2)),
    ("grad", 9, ("sent", 1, 3)),
    ("layer3", 3, ("three", 1, 1)),
    ("down0", 0, ("one", 1, 3)),
    ("down2", 0, ("s0", 0), ("three", 1, 2), ("two", 1, 3)),
    ("back", 1, ("four", 1, 1)),
    ("shard", 0, ("one", 0, 0)),
    ("back", 2, ("s1", 0)),
    ("turn", 1, ("four", 1, 2), ("two", 0, 0)),
    ("shard", 1, ("one", 0, 1)),
    ("back", 4, ("three", 1, 3)),
    ("back", 5, ("two", 0, 1)),
    ("turn", 2, ("s2", 0)),
    ("back", 6, ("three", 0, 0), ("one", 0, 2)),
    ("turn", 3, ("two", 0, 2), ("four", 1, 3)),
    ("end0", 0, ("three", 0, 1), ("one", 0, 3)),
    ("end1", 0, ("four", 1, 0), ("three", 0, 2)),
    ("end2", 0, ("two", 0, 3), ("four", 0, 1)),
    ("end3", 0, ("five", 1)),
    ("end4", 0, ("four", 0, 2), ("three", 0, 3)),
    ("end5", 0, ("four", 0, 0), ("four", 0, 3), ("s0", 1)),
    ("end6", 0, ("s1", 1)),
    ("end7", 0, ("after_first", 1), ("s2", 1)),
    ("end8", 0, ("s3", 0), ("five", 0)),
    ("end9", 0, ("after_second", 1)),
    ("end11", 0, ("s4", 0), ("s3", 1)),
    ("end12", 0, ("after_first", 0), ("after_second", 0)),
    ("end13", 0, ("done", 1)),
    ("end14", 0, ("s4", 1)),
    ("end15", 0, ("done", 0)),
]
TILE = 256

bf16 = jnp.bfloat16
f32 = jnp.float32
neg_fill = -30000.0
pad_fill = -1e30
root_half = 0.7071067811865476
bell = 0.3989422804014327
VMEM_LIMIT = 64 << 20
MESH = pl.DeviceIdType.MESH


def dot(a, b, dims=((1,), (0,))):
    return lax.dot_general(a, b, (dims, ((), ())), preferred_element_type=f32)


NT = ((1,), (1,))
TN = ((0,), (0,))


def window_constants():
    slot = np.arange(PAD)[:, None]
    lane = np.arange(HALF)[None, :]
    place = np.where(lane % 32 < 16, slot // WIN, slot % WIN)
    hot = ((slot < SLOTS) & (lane % 16 == place)).astype(np.float32)
    zero = np.zeros_like(hot)
    both = np.concatenate([np.concatenate([hot, zero], 1), np.concatenate([zero, hot], 1)], 0)
    pick = np.zeros((LANES, HALF), np.float32)
    for offset in range(2 * WIN - 1):
        for head in range(2):
            for axis in range(2):
                pick[HALF * head + 32 * axis + offset, 32 * axis + 2 * WIN - 2 - offset] = 8.0
    narrow = lambda values: values.astype(ml_dtypes.bfloat16)
    return narrow(both), narrow(hot[:, :32].T.copy()), narrow(pick)


def stack_heads(pair, heads):
    if heads == 1:
        return pair
    lane = lax.broadcasted_iota(jnp.int32, pair.shape, 1)
    zero = jnp.zeros_like(pair)
    return jnp.concatenate([jnp.where(lane < HALF, pair, zero), jnp.where(lane < HALF, zero, pair)], axis=0)


def merge_heads(stacked, heads):
    if heads == 1:
        return stacked
    top, bottom = stacked[:PAD], stacked[PAD:]
    lane = lax.broadcasted_iota(jnp.int32, top.shape, 1)
    return jnp.where(lane < HALF, top, bottom)


def place_of_lane():
    lane = lax.broadcasted_iota(jnp.int32, (1, PAD), 1)
    row = lax.div(lane, WIN)
    return row, lane - row * WIN


def attend_forward_unit(q_ref, k_ref, v_ref, mix_ref, p_ref, fill_ref, rel_ref, hot_ref, scr_ref, blocks):
    places = place_of_lane()
    eighth = jnp.asarray(0.125, bf16)
    firsts, scores, biases = [], [], []
    count = 0
    for window, start, heads in blocks:
        firsts.append(count)
        lanes, rows = slice(start, start + LANES), slice(window * PAD, (window + 1) * PAD)
        left = jnp.concatenate([rel_ref[: heads * HALF], stack_heads(k_ref[rows, lanes], heads)], axis=0)
        both = dot(left, q_ref[rows, lanes] * eighth, NT)
        for head in range(heads):
            scr_ref[count + head] = both[head * HALF : (head + 1) * HALF]
        scores.append(both[heads * HALF :])
        count += heads
    for b, (window, start, heads) in enumerate(blocks):
        parts = []
        for head in range(heads):
            along = []
            for base, place in ((0, places[0]), (32, places[1])):
                picked = scr_ref[firsts[b] + head, base : base + 16, :]
                for at in range(WIN - 1):
                    first = base + WIN - 1 - at
                    picked = jnp.where(place == at, scr_ref[firsts[b] + head, first : first + 16, :], picked)
                along.append(picked)
            bias = jnp.concatenate(along, axis=0)
            high = bias.astype(bf16)
            parts += [high, (bias - high.astype(f32)).astype(bf16)]
        biases.append(jnp.concatenate(parts, axis=0))
    for b, (window, start, heads) in enumerate(blocks):
        scores[b] = scores[b] + dot(hot_ref[: heads * PAD, : heads * HALF], biases[b])
    for b, (window, start, heads) in enumerate(blocks):
        fill = fill_ref[window * PAD : (window + 1) * PAD]
        fill = jnp.concatenate([fill, fill[:, : PAD - LANES]], axis=1)
        for head in range(heads):
            one = scores[b][head * PAD : (head + 1) * PAD]
            one = jnp.where(fill == 0.0, one, fill)
            weights = jnp.exp(one - jnp.max(one, axis=0, keepdims=True))
            total = jnp.sum(weights, axis=0, keepdims=True)
            p_ref[firsts[b] + head] = (weights * (1.0 / total)).astype(bf16)
    for b, (window, start, heads) in enumerate(blocks):
        lanes, rows = slice(start, start + LANES), slice(window * PAD, (window + 1) * PAD)
        turned = v_ref[rows, lanes].T
        parts = [
            dot(turned[head * HALF : (head + 1) * HALF], p_ref[firsts[b] + head]).astype(bf16) for head in range(heads)
        ]
        if heads == 1:
            parts.append(jnp.zeros_like(parts[0]))
        mix_ref[rows, lanes] = jnp.concatenate(parts, axis=0).T


def attend_backward_unit(
    q_ref, k_ref, v_ref, d_ref, p_ref, dq_ref, dk_ref, dv_ref, table_ref, relt_ref, hott_ref, scr_ref, blocks
):
    places = place_of_lane()
    eighth = jnp.asarray(0.125, bf16)
    firsts, d_attn, d_scores, sums, offsets = [], [], [], [], []
    count = 0
    for window, start, heads in blocks:
        firsts.append(count)
        lanes, rows = slice(start, start + LANES), slice(window * PAD, (window + 1) * PAD)
        d_attn.append(dot(stack_heads(v_ref[rows, lanes], heads), d_ref[rows, lanes], NT))
        count += heads
    for b, (window, start, heads) in enumerate(blocks):
        lanes, rows = slice(start, start + LANES), slice(window * PAD, (window + 1) * PAD)
        soft = p_ref[firsts[b] : firsts[b] + heads].reshape(heads * PAD, PAD)
        dv_ref[rows, lanes] = merge_heads(dot(soft, d_ref[rows, lanes]), heads).astype(bf16)
    for b, (window, start, heads) in enumerate(blocks):
        parts = []
        for head in range(heads):
            soft = p_ref[firsts[b] + head].astype(f32)
            weighted = d_attn[b][head * PAD : (head + 1) * PAD] * soft
            inner = jnp.sum(weighted, axis=0, keepdims=True)
            parts.append((weighted - soft * inner).astype(bf16))
        d_scores.append(parts)
    for b, (window, start, heads) in enumerate(blocks):
        lanes, rows = slice(start, start + LANES), slice(window * PAD, (window + 1) * PAD)
        turned_k = k_ref[rows, lanes].T * eighth
        parts = []
        for head in range(heads):
            left = jnp.concatenate([turned_k[head * HALF : (head + 1) * HALF], hott_ref[...]], axis=0)
            both = dot(left, d_scores[b][head])
            for axis in range(2):
                scr_ref[firsts[b] + head, axis, 16:32, :] = both[HALF + 16 * axis : HALF + 16 * axis + 16]
            parts.append(both[:HALF])
        sums.append(parts)
    for b, (window, start, heads) in enumerate(blocks):
        spread = []
        for head in range(heads):
            for axis in range(2):
                picked = scr_ref[firsts[b] + head, axis, 16:48, :]
                for at in range(WIN - 1):
                    picked = jnp.where(places[axis] == at, scr_ref[firsts[b] + head, axis, 3 + at : 35 + at, :], picked)
                spread.append(picked)
        offsets.append(jnp.concatenate(spread, axis=0).astype(bf16))
    for b, (window, start, heads) in enumerate(blocks):
        lanes, rows = slice(start, start + LANES), slice(window * PAD, (window + 1) * PAD)
        right = dot(jnp.concatenate(d_scores[b] + [offsets[b]], axis=0), q_ref[rows, lanes])
        dk_ref[rows, lanes] = (merge_heads(right[: heads * PAD], heads) * 0.125).astype(bf16)
        table_ref[: heads * HALF] += right[heads * PAD :]
        extra = dot(relt_ref[:, : heads * HALF], offsets[b])
        turned = jnp.concatenate(sums[b] if heads == 2 else sums[b] + [jnp.zeros_like(sums[b][0])], axis=0) + extra
        turned = turned.astype(bf16)
        dq_ref[rows, lanes] = turned.T


class Place:
    def __init__(self, tp, dp):
        self.tp, self.dp = tp, dp
        self.d, self.me = lax.axis_index("dp"), lax.axis_index("tp")
        c, x, y = self.d % 2, (self.d // 2) % 2, (self.d // 4) % 2
        self.c = c
        self.core = self.d + 1 - 2 * c
        peer_x, peer_y = self.d + 2 - 4 * x, self.d + 4 - 8 * y
        self.x, self.y = peer_x, peer_y
        self.first = peer_x * (1 - c) + peer_y * c
        self.second = peer_y * (1 - c) + peer_x * c
        self.bit_one = x * (1 - c) + y * c
        self.bit_two = y * (1 - c) + x * c
        self.extra = []
        for bit in range(3, dp.bit_length() - 1):
            step = 1 << bit
            self.extra.append(self.d + step * (1 - 2 * ((self.d // step) % 2)))

    def flips(self):
        a, b = self.bit_one, self.bit_two
        return [2 * a + b, 2 * (1 - a) + b, 2 * a + 1 - b, 2 * (1 - a) + 1 - b]

    def other(self, step):
        return (self.me + step) % self.tp

    def greet_start(self):
        barrier = pltpu.get_barrier_semaphore()
        for peer in [self.core, self.x, self.y] + self.extra:
            pl.semaphore_signal(barrier, inc=1, device_id=(peer, self.me), device_id_type=MESH)

        def signal(step, carry):
            pl.semaphore_signal(barrier, inc=1, device_id=(self.d, self.other(step)), device_id_type=MESH)
            return carry

        lax.fori_loop(1, self.tp, signal, 0)

    def greet_wait(self):
        pl.semaphore_wait(pltpu.get_barrier_semaphore(), 3 + len(self.extra) + self.tp - 1)


def piece(ref, block, c):
    rows, columns = ref.shape[-2] // 4, ref.shape[-1] // 2
    lead = (slice(None),) * (len(ref.shape) - 2)
    return ref.at[
        lead + (pl.ds(pl.multiple_of(block * rows, rows), rows), pl.ds(pl.multiple_of(c * columns, columns), columns))
    ]


def remote(src, dst, send, recv, device):
    return pltpu.make_async_remote_copy(
        src_ref=src, dst_ref=dst, send_sem=send, recv_sem=recv, device_id=device, device_id_type=MESH
    )


class Spread:
    def __init__(self, place, ref, send, recv, at):
        self.place, self.ref, self.send, self.recv, self.at = place, ref, send, recv, at

    def copy(self, k, arriving):
        place = self.place
        flips = place.flips()
        index = tuple(self.at) + (k,)
        if k == 3:
            columns = self.ref.shape[-1] // 2
            side = 1 - place.c if arriving else place.c
            lead = (slice(None),) * (len(self.ref.shape) - 1)
            view = self.ref.at[lead + (pl.ds(pl.multiple_of(side * columns, columns), columns),)]
            device = place.core
        else:
            device, block, came = (
                (place.first, flips[0], flips[1]) if k == 0 else (place.second, flips[k - 1], flips[k + 1])
            )
            view = piece(self.ref, came if arriving else block, place.c)
        return remote(view, view, self.send.at[index], self.recv.at[index], (device, place.me))

    def start_own(self):
        for k in (0, 1):
            self.copy(k, False).start()

    def after_first(self):
        self.copy(0, True).wait_recv()
        self.copy(2, False).start()

    def after_second(self):
        for k in (1, 2):
            self.copy(k, True).wait_recv()
        self.copy(3, False).start()

    def ready(self):
        self.copy(3, True).wait_recv()

    def sent(self):
        for k in range(4):
            self.copy(k, False).wait_send()


def repeat(count, fn, first=0):
    def step(i, carry):
        fn(i)
        return carry

    lax.fori_loop(first, count, step, 0)


def normal_rows(values):
    centre = jnp.mean(values, axis=-1, keepdims=True)
    centred = values - centre
    scale = lax.rsqrt(jnp.mean(centred * centred, axis=-1, keepdims=True) + 1e-06)
    return centred * scale, scale


def normal_back(gradient, normal, scale, gain):
    e = gradient * gain
    return scale * (
        e - jnp.mean(e, axis=-1, keepdims=True) - normal * jnp.mean(e * normal, axis=-1, keepdims=True)
    )


def block_kernel(tp, dp, names, *refs):
    r = dict(zip(names, refs))
    place = Place(tp, dp)
    me, c, one_bit, two_bit = place.me, place.c, place.bit_one, place.bit_two
    x, cot, fill, vec = r["x"], r["cot"], r["fill"], r["vec"]
    rel, relt = r["rel"], r["relt"]
    a, b, ga = r["a"], r["b"], r["ga"]
    normed, q, k, v, mix = r["normed"], r["q"], r["k"], r["v"], r["mix"]
    middle, total, slide = r["middle"], r["total"], r["slide"]
    normed_two, turned_two, hid, dbs = r["normed_two"], r["turned_two"], r["hid"], r["dbs"]
    early, late, bias = r["early"], r["late"], r["bias"]
    rows_all, width = x.shape
    part = a.shape[2]
    pieces = b.shape[1] // 2
    units = pieces * width
    windows = rows_all // PAD
    half_rows = rows_all // 2
    columns = width // TILE
    tiles = units // TILE
    halves_of_rows = [slice(0, half_rows), slice(half_rows, rows_all)]
    blocks = []
    for window in range(windows // 2):
        for start in range(0, part, LANES):
            blocks.append((window, start, min(2, (part - start) // HALF)))

    weights = [a, b]
    own_copy = [pltpu.make_async_copy(r["own_a"], a.at[me], r["local"].at[0])]
    own_copy.append(pltpu.make_async_copy(r["own_f"], b.at[me, 0:pieces], r["local"].at[1]))
    own_copy.append(pltpu.make_async_copy(r["own_g"], b.at[me, pieces:], r["local"].at[2]))
    own_copy.append(pltpu.make_async_copy(r["x_in"], hid.at[: r["x_in"].shape[0], :width], r["local"].at[3]))
    own_copy.append(pltpu.make_async_copy(r["cot_in"], dbs.at[: r["x_in"].shape[0], :width], r["local"].at[4]))

    def z_copy(w, other, arriving):
        owner = other if arriving else me
        view = piece(weights[w].at[owner], place.flips()[0], c)
        return remote(view, view, r["z_send"].at[w, other], r["z_recv"].at[w, owner], (place.d, other))

    def bias_copy(other, arriving):
        owner = other if arriving else me
        return remote(bias.at[owner], bias.at[owner], r["b_send"].at[other], r["b_recv"].at[owner], (place.d, other))

    def spread(w, s):
        return Spread(place, weights[w].at[s], r["p_send"], r["p_recv"], (w, s))

    def send(w, j):
        z_copy(w, place.other(tp - j), False).start()

    def first(w, j):
        z_copy(w, place.other(j), True).wait_recv()
        spread(w, place.other(j)).start_own()

    def second(w, j):
        spread(w, place.other(j)).after_first()

    def third(w, j):
        spread(w, place.other(j)).after_second()

    def ready(w, j):
        spread(w, place.other(j)).ready()

    def sent(w, j):
        spread(w, place.other(j)).sent()

    def z_sent(w):
        repeat(tp, lambda j: z_copy(w, place.other(j), False).wait_send(), 1)

    grads = [ga, b]
    halves, quarters, eighths, arrived, final = ([r[name + str(w)] for w in range(2)] for name in ("h", "u", "e", "t", "o"))
    outs = [r["out_a"], r["out_b"]]

    def rows_of(block, size):
        return pl.ds(pl.multiple_of(block * size, size), size)

    def lanes_of(w, side):
        count = grads[w].shape[-1] // 2
        return pl.ds(pl.multiple_of(side * count, count), count)

    def core_copy(w, s):
        return remote(
            grads[w].at[s, :, :, lanes_of(w, 1 - c)],
            halves[w].at[s],
            r["core_send"].at[w, s],
            r["core_recv"].at[w, s],
            (place.core, me),
        )

    def quarter_copy(w, s):
        size = quarters[w].shape[2]
        return remote(
            halves[w].at[s, :, rows_of(1 - one_bit, size)],
            quarters[w].at[s],
            r["one_send"].at[w, s],
            r["one_recv"].at[w, s],
            (place.first, me),
        )

    def eighth_copy(w, s):
        size = eighths[w].shape[2]
        return remote(
            quarters[w].at[s, :, rows_of(1 - two_bit, size)],
            eighths[w].at[s],
            r["two_send"].at[w, s],
            r["two_recv"].at[w, s],
            (place.second, me),
        )

    def shard_copy(w, other, arriving):
        owner = other if arriving else me
        return remote(
            eighths[w].at[other], arrived[w].at[owner], r["s_send"].at[w, other], r["s_recv"].at[w, owner], (place.d, other)
        )

    def reduce_one(w, s):
        core_copy(w, s).start()

    def reduce_two(w, s):
        core_copy(w, s).wait_recv()
        size = quarters[w].shape[2]

        def add(block):
            rows = rows_of(block, size)
            halves[w][s, :, rows] += grads[w][s, :, rows, lanes_of(w, c)]

        add(1 - one_bit)
        quarter_copy(w, s).start()
        add(one_bit)

    def reduce_three(w, s):
        size = eighths[w].shape[2]
        quarter_copy(w, s).wait_recv()

        def add(two):
            rows = rows_of(two, size)
            quarters[w][s, :, rows] += halves[w][s, :, rows_of(2 * one_bit + two, size)]

        add(1 - two_bit)
        eighth_copy(w, s).start()
        add(two_bit)

    def reduce_four(w, j):
        s = place.other(j)
        eighth_copy(w, s).wait_recv()
        eighths[w][s] += quarters[w][s, :, rows_of(two_bit, eighths[w].shape[2])]
        if j > 0:
            shard_copy(w, s, False).start()

    def out_spread(w):
        return Spread(place, outs[w], r["q_send"], r["q_recv"], (w,))

    def reduce_five(w):
        repeat(tp, lambda j: shard_copy(w, place.other(j), True).wait_recv(), 1)
        arrived[w][me] = eighths[w][me]
        value = arrived[w][0].astype(f32)
        for s in range(1, tp):
            value += arrived[w][s].astype(f32)
        final[w][...] = value.astype(bf16)
        for i, peer in enumerate(place.extra):
            copy = remote(final[w], r["x" + str(w)].at[i], r["x_send"].at[w, i], r["x_recv"].at[w, i], (peer, me))
            copy.start()
            copy.wait()
            final[w][...] += r["x" + str(w)][i]
        put = pltpu.make_async_copy(final[w], piece(outs[w], place.flips()[0], c), r["put"].at[w])
        put.start()
        put.wait()
        out_spread(w).start_own()

    def reduce_done(w):
        out_spread(w).ready()
        out_spread(w).sent()

        def one(j):
            s = place.other(j)
            core_copy(w, s).wait_send()
            quarter_copy(w, s).wait_send()
            eighth_copy(w, s).wait_send()

        repeat(tp, one)
        repeat(tp, lambda j: shard_copy(w, place.other(j), False).wait_send(), 1)

    levels = [place.core, place.x, place.y] + place.extra
    table = r["table"]
    small = [[r["early"]], [r["late"], r["fold"]]]
    small_in = [[r["early_in"]], [r["late_in"], r["fold_in"]]]
    small_z = [[r["early_z"]], [r["late_z"], r["fold_z"]]]
    small_out = [[r["early_out"]], [r["late_out"], r["fold_out"]]]

    def small_copy(group, i, level):
        at = group + i
        return remote(
            small[group][i],
            small_in[group][i].at[level],
            r["v_send"].at[at, level],
            r["v_recv"].at[at, level],
            (levels[level], me),
        )

    def small_start(group):
        for i in range(len(small[group])):
            small_copy(group, i, 0).start()

    def small_level(group, level):
        for i in range(len(small[group])):
            small_copy(group, i, level).wait()
            small[group][i][...] += small_in[group][i][level]
            if level + 1 < len(levels):
                small_copy(group, i, level + 1).start()

    def small_shard(group, i, other, arriving):
        owner = other if arriving else me
        at = group + i
        return remote(
            small[group][i], small_z[group][i].at[owner], r["vz_send"].at[at, other], r["vz_recv"].at[at, owner], (place.d, other)
        )

    def small_across(group):
        for level in range(2, len(levels)):
            small_level(group, level)
        for i in range(len(small[group])):
            repeat(tp, lambda j: small_shard(group, i, place.other(j), False).start(), 1)

    def small_finish(group):
        for i in range(len(small[group])):
            repeat(tp, lambda j: small_shard(group, i, place.other(j), True).wait_recv(), 1)
            landed = small_z[group][i]
            landed[me] = small[group][i][...]
            value = landed[0]
            for s in range(1, tp):
                value += landed[s]
            small_out[group][i][...] = value

    def small_sent():
        for group in range(2):
            for i in range(len(small[group])):
                repeat(tp, lambda j: small_shard(group, i, place.other(j), False).wait_send(), 1)

    def chunk(i):
        return pl.ds(pl.multiple_of(i * CHUNK, CHUNK), CHUNK)

    chunks = rows_all // CHUNK

    def keep_rows(rows, count):
        keep = (fill[rows] == 0.0).astype(f32)
        return jnp.concatenate([keep] * (count // LANES), axis=1)

    def fill_rows(i):
        row = i * CHUNK + lax.broadcasted_iota(jnp.int32, (CHUNK, LANES), 0)
        window = sum((row >= PAD * at).astype(jnp.int32) for at in range(1, windows))
        inside = row - PAD * window
        down = (inside * 4682) >> 16
        across = inside - WIN * down
        window = me * windows + window
        lower = window // GRID if GRID & (GRID - 1) else window >> (GRID.bit_length() - 1)
        kept = (lower * WIN + down < r["heights"][0]) & ((window - lower * GRID) * WIN + across < r["widths"][0])
        value = jnp.where(kept, 0.0, neg_fill)
        fill[chunk(i)] = jnp.where(inside < SLOTS, value, pad_fill).astype(f32)

    def norm_one(i):
        rows = chunk(i)
        normal, _ = normal_rows(x[rows].astype(f32))
        normed[rows] = (normal * vec[0:1] + vec[2:3]).astype(bf16)

    def project(s):
        for t, target in enumerate((q, k, v)):
            for rows in halves_of_rows:
                value = dot(normed[rows], a[s, t], NT)
                if t != 1:
                    value = value + bias[s, t // 2 : 1 + t // 2, :part]
                target[s, rows, :part] = value.astype(bf16)

    def unit_view(ref, s, at):
        return ref.at[s, pl.ds(pl.multiple_of(at * half_rows, half_rows), half_rows)]

    def p_out(i):
        return pltpu.make_async_copy(r["p"].at[i % 2], r["p_hbm"].at[i], r["p_sem"].at[i % 2])

    def p_in(i):
        return pltpu.make_async_copy(r["p_hbm"].at[i], r["p"].at[i % 2], r["p_sem"].at[i % 2])

    def attend(i, s, at):
        attend_forward_unit(
            unit_view(q, s, at),
            unit_view(k, s, at),
            unit_view(v, s, at),
            unit_view(mix, s, at),
            r["p"].at[i % 2],
            fill.at[pl.ds(pl.multiple_of(at * half_rows, half_rows), half_rows)],
            rel,
            r["hot"],
            r["scr_a"],
            blocks,
        )

    def attend_back(i, s, at):
        views = [unit_view(ref, s, at) for ref in (q, k, v)]
        attend_backward_unit(
            *views, unit_view(mix, s, at), r["p"].at[i % 2], *views, table, relt, r["hott"], r["scr_b"], blocks
        )

    def mix_out(n):
        tile = pl.ds(pl.multiple_of(n * TILE, TILE), TILE)
        for rows in halves_of_rows:
            value = dot(mix[0, rows, :part], a[0, 3, :, tile])
            for s in range(1, tp):
                value = value + dot(mix[s, rows, :part], a[s, 3, :, tile])
            middle[rows, tile] = x[rows, tile].astype(f32) + keep_rows(rows, TILE) * (value + vec[4:5, tile])

    def norm_two(i):
        rows = chunk(i)
        value = middle[rows]
        normal, _ = normal_rows(value)
        normed_two[rows] = (normal * vec[1:2] + vec[3:4]).astype(bf16)
        total[rows] = value + keep_rows(rows, width) * vec[5:6]
        slide[rows] = jnp.zeros_like(value)

    def tile_of(n):
        inner = n if pieces == 1 else n % columns
        block = 0 if pieces == 1 else n // columns
        return pl.ds(pl.multiple_of(n * TILE, TILE), TILE), block, pl.ds(pl.multiple_of(inner * TILE, TILE), TILE)

    def layers(s, j):
        def one(n):
            run("layers", j * tiles + n)
            tile, block, inner = tile_of(n)
            column = None
            for rows in halves_of_rows:
                before = dot(normed_two[rows], b[s, block, :, inner]) + bias[s, pl.ds(2 + block, 1), inner]
                keep = keep_rows(rows, TILE)
                phi = 0.5 * (1.0 + lax.erf(before * root_half))
                hid[rows, tile] = (before * phi * keep).astype(bf16)
                slope = phi + before * (jnp.exp(-0.5 * before * before) * bell)
                down = (slope * (dot(cot[rows], b[s, pieces + block, inner, :], NT) * keep)).astype(bf16)
                dbs[rows, tile] = down
                part_sum = jnp.sum(down.astype(f32), axis=0, keepdims=True)
                column = part_sum if column is None else column + part_sum
            early[pl.ds(4 + s * pieces + block, 1), inner] = column

        repeat(tiles, one)

    def layers_add(s, j):
        def one(n):
            run("add", j * columns + n)
            tile = pl.ds(pl.multiple_of(n * TILE, TILE), TILE)
            for rows in halves_of_rows:
                for i in range(pieces):
                    part_of = slice(i * width, (i + 1) * width)
                    total[rows, tile] += dot(hid[rows, part_of], b[s, pieces + i, :, tile])
                    slide[rows, tile] += dot(dbs[rows, part_of], b[s, i, tile, :], NT)

        repeat(columns, one)

    def layers_grad(s, j):
        def one(n):
            run("grad", j * tiles + n)
            tile, block, inner = tile_of(n)
            b[s, pieces + block, inner, :] = dot(hid[:, tile], cot[...], TN).astype(bf16)
            b[s, block, :, inner] = dot(turned_two[...], dbs[:, tile]).astype(bf16)

        repeat(tiles, one)

    def middle_back(i):
        rows = chunk(i)
        hid[rows, :width] = total[rows].astype(bf16)
        keep = keep_rows(rows, width)
        gradient = slide[rows]
        normal, scale = normal_rows(middle[rows])
        outer = cot[rows].astype(f32)
        down = outer + normal_back(gradient, normal, scale, vec[1:2])
        slide[rows] = down
        masked = down * keep
        dbs[rows, :width] = masked.astype(bf16)
        total[rows] = jnp.zeros_like(down)
        for at, value in enumerate((gradient * normal, gradient, masked, outer * keep)):
            early[at : at + 1] = early[at : at + 1] + jnp.sum(value, axis=0, keepdims=True)

    def mix_back(s):
        ga[s, 3] = dot(mix[s, :, :part], dbs[:, :width], TN).astype(bf16)
        for rows in halves_of_rows:
            mix[s, rows, :part] = dot(dbs[rows, :width], a[s, 3], NT).astype(bf16)

    def project_back(s):
        for t, source in enumerate((q, k, v)):
            ga[s, t] = dot(source[s, :, :part], normed[...], TN).astype(bf16)
        for i, source in ((0, q), (1, v)):
            value = jnp.sum(source[s, :, :part].astype(f32), axis=0, keepdims=True)
            first_lane = i * (width // 2)
            late[pl.ds(2 + s, 1), first_lane : first_lane + part] = value

        def one(n):
            tile = pl.ds(pl.multiple_of(n * TILE, TILE), TILE)
            for rows in halves_of_rows:
                total[rows, tile] += (
                    dot(q[s, rows, :part], a[s, 0, :, tile])
                    + dot(k[s, rows, :part], a[s, 1, :, tile])
                    + dot(v[s, rows, :part], a[s, 2, :, tile])
                )

        repeat(columns, one)

    def input_back(i):
        rows = chunk(i)
        gradient = total[rows]
        normal, scale = normal_rows(x[rows].astype(f32))
        middle[rows] = slide[rows] + normal_back(gradient, normal, scale, vec[0:1])
        late[0:1] = late[0:1] + jnp.sum(gradient * normal, axis=0, keepdims=True)
        late[1:2] = late[1:2] + jnp.sum(gradient, axis=0, keepdims=True)

    plan = make_plan(tp, tiles, columns)

    def run(name, index=0):
        for at, steps in sorted(plan.get(name, {}).items()):

            @pl.when(index == at)
            def _(steps=steps):
                for fn, *args in steps:
                    do[fn](*args)

    def bias_ready():
        repeat(tp, lambda j: bias_copy(place.other(j), True).wait_recv(), 1)

    do = dict(
        send=send,
        first=first,
        second=second,
        third=third,
        ready=ready,
        sent=sent,
        bias_ready=bias_ready,
        one=lambda w, j: reduce_one(w, place.other(j)),
        two=lambda w, j: reduce_two(w, place.other(j)),
        three=lambda w, j: reduce_three(w, place.other(j)),
        four=reduce_four,
        z_sent=z_sent,
        five=reduce_five,
        after_first=lambda w: out_spread(w).after_first(),
        after_second=lambda w: out_spread(w).after_second(),
        s0=small_start,
        s1=lambda group: small_level(group, 0),
        s2=lambda group: small_level(group, 1),
        s3=small_across,
        s4=small_finish,
        done=reduce_done,
    )

    place.greet_start()
    for copy in own_copy:
        copy.start()
    bias[me] = vec[8:16]
    for copy in own_copy:
        copy.wait()
    place.greet_wait()
    run("start")
    repeat(tp, lambda j: bias_copy(place.other(tp - j), False).start(), 1)
    slots = r["x_in"].shape[0] // windows
    for window in range(windows):
        for staged, target in ((hid, x), (dbs, cot)):
            target[window * PAD : window * PAD + slots] = staged[window * slots : (window + 1) * slots, :width]
            target[window * PAD + slots : (window + 1) * PAD] = jnp.zeros((PAD - slots, width), bf16)
    repeat(chunks, norm_one)
    repeat(chunks, fill_rows)
    picked = dot(r["pick"][...], r["offsets"][...])
    lane = lax.broadcasted_iota(jnp.int32, picked.shape, 1)
    head = lax.broadcasted_iota(jnp.int32, picked.shape, 0)
    picked = jnp.where((lane < HALF) == (head < HALF), picked, 0.0)
    rel[...] = picked.astype(bf16)
    relt[...] = (picked * 0.125).T.astype(bf16)
    lead = part - part % LANES
    if lead < part:
        for ref in (q, k, v, mix):
            for s in range(tp):
                ref[s, :, lead:] = jnp.zeros((rows_all, LANES), bf16)
    for ref in (early, late, table, r["scr_b"]):
        ref[...] = jnp.zeros_like(ref)

    def forward_unit(i):
        j, at = i // 2, i % 2
        s = place.other(j)

        @pl.when(at == 0)
        def _():
            run("project", j)
            project(s)

        run("unit", i)

        @pl.when(i >= 2)
        def _():
            p_out(i - 2).wait()

        attend(i, s, at)
        p_out(i).start()

    unit_count = 2 * tp
    repeat(unit_count, forward_unit)
    run("mid")
    p_out(unit_count - 2).wait()
    p_out(unit_count - 1).wait()
    repeat(columns, mix_out)
    run("mid1")
    repeat(chunks, norm_two)
    turned_two[...] = normed_two[...].T

    def layer_step(j):
        s = place.other(j)
        layers(s, j)
        layers_add(s, j)
        layers_grad(s, j)
        run("layer3", j)

    repeat(tp, layer_step)

    run("down0")
    repeat(chunks, middle_back)
    for window in range(windows):
        normed_two[window * slots : (window + 1) * slots] = hid[window * PAD : window * PAD + slots, :width]
    put_out = pltpu.make_async_copy(normed_two.at[: windows * slots], r["out"], r["local"].at[1])
    put_out.start()
    run("down1")
    p_in(0).start()
    repeat(tp, lambda j: mix_back(place.other(j)))
    run("down2")

    def backward_unit(i):
        j, at = i // 2, i % 2
        s = place.other(j)
        run("back", i)

        @pl.when(i + 1 < unit_count)
        def _():
            p_in(i + 1).start()

        p_in(i).wait()
        attend_back(i, s, at)

        @pl.when(at == 1)
        def _():
            run("turn", j)
            project_back(s)
            run("shard", j)

    repeat(unit_count, backward_unit)
    for at in range(4):
        run("end" + str(at))
        repeat(chunks * (at + 1) // 4, input_back, chunks * at // 4)
    for window in range(windows):
        total[window * slots : (window + 1) * slots] = middle[window * PAD : window * PAD + slots]
    put_in = pltpu.make_async_copy(total.at[: windows * slots], r["grad_x"], r["local"].at[2])
    put_in.start()
    r["fold"][:, :HALF] = table[:32, :HALF] + table[HALF : HALF + 32, HALF:]
    r["fold"][:, HALF:] = table[32:HALF, :HALF] + table[HALF + 32 :, HALF:]
    for at in range(4, ENDS):
        run("end" + str(at))
    for j in range(1, tp):
        sent(0, j)
    z_sent(0)
    small_sent()
    repeat(tp, lambda j: bias_copy(place.other(tp - j), False).wait_send(), 1)
    put_out.wait()
    put_in.wait()


def make_plan(tp, tiles, columns):
    plan = {}
    if PLACES and (tp, tiles, columns) == (4, 3, 3):
        for place, index, *steps in PLACES:
            plan.setdefault(place, {})[index] = steps
        return plan

    def at(place, index, *step):
        if place in ("layer0", "layer1", "layer2"):
            place, count = dict(layer0=("layers", tiles), layer1=("add", columns), layer2=("grad", tiles))[place]
            index *= count
        plan.setdefault(place, {}).setdefault(index, []).append(step)

    others = list(range(1, tp))
    arrivals = [(w, j) for w in (0, 1) for j in others]
    order = [("unit", 1)]
    for j in others:
        order += [("project", j), ("unit", 2 * j), ("unit", 2 * j + 1)]
    order.append(("mid", 0))
    order += [("layer" + str(stage), j) for j in range(tp) for stage in range(4)]
    slots = len(arrivals) + 2
    own_end = order.index(("layer3", 0))
    marks = [s * own_end // (slots - 1) for s in range(slots)]
    need = {0: "project", 1: "layer0"}
    limit = len(order) - 1
    for slot in reversed(range(slots)):
        if slot >= 2:
            w, j = arrivals[slot - 2]
            limit = min(limit, order.index((need[w], j)))
        limit = min(limit, marks[slot])
        marks = marks[:slot] + [limit] + marks[slot + 1 :]
    for ahead in range(min(2, len(arrivals))):
        at("start", 0, "send", *arrivals[ahead])
    for slot in range(slots):
        for name, behind in (("third", 2), ("second", 1), ("first", 0)):
            if 0 <= slot - behind < len(arrivals):
                at(*order[marks[slot]], name, *arrivals[slot - behind])
        if slot + 2 < len(arrivals):
            at(*order[marks[slot]], "send", *arrivals[slot + 2])
    if tp > 1:
        at("project", 1, "bias_ready")
        at("layer2", 0, "z_sent", 1)
    for j in others:
        at("project", j, "ready", 0, j)
        at("layer0", j, "ready", 1, j)
        at("layer2", j, "sent", 1, j)

    last = tp - 1
    for j in range(tp):
        at("layer3", j, "one", 1, j)
    for j in range(tp):
        at(*(("layer1", j + 1) if j < last else ("down1", 0)), "two", 1, j)
    for j in range(tp):
        at(*(("layer1", j + 2) if j + 2 <= last else ("down1", 0) if j < last else ("shard", 0)), "three", 1, j)
    for j in range(tp):
        where = ("layer1", j + 3) if j + 3 <= last else ("down1", 0) if j + 2 <= last else ("back", 1) if j < last else ("turn", min(1, last))
        at(*where, "four", 1, j)
    late = lambda n: ("shard", n) if n <= last else ("end0", 0)
    at(*late(1), "five", 1)
    at(*late(2), "after_first", 1)
    at(*late(3), "after_second", 1)

    for j in range(tp):
        at("shard", j, "one", 0, j)
    for j in range(tp):
        at(*(("back", 2 * j + 3) if j < last else ("end4", 0)), "two", 0, j)
    for j in range(tp):
        at(*(("shard", j + 1) if j < last else ("end6", 0)), "three", 0, j)
    for j in range(tp):
        at(*(("back", 2 * j + 5) if j + 2 <= last else ("end0", 0) if j < last else ("end7", 0)), "four", 0, j)
    for group, places in enumerate((("down2", "end0", "end1", "end2", "end3"), ("end4", "end5", "end6", "end7", "end8"))):
        for step, place in enumerate(places):
            at(place, 0, "s" + str(step), group)
    at("end9", 0, "five", 0)
    at("end9", 0, "after_first", 0)
    at("end10", 0, "after_second", 0)
    at("end11", 0, "done", 1)
    at("end11", 0, "done", 0)
    return plan


def whole_block(tp, dp, x, cot, heights, widths, vec, own_a, own_f, own_g, offsets):
    width = x.shape[1]
    windows = x.shape[0] // SLOTS
    rows = windows * PAD
    part = own_a.shape[1]
    pieces = own_f.shape[0]
    units = pieces * width
    heads = (windows // 2) * (part // HEAD_DIM)
    wide = -(-part // LANES) * LANES
    unit_count = 2 * tp
    hot, hott, pick = window_constants()
    scalar = pl.BlockSpec(memory_space=pltpu.SMEM)
    any_space = pl.BlockSpec(memory_space=pl.ANY)
    vmem = pl.BlockSpec(memory_space=pltpu.VMEM)
    dma = pltpu.SemaphoreType.DMA
    inputs = [
        ("x_in", x, any_space),
        ("cot_in", cot, any_space),
        ("heights", heights, scalar),
        ("widths", widths, scalar),
        ("vec", vec, vmem),
        ("own_a", own_a, any_space),
        ("own_f", own_f, any_space),
        ("own_g", own_g, any_space),
        ("offsets", offsets, vmem),
        ("hot", hot, vmem),
        ("hott", hott, vmem),
        ("pick", pick, vmem),
    ]
    shape = jax.ShapeDtypeStruct
    outputs = [
        ("out", shape(x.shape, bf16), any_space),
        ("grad_x", shape(x.shape, f32), any_space),
        ("out_a", shape(own_a.shape, bf16), any_space),
        ("out_b", shape((2 * pieces, width, width), bf16), any_space),
        ("early_out", shape((8, width), f32), vmem),
        ("late_out", shape((8, width), f32), vmem),
        ("fold_out", shape((32, LANES), f32), vmem),
        ("p_hbm", shape((unit_count, heads, PAD, PAD), bf16), any_space),
    ]
    buffer = lambda dims, kind: pltpu.VMEM(tuple(dims), kind)
    scratch = [
        ("a", buffer((tp,) + own_a.shape, bf16)),
        ("b", buffer((tp, 2 * pieces, width, width), bf16)),
        ("ga", buffer((tp,) + own_a.shape, bf16)),
        ("bias", buffer((tp, 8, width), f32)),
        ("x", buffer((rows, width), bf16)),
        ("cot", buffer((rows, width), bf16)),
        ("fill", buffer((rows, LANES), f32)),
        ("rel", buffer((LANES, LANES), bf16)),
        ("relt", buffer((LANES, LANES), bf16)),
        ("normed", buffer((rows, width), bf16)),
    ]
    scratch += [(name, buffer((tp, rows, wide), bf16)) for name in ("q", "k", "v", "mix")]
    scratch += [("p", buffer((2, heads, PAD, PAD), bf16))]
    scratch += [(name, buffer((rows, width), f32)) for name in ("middle", "total", "slide")]
    scratch += [("normed_two", buffer((rows, width), bf16)), ("turned_two", buffer((width, rows), bf16))]
    scratch += [(name, buffer((rows, units), bf16)) for name in ("hid", "dbs")]
    scratch += [
        ("early", buffer((8, width), f32)),
        ("late", buffer((8, width), f32)),
        ("table", buffer((LANES, LANES), f32)),
        ("fold", buffer((32, LANES), f32)),
        ("scr_a", buffer((heads, HALF, PAD), f32)),
        ("scr_b", buffer((heads, 2, 48, PAD), f32)),
    ]
    levels = dp.bit_length() - 1
    more = levels - 3
    for w, own in enumerate((own_a.shape, (2 * pieces, width, width))):
        n, count, lanes = own[0], own[1], own[2] // 2
        scratch += [
            ("h" + str(w), buffer((tp, n, count, lanes), bf16)),
            ("u" + str(w), buffer((tp, n, count // 2, lanes), bf16)),
            ("e" + str(w), buffer((tp, n, count // 4, lanes), bf16)),
            ("t" + str(w), buffer((tp, n, count // 4, lanes), bf16)),
            ("o" + str(w), buffer((n, count // 4, lanes), bf16)),
        ]
        if more:
            scratch += [("x" + str(w), buffer((more, n, count // 4, lanes), bf16))]
    for name, dims in (("early", (8, width)), ("late", (8, width)), ("fold", (32, LANES))):
        scratch += [(name + "_in", buffer((levels,) + dims, f32)), (name + "_z", buffer((tp,) + dims, f32))]
    semaphores = dict(local=(5,), p_sem=(2,), put=(2,))
    for name, dims in dict(
        z=(2, tp), p=(2, tp, 4), b=(tp,), core=(2, tp), one=(2, tp), two=(2, tp), s=(2, tp), q=(2, 4), x=(2, max(more, 1)), v=(3, levels), vz=(3, tp)
    ).items():
        semaphores[name + "_send"] = semaphores[name + "_recv"] = dims
    scratch += [(name, dma(dims)) for name, dims in semaphores.items()]
    names = [entry[0] for entry in inputs + outputs + scratch]
    return pl.pallas_call(
        lambda *refs: block_kernel(tp, dp, names, *refs),
        in_specs=[entry[2] for entry in inputs],
        out_specs=[entry[2] for entry in outputs],
        out_shape=[entry[1] for entry in outputs],
        scratch_shapes=[entry[1] for entry in scratch],
        compiler_params=pltpu.CompilerParams(collective_id=1, has_side_effects=True, vmem_limit_bytes=VMEM_LIMIT),
    )(*[entry[1] for entry in inputs])


def body(
    tokens,
    heights,
    widths,
    norm_gain,
    norm_bias,
    w_qkv,
    b_qv,
    rel_pos,
    w_proj,
    b_proj,
    w_fc1,
    b_fc1,
    w_fc2,
    b_fc2,
    cotangent,
):
    tp, dp = lax.axis_size("tp"), lax.axis_size("dp")
    width = tokens.shape[1]
    part, units = w_qkv.shape[2], w_fc1.shape[1]
    blocks = units // width
    pad = lambda values, rows, lanes=0: jnp.pad(values, ((0, rows), (0, lanes)))
    vec = [norm_gain, norm_bias, b_proj[None], pad(b_fc2[None], 2), pad(b_qv, 0, width - part)]
    vec = jnp.concatenate(vec + [pad(b_fc1.reshape(blocks, width), 6 - blocks)]).astype(f32)
    offsets = jnp.pad(rel_pos, ((0, 0), (0, 32 - rel_pos.shape[1]), (0, 0))).reshape(HALF, HEAD_DIM)
    offsets = jnp.concatenate([offsets, offsets], axis=1)
    turned = jnp.concatenate([w_qkv.transpose(0, 2, 1), w_proj[None]], axis=0)
    first = w_fc1[None] if blocks == 1 else w_fc1.reshape(width, blocks, width).transpose(1, 0, 2)
    out, grad_x, out_a, out_b, early, late, fold, _ = whole_block(
        tp, dp, tokens, cotangent, heights, widths, vec, turned, first, w_fc2.reshape(blocks, width, width), offsets
    )
    me = lax.axis_index("tp")
    count = 2 * WIN - 1
    grad_rel = jnp.stack([fold[:count, :HALF], fold[:count, HALF:]])[:, ::-1, :]
    mine = lax.dynamic_slice_in_dim(late, 2 + me, 1, 0)
    return (
        out,
        grad_x,
        jnp.stack([late[0], early[0]]),
        jnp.stack([late[1], early[1]]),
        out_a[:3].transpose(0, 2, 1).astype(f32),
        jnp.concatenate([mine[:, :part], mine[:, width // 2 : width // 2 + part]]),
        grad_rel,
        out_a[3].astype(f32),
        early[2],
        out_b[:blocks].transpose(1, 0, 2).reshape(width, units).astype(f32),
        lax.dynamic_slice_in_dim(early, 4 + me * blocks, blocks, 0).reshape(-1),
        out_b[blocks:].reshape(units, width).astype(f32),
        early[3],
    )


def solution(mesh):
    rows = P(("dp", "tp"), None)
    return jax.shard_map(
        body,
        mesh=mesh,
        in_specs=(
            rows,
            P("dp"),
            P("dp"),
            P(),
            P(),
            P(None, None, "tp"),
            P(None, "tp"),
            P(),
            P("tp", None),
            P(),
            P(None, "tp"),
            P("tp"),
            P("tp", None),
            P(),
            rows,
        ),
        out_specs=(
            rows,
            rows,
            P(),
            P(),
            P(None, None, "tp"),
            P(None, "tp"),
            P(),
            P("tp", None),
            P(),
            P(None, "tp"),
            P("tp"),
            P("tp", None),
            P(),
        ),
        check_vma=False,
    )
```

```python
import jax
import jax.numpy as jnp
import ml_dtypes
import numpy as np
from jax import lax
from jax.experimental import pallas as pl
from jax.experimental.pallas import tpu as pltpu
from jax.sharding import PartitionSpec as P

HEAD_DIM = 64
WIN = 14
GRID = 4
SLOTS = WIN * WIN
PAD = 208
LANES = 128
HALF = 64
CHUNK = 64
ENDS = 20
PLACES = [
    ("start", 0, ("send", 0, 1)),
    ("warm", 0, ("send", 0, 2), ("first", 0, 1), ("send", 0, 3), ("second", 0, 1)),
    ("warm", 1, ("send", 1, 1), ("first", 0, 2)),
    ("project", 0, ("first", 0, 3)),
    ("unit", 0, ("send", 1, 3), ("third", 0, 1)),
    ("project", 1, ("bias_ready",), ("ready", 0, 1), ("second", 0, 2)),
    ("unit", 3, ("second", 0, 3), ("third", 0, 2)),
    ("project", 2, ("first", 1, 1), ("send", 1, 2), ("ready", 0, 2)),
    ("unit", 4, ("third", 0, 3)),
    ("project", 3, ("first", 1, 3), ("ready", 0, 3)),
    ("mid1", 0, ("second", 1, 1)),
    ("layers", 0, ("first", 1, 2)),
    ("add", 0, ("third", 1, 1)),
    ("grad", 0, ("z_sent", 1)),
    ("layer3", 0, ("second", 1, 2), ("one", 1, 0)),
    ("layers", 3, ("ready", 1, 1)),
    ("add", 4, ("second", 1, 3)),
    ("grad", 3, ("third", 1, 2), ("two", 1, 0), ("sent", 1, 1)),
    ("layer3", 1, ("ready", 1, 2)),
    ("layers", 6, ("one", 1, 1)),
    ("layers", 8, ("third", 1, 3)),
    ("add", 7, ("two", 1, 1)),
    ("grad", 6, ("sent", 1, 2)),
    ("layer3", 2, ("one", 1, 2), ("ready", 1, 3)),
    ("add", 10, ("two", 1, 2), ("three", 1, 1)),
    ("grad", 9, ("sent", 1, 3)),
    ("layer3", 3, ("one", 1, 3)),
    ("down0", 1, ("two", 1, 3)),
    ("down2", 0, ("three", 1, 2)),
    ("back", 0, ("s0", 0), ("four", 1, 1)),
    ("turn", 0, ("three", 1, 3)),
    ("shard", 0, ("one", 0, 0)),
    ("after", 0, ("four", 1, 2), ("three", 1, 0)),
    ("back", 3, ("s1", 0), ("two", 0, 0)),
    ("back", 4, ("four", 1, 3), ("one", 0, 1)),
    ("turn", 2, ("s2", 0), ("two", 0, 1)),
    ("shard", 2, ("one", 0, 2)),
    ("after", 2, ("four", 1, 0)),
    ("back", 6, ("two", 0, 2)),
    ("turn", 3, ("three", 0, 1), ("three", 0, 0)),
    ("shard", 3, ("one", 0, 3), ("three", 0, 2)),
    ("end0", 0, ("s3", 0), ("two", 0, 3), ("five", 1), ("four", 0, 1)),
    ("end1", 0, ("four", 0, 0)),
    ("end2", 0, ("s4", 0), ("four", 0, 2)),
    ("end4", 0, ("s0", 1), ("s1", 1), ("three", 0, 3), ("s2", 1), ("after_first", 1), ("s3", 1), ("four", 0, 3), ("five", 0), ("after_second", 1), ("s4", 1), ("done", 1), ("after_first", 0), ("after_second", 0), ("done", 0)),
]
TILE = 256

bf16 = jnp.bfloat16
f32 = jnp.float32
neg_fill = -30000.0
pad_fill = -1e30
root_half = 0.7071067811865476
bell = 0.3989422804014327
VMEM_LIMIT = 64 << 20
MESH = pl.DeviceIdType.MESH


def dot(a, b, dims=((1,), (0,))):
    return lax.dot_general(a, b, (dims, ((), ())), preferred_element_type=f32)


NT = ((1,), (1,))
TN = ((0,), (0,))


def window_constants():
    slot = np.arange(PAD)[:, None]
    lane = np.arange(HALF)[None, :]
    place = np.where(lane % 32 < 16, slot // WIN, slot % WIN)
    hot = ((slot < SLOTS) & (lane % 16 == place)).astype(np.float32)
    zero = np.zeros_like(hot)
    both = np.concatenate([np.concatenate([hot, zero], 1), np.concatenate([zero, hot], 1)], 0)
    pick = np.zeros((LANES, HALF), np.float32)
    for offset in range(2 * WIN - 1):
        for head in range(2):
            for axis in range(2):
                pick[HALF * head + 32 * axis + offset, 32 * axis + 2 * WIN - 2 - offset] = 8.0
    narrow = lambda values: values.astype(ml_dtypes.bfloat16)
    return narrow(both), narrow(hot[:, :32].T.copy()), narrow(pick)


def stack_heads(pair, heads):
    if heads == 1:
        return pair
    lane = lax.broadcasted_iota(jnp.int32, pair.shape, 1)
    zero = jnp.zeros_like(pair)
    return jnp.concatenate([jnp.where(lane < HALF, pair, zero), jnp.where(lane < HALF, zero, pair)], axis=0)


def merge_heads(stacked, heads):
    if heads == 1:
        return stacked
    top, bottom = stacked[:PAD], stacked[PAD:]
    lane = lax.broadcasted_iota(jnp.int32, top.shape, 1)
    return jnp.where(lane < HALF, top, bottom)


def place_of_lane():
    lane = lax.broadcasted_iota(jnp.int32, (1, PAD), 1)
    row = lax.div(lane, WIN)
    return row, lane - row * WIN


def attend_forward_unit(q_ref, k_ref, v_ref, mix_ref, p_ref, fill_ref, rel_ref, hot_ref, scr_ref, blocks):
    places = place_of_lane()
    eighth = jnp.asarray(0.125, bf16)
    firsts, scores, biases = [], [], []
    count = 0
    for window, start, heads in blocks:
        firsts.append(count)
        lanes, rows = slice(start, start + LANES), slice(window * PAD, (window + 1) * PAD)
        left = jnp.concatenate([rel_ref[: heads * HALF], stack_heads(k_ref[rows, lanes], heads)], axis=0)
        both = dot(left, q_ref[rows, lanes] * eighth, NT)
        for head in range(heads):
            scr_ref[count + head] = both[head * HALF : (head + 1) * HALF]
        scores.append(both[heads * HALF :])
        count += heads
    for b, (window, start, heads) in enumerate(blocks):
        parts = []
        for head in range(heads):
            along = []
            for base, place in ((0, places[0]), (32, places[1])):
                picked = scr_ref[firsts[b] + head, base : base + 16, :]
                for at in range(WIN - 1):
                    first = base + WIN - 1 - at
                    picked = jnp.where(place == at, scr_ref[firsts[b] + head, first : first + 16, :], picked)
                along.append(picked)
            bias = jnp.concatenate(along, axis=0)
            high = bias.astype(bf16)
            parts += [high, (bias - high.astype(f32)).astype(bf16)]
        biases.append(jnp.concatenate(parts, axis=0))
    for b, (window, start, heads) in enumerate(blocks):
        scores[b] = scores[b] + dot(hot_ref[: heads * PAD, : heads * HALF], biases[b])
    for b, (window, start, heads) in enumerate(blocks):
        fill = fill_ref[window * PAD : (window + 1) * PAD]
        fill = jnp.concatenate([fill, fill[:, : PAD - LANES]], axis=1)
        for head in range(heads):
            one = scores[b][head * PAD : (head + 1) * PAD]
            one = jnp.where(fill == 0.0, one, fill)
            weights = jnp.exp(one - jnp.max(one, axis=0, keepdims=True))
            total = jnp.sum(weights, axis=0, keepdims=True)
            p_ref[firsts[b] + head] = (weights * (1.0 / total)).astype(bf16)
    for b, (window, start, heads) in enumerate(blocks):
        lanes, rows = slice(start, start + LANES), slice(window * PAD, (window + 1) * PAD)
        turned = v_ref[rows, lanes].T
        parts = [
            dot(turned[head * HALF : (head + 1) * HALF], p_ref[firsts[b] + head]).astype(bf16) for head in range(heads)
        ]
        if heads == 1:
            parts.append(jnp.zeros_like(parts[0]))
        mix_ref[rows, lanes] = jnp.concatenate(parts, axis=0).T


def attend_backward_unit(
    q_ref, k_ref, v_ref, d_ref, p_ref, dq_ref, dk_ref, dv_ref, table_ref, relt_ref, hott_ref, scr_ref, blocks
):
    places = place_of_lane()
    eighth = jnp.asarray(0.125, bf16)
    firsts, d_attn, d_scores, sums, offsets = [], [], [], [], []
    count = 0
    for window, start, heads in blocks:
        firsts.append(count)
        lanes, rows = slice(start, start + LANES), slice(window * PAD, (window + 1) * PAD)
        d_attn.append(dot(stack_heads(v_ref[rows, lanes], heads), d_ref[rows, lanes], NT))
        count += heads
    for b, (window, start, heads) in enumerate(blocks):
        lanes, rows = slice(start, start + LANES), slice(window * PAD, (window + 1) * PAD)
        soft = p_ref[firsts[b] : firsts[b] + heads].reshape(heads * PAD, PAD)
        dv_ref[rows, lanes] = merge_heads(dot(soft, d_ref[rows, lanes]), heads).astype(bf16)
    for b, (window, start, heads) in enumerate(blocks):
        parts = []
        for head in range(heads):
            soft = p_ref[firsts[b] + head].astype(f32)
            weighted = d_attn[b][head * PAD : (head + 1) * PAD] * soft
            inner = jnp.sum(weighted, axis=0, keepdims=True)
            parts.append((weighted - soft * inner).astype(bf16))
        d_scores.append(parts)
    for b, (window, start, heads) in enumerate(blocks):
        lanes, rows = slice(start, start + LANES), slice(window * PAD, (window + 1) * PAD)
        turned_k = k_ref[rows, lanes].T * eighth
        parts = []
        for head in range(heads):
            left = jnp.concatenate([turned_k[head * HALF : (head + 1) * HALF], hott_ref[...]], axis=0)
            both = dot(left, d_scores[b][head])
            for axis in range(2):
                scr_ref[firsts[b] + head, axis, 16:32, :] = both[HALF + 16 * axis : HALF + 16 * axis + 16]
            parts.append(both[:HALF])
        sums.append(parts)
    for b, (window, start, heads) in enumerate(blocks):
        spread = []
        for head in range(heads):
            for axis in range(2):
                picked = scr_ref[firsts[b] + head, axis, 16:48, :]
                for at in range(WIN - 1):
                    picked = jnp.where(places[axis] == at, scr_ref[firsts[b] + head, axis, 3 + at : 35 + at, :], picked)
                spread.append(picked)
        offsets.append(jnp.concatenate(spread, axis=0).astype(bf16))
    for b, (window, start, heads) in enumerate(blocks):
        lanes, rows = slice(start, start + LANES), slice(window * PAD, (window + 1) * PAD)
        right = dot(jnp.concatenate(d_scores[b] + [offsets[b]], axis=0), q_ref[rows, lanes])
        dk_ref[rows, lanes] = (merge_heads(right[: heads * PAD], heads) * 0.125).astype(bf16)
        table_ref[: heads * HALF] += right[heads * PAD :]
        extra = dot(relt_ref[:, : heads * HALF], offsets[b])
        turned = jnp.concatenate(sums[b] if heads == 2 else sums[b] + [jnp.zeros_like(sums[b][0])], axis=0) + extra
        turned = turned.astype(bf16)
        dq_ref[rows, lanes] = turned.T


class Place:
    def __init__(self, tp, dp):
        self.tp, self.dp = tp, dp
        self.d, self.me = lax.axis_index("dp"), lax.axis_index("tp")
        c, x, y = self.d % 2, (self.d // 2) % 2, (self.d // 4) % 2
        self.c = c
        self.core = self.d + 1 - 2 * c
        peer_x, peer_y = self.d + 2 - 4 * x, self.d + 4 - 8 * y
        self.x, self.y = peer_x, peer_y
        self.first = peer_x * (1 - c) + peer_y * c
        self.second = peer_y * (1 - c) + peer_x * c
        self.bit_one = x * (1 - c) + y * c
        self.bit_two = y * (1 - c) + x * c
        self.extra = []
        for bit in range(3, dp.bit_length() - 1):
            step = 1 << bit
            self.extra.append(self.d + step * (1 - 2 * ((self.d // step) % 2)))

    def flips(self):
        a, b = self.bit_one, self.bit_two
        return [2 * a + b, 2 * (1 - a) + b, 2 * a + 1 - b, 2 * (1 - a) + 1 - b]

    def other(self, step):
        return (self.me + step) % self.tp

    def greet_start(self):
        barrier = pltpu.get_barrier_semaphore()
        for peer in [self.core, self.x, self.y] + self.extra:
            pl.semaphore_signal(barrier, inc=1, device_id=(peer, self.me), device_id_type=MESH)

        def signal(step, carry):
            pl.semaphore_signal(barrier, inc=1, device_id=(self.d, self.other(step)), device_id_type=MESH)
            return carry

        lax.fori_loop(1, self.tp, signal, 0)

    def greet_wait(self):
        pl.semaphore_wait(pltpu.get_barrier_semaphore(), 3 + len(self.extra) + self.tp - 1)


def piece(ref, block, c):
    rows, columns = ref.shape[-2] // 4, ref.shape[-1] // 2
    lead = (slice(None),) * (len(ref.shape) - 2)
    return ref.at[
        lead + (pl.ds(pl.multiple_of(block * rows, rows), rows), pl.ds(pl.multiple_of(c * columns, columns), columns))
    ]


def remote(src, dst, send, recv, device):
    return pltpu.make_async_remote_copy(
        src_ref=src, dst_ref=dst, send_sem=send, recv_sem=recv, device_id=device, device_id_type=MESH
    )


class Spread:
    def __init__(self, place, ref, send, recv, at):
        self.place, self.ref, self.send, self.recv, self.at = place, ref, send, recv, at

    def copy(self, k, arriving):
        place = self.place
        flips = place.flips()
        index = tuple(self.at) + (k,)
        if k == 3:
            columns = self.ref.shape[-1] // 2
            side = 1 - place.c if arriving else place.c
            lead = (slice(None),) * (len(self.ref.shape) - 1)
            view = self.ref.at[lead + (pl.ds(pl.multiple_of(side * columns, columns), columns),)]
            device = place.core
        else:
            device, block, came = (
                (place.first, flips[0], flips[1]) if k == 0 else (place.second, flips[k - 1], flips[k + 1])
            )
            view = piece(self.ref, came if arriving else block, place.c)
        return remote(view, view, self.send.at[index], self.recv.at[index], (device, place.me))

    def start_own(self):
        for k in (0, 1):
            self.copy(k, False).start()

    def after_first(self):
        self.copy(0, True).wait_recv()
        self.copy(2, False).start()

    def after_second(self):
        for k in (1, 2):
            self.copy(k, True).wait_recv()
        self.copy(3, False).start()

    def ready(self):
        self.copy(3, True).wait_recv()

    def sent(self):
        for k in range(4):
            self.copy(k, False).wait_send()


def repeat(count, fn, first=0):
    def step(i, carry):
        fn(i)
        return carry

    lax.fori_loop(first, count, step, 0)


def normal_rows(values):
    centre = jnp.mean(values, axis=-1, keepdims=True)
    centred = values - centre
    scale = lax.rsqrt(jnp.mean(centred * centred, axis=-1, keepdims=True) + 1e-06)
    return centred * scale, scale


def normal_back(gradient, normal, scale, gain):
    e = gradient * gain
    return scale * (
        e - jnp.mean(e, axis=-1, keepdims=True) - normal * jnp.mean(e * normal, axis=-1, keepdims=True)
    )


def block_kernel(tp, dp, names, *refs):
    r = dict(zip(names, refs))
    place = Place(tp, dp)
    me, c, one_bit, two_bit = place.me, place.c, place.bit_one, place.bit_two
    x, cot, fill, vec = r["x"], r["cot"], r["fill"], r["vec"]
    rel, relt = r["rel"], r["relt"]
    a, b, ga = r["a"], r["b"], r["ga"]
    normed, q, k, v, mix = r["normed"], r["q"], r["k"], r["v"], r["mix"]
    middle, total, slide = r["middle"], r["total"], r["slide"]
    normed_two, turned_two, hid, dbs = r["normed_two"], r["turned_two"], r["hid"], r["dbs"]
    early, late, bias = r["early"], r["late"], r["bias"]
    rows_all, width = x.shape
    held_units = r["p"].shape[0]
    part = a.shape[2]
    pieces = b.shape[1] // 2
    units = pieces * width
    windows = rows_all // PAD
    half_rows = rows_all // 2
    columns = width // TILE
    tiles = units // TILE
    halves_of_rows = [slice(0, half_rows), slice(half_rows, rows_all)]
    blocks = []
    for window in range(windows // 2):
        for start in range(0, part, LANES):
            blocks.append((window, start, min(2, (part - start) // HALF)))

    weights = [a, b]
    own_copy = [pltpu.make_async_copy(r["own_a"], a.at[me, 0:3], r["local"].at[0])]
    own_copy.append(pltpu.make_async_copy(r["own_p"], a.at[me, 3:4], r["local"].at[5]))
    own_copy.append(pltpu.make_async_copy(r["own_f"], b.at[me, 0:pieces], r["local"].at[1]))
    own_copy.append(pltpu.make_async_copy(r["own_g"], b.at[me, pieces:], r["local"].at[2]))
    own_copy.append(pltpu.make_async_copy(r["x_in"], hid.at[: r["x_in"].shape[0], :width], r["local"].at[3]))
    own_copy.append(pltpu.make_async_copy(r["cot_in"], dbs.at[: r["x_in"].shape[0], :width], r["local"].at[4]))

    def z_copy(w, other, arriving):
        owner = other if arriving else me
        view = piece(weights[w].at[owner], place.flips()[0], c)
        return remote(view, view, r["z_send"].at[w, other], r["z_recv"].at[w, owner], (place.d, other))

    def bias_copy(other, arriving):
        owner = other if arriving else me
        return remote(bias.at[owner], bias.at[owner], r["b_send"].at[other], r["b_recv"].at[owner], (place.d, other))

    def spread(w, s):
        return Spread(place, weights[w].at[s], r["p_send"], r["p_recv"], (w, s))

    def send(w, j):
        z_copy(w, place.other(tp - j), False).start()

    def first(w, j):
        z_copy(w, place.other(j), True).wait_recv()
        spread(w, place.other(j)).start_own()

    def second(w, j):
        spread(w, place.other(j)).after_first()

    def third(w, j):
        spread(w, place.other(j)).after_second()

    def ready(w, j):
        spread(w, place.other(j)).ready()

    def sent(w, j):
        spread(w, place.other(j)).sent()

    def z_sent(w):
        repeat(tp, lambda j: z_copy(w, place.other(j), False).wait_send(), 1)

    grads = [ga, b]
    halves, quarters, eighths, arrived, final = ([r[name + str(w)] for w in range(2)] for name in ("h", "u", "e", "t", "o"))
    outs = [r["out_a"], r["out_b"]]

    def rows_of(block, size):
        return pl.ds(pl.multiple_of(block * size, size), size)

    def lanes_of(w, side):
        count = grads[w].shape[-1] // 2
        return pl.ds(pl.multiple_of(side * count, count), count)

    def core_copy(w, s):
        return remote(
            grads[w].at[s, :, :, lanes_of(w, 1 - c)],
            halves[w].at[s],
            r["core_send"].at[w, s],
            r["core_recv"].at[w, s],
            (place.core, me),
        )

    def quarter_copy(w, s):
        size = quarters[w].shape[2]
        return remote(
            halves[w].at[s, :, rows_of(1 - one_bit, size)],
            quarters[w].at[s],
            r["one_send"].at[w, s],
            r["one_recv"].at[w, s],
            (place.first, me),
        )

    def eighth_copy(w, s):
        size = eighths[w].shape[2]
        return remote(
            quarters[w].at[s, :, rows_of(1 - two_bit, size)],
            eighths[w].at[s],
            r["two_send"].at[w, s],
            r["two_recv"].at[w, s],
            (place.second, me),
        )

    def shard_copy(w, other, arriving):
        owner = other if arriving else me
        return remote(
            eighths[w].at[other], arrived[w].at[owner], r["s_send"].at[w, other], r["s_recv"].at[w, owner], (place.d, other)
        )

    def reduce_one(w, s):
        core_copy(w, s).start()

    def reduce_two(w, s):
        core_copy(w, s).wait_recv()
        size = quarters[w].shape[2]

        def add(block):
            rows = rows_of(block, size)
            halves[w][s, :, rows] += grads[w][s, :, rows, lanes_of(w, c)]

        add(1 - one_bit)
        quarter_copy(w, s).start()
        add(one_bit)

    def reduce_three(w, s):
        size = eighths[w].shape[2]
        quarter_copy(w, s).wait_recv()

        def add(two):
            rows = rows_of(two, size)
            quarters[w][s, :, rows] += halves[w][s, :, rows_of(2 * one_bit + two, size)]

        add(1 - two_bit)
        eighth_copy(w, s).start()
        add(two_bit)

    def reduce_four(w, j):
        s = place.other(j)
        eighth_copy(w, s).wait_recv()
        eighths[w][s] += quarters[w][s, :, rows_of(two_bit, eighths[w].shape[2])]
        if j > 0:
            shard_copy(w, s, False).start()

    def out_spread(w):
        return Spread(place, outs[w], r["q_send"], r["q_recv"], (w,))

    def reduce_five(w):
        repeat(tp, lambda j: shard_copy(w, place.other(j), True).wait_recv(), 1)
        arrived[w][me] = eighths[w][me]
        value = arrived[w][0].astype(f32)
        for s in range(1, tp):
            value += arrived[w][s].astype(f32)
        final[w][...] = value.astype(bf16)
        for i, peer in enumerate(place.extra):
            copy = remote(final[w], r["x" + str(w)].at[i], r["x_send"].at[w, i], r["x_recv"].at[w, i], (peer, me))
            copy.start()
            copy.wait()
            final[w][...] += r["x" + str(w)][i]
        put = pltpu.make_async_copy(final[w], piece(outs[w], place.flips()[0], c), r["put"].at[w])
        put.start()
        put.wait()
        out_spread(w).start_own()

    def reduce_done(w):
        out_spread(w).ready()
        out_spread(w).sent()

        def one(j):
            s = place.other(j)
            core_copy(w, s).wait_send()
            quarter_copy(w, s).wait_send()
            eighth_copy(w, s).wait_send()

        repeat(tp, one)
        repeat(tp, lambda j: shard_copy(w, place.other(j), False).wait_send(), 1)

    levels = [place.core, place.x, place.y] + place.extra
    table = r["table"]
    small = [[r["early"]], [r["late"], r["fold"]]]
    small_in = [[r["early_in"]], [r["late_in"], r["fold_in"]]]
    small_z = [[r["early_z"]], [r["late_z"], r["fold_z"]]]
    small_out = [[r["early_out"]], [r["late_out"], r["fold_out"]]]

    def small_copy(group, i, level):
        at = group + i
        return remote(
            small[group][i],
            small_in[group][i].at[level],
            r["v_send"].at[at, level],
            r["v_recv"].at[at, level],
            (levels[level], me),
        )

    def small_start(group):
        for i in range(len(small[group])):
            small_copy(group, i, 0).start()

    def small_level(group, level):
        for i in range(len(small[group])):
            small_copy(group, i, level).wait()
            small[group][i][...] += small_in[group][i][level]
            if level + 1 < len(levels):
                small_copy(group, i, level + 1).start()

    def small_shard(group, i, other, arriving):
        owner = other if arriving else me
        at = group + i
        return remote(
            small[group][i], small_z[group][i].at[owner], r["vz_send"].at[at, other], r["vz_recv"].at[at, owner], (place.d, other)
        )

    def small_across(group):
        for level in range(2, len(levels)):
            small_level(group, level)
        for i in range(len(small[group])):
            repeat(tp, lambda j: small_shard(group, i, place.other(j), False).start(), 1)

    def small_finish(group):
        for i in range(len(small[group])):
            repeat(tp, lambda j: small_shard(group, i, place.other(j), True).wait_recv(), 1)
            landed = small_z[group][i]
            landed[me] = small[group][i][...]
            value = landed[0]
            for s in range(1, tp):
                value += landed[s]
            small_out[group][i][...] = value

    def small_sent():
        for group in range(2):
            for i in range(len(small[group])):
                repeat(tp, lambda j: small_shard(group, i, place.other(j), False).wait_send(), 1)

    def chunk(i):
        return pl.ds(pl.multiple_of(i * CHUNK, CHUNK), CHUNK)

    chunks = rows_all // CHUNK

    def keep_rows(rows, count):
        keep = (fill[rows] == 0.0).astype(f32)
        return jnp.concatenate([keep] * (count // LANES), axis=1)

    def fill_rows(i):
        row = i * CHUNK + lax.broadcasted_iota(jnp.int32, (CHUNK, LANES), 0)
        window = sum((row >= PAD * at).astype(jnp.int32) for at in range(1, windows))
        inside = row - PAD * window
        down = (inside * 4682) >> 16
        across = inside - WIN * down
        window = me * windows + window
        lower = window // GRID if GRID & (GRID - 1) else window >> (GRID.bit_length() - 1)
        kept = (lower * WIN + down < r["heights"][0]) & ((window - lower * GRID) * WIN + across < r["widths"][0])
        value = jnp.where(kept, 0.0, neg_fill)
        fill[chunk(i)] = jnp.where(inside < SLOTS, value, pad_fill).astype(f32)

    def norm_one(i):
        rows = chunk(i)
        normal, _ = normal_rows(x[rows].astype(f32))
        normed[rows] = (normal * vec[0:1] + vec[2:3]).astype(bf16)

    def project(s):
        for t, target in enumerate((q, k, v)):
            for rows in halves_of_rows:
                value = dot(normed[rows], a[s, t], NT)
                if t != 1:
                    value = value + bias[s, t // 2 : 1 + t // 2, :part]
                target[s, rows, :part] = value.astype(bf16)

    def unit_view(ref, s, at):
        return ref.at[s, pl.ds(pl.multiple_of(at * half_rows, half_rows), half_rows)]

    def p_out(i):
        return pltpu.make_async_copy(r["p"].at[i % held_units], r["p_hbm"].at[i], r["p_sem"].at[i % held_units])

    def p_in(i):
        return pltpu.make_async_copy(r["p_hbm"].at[i], r["p"].at[i % held_units], r["p_sem"].at[i % held_units])

    def attend(i, s, at):
        attend_forward_unit(
            unit_view(q, s, at),
            unit_view(k, s, at),
            unit_view(v, s, at),
            unit_view(mix, s, at),
            r["p"].at[i % held_units],
            fill.at[pl.ds(pl.multiple_of(at * half_rows, half_rows), half_rows)],
            rel,
            r["hot"],
            r["scr_a"],
            blocks,
        )

    def attend_back(i, s, at):
        views = [unit_view(ref, s, at) for ref in (q, k, v)]
        attend_backward_unit(
            *views, unit_view(mix, s, at), r["p"].at[i % held_units], *views, table, relt, r["hott"], r["scr_b"], blocks
        )

    def mix_out(n):
        tile = pl.ds(pl.multiple_of(n * TILE, TILE), TILE)
        for rows in halves_of_rows:
            value = dot(mix[0, rows, :part], a[0, 3, :, tile])
            for s in range(1, tp):
                value = value + dot(mix[s, rows, :part], a[s, 3, :, tile])
            middle[rows, tile] = x[rows, tile].astype(f32) + keep_rows(rows, TILE) * (value + vec[4:5, tile])

    def norm_two(i):
        rows = chunk(i)
        value = middle[rows]
        normal, _ = normal_rows(value)
        normed_two[rows] = (normal * vec[1:2] + vec[3:4]).astype(bf16)
        total[rows] = value + keep_rows(rows, width) * vec[5:6]
        slide[rows] = jnp.zeros_like(value)

    def tile_of(n):
        inner = n if pieces == 1 else n % columns
        block = 0 if pieces == 1 else n // columns
        return pl.ds(pl.multiple_of(n * TILE, TILE), TILE), block, pl.ds(pl.multiple_of(inner * TILE, TILE), TILE)

    def layers(s, j):
        def one(n):
            run("layers", j * tiles + n)
            tile, block, inner = tile_of(n)
            column = None
            for rows in halves_of_rows:
                before = dot(normed_two[rows], b[s, block, :, inner]) + bias[s, pl.ds(2 + block, 1), inner]
                keep = keep_rows(rows, TILE)
                phi = 0.5 * (1.0 + lax.erf(before * root_half))
                hid[rows, tile] = (before * phi * keep).astype(bf16)
                slope = phi + before * (jnp.exp(-0.5 * before * before) * bell)
                down = (slope * (dot(cot[rows], b[s, pieces + block, inner, :], NT) * keep)).astype(bf16)
                dbs[rows, tile] = down
                part_sum = jnp.sum(down.astype(f32), axis=0, keepdims=True)
                column = part_sum if column is None else column + part_sum
            early[pl.ds(4 + s * pieces + block, 1), inner] = column

        repeat(tiles, one)

    def layers_add(s, j):
        def one(n):
            run("add", j * columns + n)
            tile = pl.ds(pl.multiple_of(n * TILE, TILE), TILE)
            for rows in halves_of_rows:
                for i in range(pieces):
                    part_of = slice(i * width, (i + 1) * width)
                    total[rows, tile] += dot(hid[rows, part_of], b[s, pieces + i, :, tile])
                    slide[rows, tile] += dot(dbs[rows, part_of], b[s, i, tile, :], NT)

        repeat(columns, one)

    def layers_grad(s, j):
        def one(n):
            run("grad", j * tiles + n)
            tile, block, inner = tile_of(n)
            b[s, pieces + block, inner, :] = dot(hid[:, tile], cot[...], TN).astype(bf16)
            b[s, block, :, inner] = dot(turned_two[...], dbs[:, tile]).astype(bf16)

        repeat(tiles, one)

    def middle_back(i):
        rows = chunk(i)
        hid[rows, :width] = total[rows].astype(bf16)
        keep = keep_rows(rows, width)
        gradient = slide[rows]
        normal, scale = normal_rows(middle[rows])
        outer = cot[rows].astype(f32)
        down = outer + normal_back(gradient, normal, scale, vec[1:2])
        slide[rows] = down
        masked = down * keep
        dbs[rows, :width] = masked.astype(bf16)
        total[rows] = jnp.zeros_like(down)
        for at, value in enumerate((gradient * normal, gradient, masked, outer * keep)):
            early[at : at + 1] = early[at : at + 1] + jnp.sum(value, axis=0, keepdims=True)

    def mix_back(s):
        ga[s, 3] = dot(mix[s, :, :part], dbs[:, :width], TN).astype(bf16)
        for rows in halves_of_rows:
            mix[s, rows, :part] = dot(dbs[rows, :width], a[s, 3], NT).astype(bf16)

    def project_grad(s):
        turned = jnp.concatenate([source[s, :, :part].T for source in (q, k, v)], axis=0)
        for n in range(columns):
            tile = slice(n * TILE, (n + 1) * TILE)
            ga[s, 0:3, :, tile] = dot(turned, normed[:, tile]).astype(bf16).reshape(3, part, TILE)

    def project_back(s):
        for i, source in ((0, q), (1, v)):
            value = jnp.sum(source[s, :, :part].astype(f32), axis=0, keepdims=True)
            first_lane = i * (width // 2)
            late[pl.ds(2 + s, 1), first_lane : first_lane + part] = value

        def one(n):
            tile = pl.ds(pl.multiple_of(n * TILE, TILE), TILE)
            for rows in halves_of_rows:
                total[rows, tile] += (
                    dot(q[s, rows, :part], a[s, 0, :, tile])
                    + dot(k[s, rows, :part], a[s, 1, :, tile])
                    + dot(v[s, rows, :part], a[s, 2, :, tile])
                )

        repeat(columns, one)

    def input_back(i):
        rows = chunk(i)
        gradient = total[rows]
        normal, scale = normal_rows(x[rows].astype(f32))
        middle[rows] = slide[rows] + normal_back(gradient, normal, scale, vec[0:1])
        late[0:1] = late[0:1] + jnp.sum(gradient * normal, axis=0, keepdims=True)
        late[1:2] = late[1:2] + jnp.sum(gradient, axis=0, keepdims=True)

    last = tp - 1
    plan = make_plan(tp, tiles, columns)

    def run(name, index=0):
        if isinstance(index, int):
            for fn, *args in plan.get(name, {}).get(index, []):
                do[fn](*args)
            return
        for at, steps in sorted(plan.get(name, {}).items()):

            @pl.when(index == at)
            def _(steps=steps):
                for fn, *args in steps:
                    do[fn](*args)

    def bias_ready():
        repeat(tp, lambda j: bias_copy(place.other(j), True).wait_recv(), 1)

    turn_of = lambda w, j: last - j if w == 0 else j
    do = dict(
        send=send,
        first=first,
        second=second,
        third=third,
        ready=ready,
        sent=sent,
        bias_ready=bias_ready,
        one=lambda w, j: reduce_one(w, place.other(turn_of(w, j))),
        two=lambda w, j: reduce_two(w, place.other(turn_of(w, j))),
        three=lambda w, j: reduce_three(w, place.other(turn_of(w, j))),
        four=lambda w, j: reduce_four(w, turn_of(w, j)),
        z_sent=z_sent,
        five=reduce_five,
        after_first=lambda w: out_spread(w).after_first(),
        after_second=lambda w: out_spread(w).after_second(),
        s0=small_start,
        s1=lambda group: small_level(group, 0),
        s2=lambda group: small_level(group, 1),
        s3=small_across,
        s4=small_finish,
        done=reduce_done,
    )

    place.greet_start()
    for copy in own_copy:
        copy.start()
    vec[...] = jnp.zeros_like(vec)
    for at, name in ((0, "gain"), (2, "shift")):
        vec[at : at + 2] = r[name][...].astype(f32)
    vec[4] = r["b_proj"][...].astype(f32)
    vec[5] = r["b_fc2"][...].astype(f32)
    vec[8:10, :part] = r["b_qv"][...].astype(f32)
    for i in range(pieces):
        vec[10 + i] = r["b_fc1"][i * width : (i + 1) * width].astype(f32)
    bias[me] = vec[8:16]
    offsets = r["offsets"]
    offsets[...] = jnp.zeros_like(offsets)
    for at in range(2 * WIN - 1):
        pair = r["rel_pos"][at].astype(f32)
        for axis in range(2):
            offsets[32 * axis + at : 32 * axis + at + 1, :HEAD_DIM] = pair[axis : axis + 1]
    offsets[...] = offsets[...] + pltpu.roll(offsets[...], HALF, 1)
    for copy in own_copy:
        copy.wait()
    place.greet_wait()
    run("start")
    repeat(tp, lambda j: bias_copy(place.other(tp - j), False).start(), 1)
    slots = r["x_in"].shape[0] // windows

    def unpack_rows(staged, target):
        for window in range(windows):
            target[window * PAD : window * PAD + slots] = staged[window * slots : (window + 1) * slots, :width]
            target[window * PAD + slots : (window + 1) * PAD] = jnp.zeros((PAD - slots, width), bf16)

    unpack_rows(hid, x)
    run("warm", 0)
    repeat(chunks, norm_one)
    run("warm", 1)
    repeat(chunks, fill_rows)
    picked = dot(r["pick"][...], offsets[...].astype(bf16))
    lane = lax.broadcasted_iota(jnp.int32, picked.shape, 1)
    head = lax.broadcasted_iota(jnp.int32, picked.shape, 0)
    picked = jnp.where((lane < HALF) == (head < HALF), picked, 0.0)
    rel[...] = picked.astype(bf16)
    relt[...] = (picked * 0.125).T.astype(bf16)
    lead = part - part % LANES
    if lead < part:
        for ref in (q, k, v, mix):
            for s in range(tp):
                ref[s, :, lead:] = jnp.zeros((rows_all, LANES), bf16)
    for ref in (early, late, table, r["scr_b"]):
        ref[...] = jnp.zeros_like(ref)

    def forward_unit(i):
        j, at = i // 2, i % 2
        s = place.other(j)

        @pl.when(at == 0)
        def _():
            run("project", j)
            project(s)

        run("unit", i)

        @pl.when(i >= held_units)
        def _():
            p_out(i - held_units).wait()

        attend(i, s, at)

        @pl.when(i < unit_count - held_units)
        def _():
            p_out(i).start()

    unit_count = 2 * tp
    repeat(unit_count, forward_unit)
    run("mid")
    repeat(columns, mix_out)
    run("mid1")
    repeat(chunks, norm_two)
    turned_two[...] = normed_two[...].T
    unpack_rows(dbs, cot)

    def layer_step(j):
        s = place.other(j)
        layers(s, j)
        layers_add(s, j)
        layers_grad(s, j)
        run("layer3", j)

    repeat(tp, layer_step)

    for at in range(2):
        run("down0", at)
        repeat(chunks * (at + 1) // 2, middle_back, chunks * at // 2)
    for window in range(windows):
        normed_two[window * slots : (window + 1) * slots] = hid[window * PAD : window * PAD + slots, :width]
    put_out = pltpu.make_async_copy(normed_two.at[: windows * slots], r["out"], r["local"].at[1])
    put_out.start()
    run("down1")
    repeat(tp, lambda j: mix_back(place.other(j)))
    run("down2")

    def backward_unit(i):
        j, at = i // 2, i % 2
        s = place.other(last - j)
        unit = 2 * (last - j) + at
        run("back", i)

        @pl.when(unit < unit_count - held_units)
        def _():
            p_in(unit).wait()

        attend_back(unit, s, at)

        @pl.when(unit >= held_units)
        def _():
            p_in(unit - held_units).start()

        @pl.when(at == 1)
        def _():
            run("turn", j)
            project_grad(s)
            run("shard", j)
            project_back(s)
            run("after", j)

    repeat(unit_count, backward_unit)
    for at in range(4):
        run("end" + str(at))
        repeat(chunks * (at + 1) // 4, input_back, chunks * at // 4)
    for window in range(windows):
        total[window * slots : (window + 1) * slots] = middle[window * PAD : window * PAD + slots]
    put_in = pltpu.make_async_copy(total.at[: windows * slots], r["grad_x"], r["local"].at[2])
    put_in.start()
    r["fold"][:, :HALF] = table[:32, :HALF] + table[HALF : HALF + 32, HALF:]
    r["fold"][:, HALF:] = table[32:HALF, :HALF] + table[HALF + 32 :, HALF:]
    for at in range(4, ENDS):
        run("end" + str(at))
    for j in range(1, tp):
        sent(0, j)
    z_sent(0)
    small_sent()
    repeat(tp, lambda j: bias_copy(place.other(tp - j), False).wait_send(), 1)
    put_out.wait()
    put_in.wait()


def make_plan(tp, tiles, columns):
    plan = {}
    if PLACES and (tp, tiles, columns) == (4, 3, 3):
        for place, index, *steps in PLACES:
            plan.setdefault(place, {})[index] = steps
        return plan

    def at(place, index, *step):
        if place in ("layer0", "layer1", "layer2"):
            place, count = dict(layer0=("layers", tiles), layer1=("add", columns), layer2=("grad", tiles))[place]
            index *= count
        plan.setdefault(place, {}).setdefault(index, []).append(step)

    others = list(range(1, tp))
    arrivals = [(w, j) for w in (0, 1) for j in others]
    order = [("unit", 1)]
    for j in others:
        order += [("project", j), ("unit", 2 * j), ("unit", 2 * j + 1)]
    order.append(("mid", 0))
    order += [("layer" + str(stage), j) for j in range(tp) for stage in range(4)]
    slots = len(arrivals) + 2
    own_end = order.index(("layer3", 0))
    marks = [s * own_end // (slots - 1) for s in range(slots)]
    need = {0: "project", 1: "layer0"}
    limit = len(order) - 1
    for slot in reversed(range(slots)):
        if slot >= 2:
            w, j = arrivals[slot - 2]
            limit = min(limit, order.index((need[w], j)))
        limit = min(limit, marks[slot])
        marks = marks[:slot] + [limit] + marks[slot + 1 :]
    for ahead in range(min(2, len(arrivals))):
        at("start", 0, "send", *arrivals[ahead])
    for slot in range(slots):
        for name, behind in (("third", 2), ("second", 1), ("first", 0)):
            if 0 <= slot - behind < len(arrivals):
                at(*order[marks[slot]], name, *arrivals[slot - behind])
        if slot + 2 < len(arrivals):
            at(*order[marks[slot]], "send", *arrivals[slot + 2])
    if tp > 1:
        at("project", 1, "bias_ready")
        at("layer2", 0, "z_sent", 1)
    for j in others:
        at("project", j, "ready", 0, j)
        at("layer0", j, "ready", 1, j)
        at("layer2", j, "sent", 1, j)

    last = tp - 1
    for j in range(tp):
        at("layer3", j, "one", 1, j)
    for j in range(tp):
        at(*(("layer1", j + 1) if j < last else ("down1", 0)), "two", 1, j)
    for j in range(tp):
        at(*(("layer1", j + 2) if j + 2 <= last else ("down1", 0) if j < last else ("shard", 0)), "three", 1, j)
    for j in range(tp):
        where = ("layer1", j + 3) if j + 3 <= last else ("down1", 0) if j + 2 <= last else ("back", 1) if j < last else ("turn", min(1, last))
        at(*where, "four", 1, j)
    late = lambda n: ("shard", n) if n <= last else ("end0", 0)
    at(*late(1), "five", 1)
    at(*late(2), "after_first", 1)
    at(*late(3), "after_second", 1)

    for j in range(tp):
        at("shard", j, "one", 0, j)
    for j in range(tp):
        at(*(("back", 2 * j + 3) if j < last else ("end4", 0)), "two", 0, j)
    for j in range(tp):
        at(*(("shard", j + 1) if j < last else ("end6", 0)), "three", 0, j)
    for j in range(tp):
        at(*(("back", 2 * j + 5) if j + 2 <= last else ("end0", 0) if j < last else ("end7", 0)), "four", 0, j)
    for group, places in enumerate((("down2", "end0", "end1", "end2", "end3"), ("end4", "end5", "end6", "end7", "end8"))):
        for step, place in enumerate(places):
            at(place, 0, "s" + str(step), group)
    at("end9", 0, "five", 0)
    at("end9", 0, "after_first", 0)
    at("end10", 0, "after_second", 0)
    at("end11", 0, "done", 1)
    at("end11", 0, "done", 0)
    return plan


def whole_block(tp, dp, x, cot, heights, widths, gain, shift, b_qv, b_proj, b_fc1, b_fc2, rel_pos, own_a, own_p, own_f, own_g):
    width = x.shape[1]
    windows = x.shape[0] // SLOTS
    rows = windows * PAD
    part = own_a.shape[1]
    pieces = own_f.shape[0]
    units = pieces * width
    heads = (windows // 2) * (part // HEAD_DIM)
    wide = -(-part // LANES) * LANES
    unit_count = 2 * tp
    held_units = 4 if dp <= 8 else 2
    hot, hott, pick = window_constants()
    scalar = pl.BlockSpec(memory_space=pltpu.SMEM)
    any_space = pl.BlockSpec(memory_space=pl.ANY)
    vmem = pl.BlockSpec(memory_space=pltpu.VMEM)
    dma = pltpu.SemaphoreType.DMA
    inputs = [
        ("x_in", x, any_space),
        ("cot_in", cot, any_space),
        ("heights", heights, scalar),
        ("widths", widths, scalar),
        ("gain", gain, vmem),
        ("shift", shift, vmem),
        ("b_qv", b_qv, vmem),
        ("b_proj", b_proj, vmem),
        ("b_fc1", b_fc1, vmem),
        ("b_fc2", b_fc2, vmem),
        ("rel_pos", rel_pos, vmem),
        ("own_a", own_a, any_space),
        ("own_p", own_p, any_space),
        ("own_f", own_f, any_space),
        ("own_g", own_g, any_space),
        ("hot", hot, vmem),
        ("hott", hott, vmem),
        ("pick", pick, vmem),
    ]
    shape = jax.ShapeDtypeStruct
    outputs = [
        ("out", shape(x.shape, bf16), any_space),
        ("grad_x", shape(x.shape, f32), any_space),
        ("out_a", shape((4, part, width), bf16), any_space),
        ("out_b", shape((2 * pieces, width, width), bf16), any_space),
        ("early_out", shape((8, width), f32), vmem),
        ("late_out", shape((8, width), f32), vmem),
        ("fold_out", shape((32, LANES), f32), vmem),
        ("p_hbm", shape((max(unit_count - held_units, 1), heads, PAD, PAD), bf16), any_space),
    ]
    buffer = lambda dims, kind: pltpu.VMEM(tuple(dims), kind)
    scratch = [
        ("a", buffer((tp, 4, part, width), bf16)),
        ("b", buffer((tp, 2 * pieces, width, width), bf16)),
        ("ga", buffer((tp, 4, part, width), bf16)),
        ("bias", buffer((tp, 8, width), f32)),
        ("x", buffer((rows, width), bf16)),
        ("cot", buffer((rows, width), bf16)),
        ("fill", buffer((rows, LANES), f32)),
        ("vec", buffer((16, width), f32)),
        ("offsets", buffer((HALF, LANES), f32)),
        ("rel", buffer((LANES, LANES), bf16)),
        ("relt", buffer((LANES, LANES), bf16)),
        ("normed", buffer((rows, width), bf16)),
    ]
    scratch += [(name, buffer((tp, rows, wide), bf16)) for name in ("q", "k", "v", "mix")]
    scratch += [("p", buffer((held_units, heads, PAD, PAD), bf16))]
    scratch += [(name, buffer((rows, width), f32)) for name in ("middle", "total", "slide")]
    scratch += [("normed_two", buffer((rows, width), bf16)), ("turned_two", buffer((width, rows), bf16))]
    scratch += [(name, buffer((rows, units), bf16)) for name in ("hid", "dbs")]
    scratch += [
        ("early", buffer((8, width), f32)),
        ("late", buffer((8, width), f32)),
        ("table", buffer((LANES, LANES), f32)),
        ("fold", buffer((32, LANES), f32)),
        ("scr_a", buffer((heads, HALF, PAD), f32)),
        ("scr_b", buffer((heads, 2, 48, PAD), f32)),
    ]
    levels = dp.bit_length() - 1
    more = levels - 3
    for w, own in enumerate(((4, part, width), (2 * pieces, width, width))):
        n, count, lanes = own[0], own[1], own[2] // 2
        scratch += [
            ("h" + str(w), buffer((tp, n, count, lanes), bf16)),
            ("u" + str(w), buffer((tp, n, count // 2, lanes), bf16)),
            ("e" + str(w), buffer((tp, n, count // 4, lanes), bf16)),
            ("t" + str(w), buffer((tp, n, count // 4, lanes), bf16)),
            ("o" + str(w), buffer((n, count // 4, lanes), bf16)),
        ]
        if more:
            scratch += [("x" + str(w), buffer((more, n, count // 4, lanes), bf16))]
    for name, dims in (("early", (8, width)), ("late", (8, width)), ("fold", (32, LANES))):
        scratch += [(name + "_in", buffer((levels,) + dims, f32)), (name + "_z", buffer((tp,) + dims, f32))]
    semaphores = dict(local=(6,), p_sem=(held_units,), put=(2,))
    for name, dims in dict(
        z=(2, tp), p=(2, tp, 4), b=(tp,), core=(2, tp), one=(2, tp), two=(2, tp), s=(2, tp), q=(2, 4), x=(2, max(more, 1)), v=(3, levels), vz=(3, tp)
    ).items():
        semaphores[name + "_send"] = semaphores[name + "_recv"] = dims
    scratch += [(name, dma(dims)) for name, dims in semaphores.items()]
    names = [entry[0] for entry in inputs + outputs + scratch]
    return pl.pallas_call(
        lambda *refs: block_kernel(tp, dp, names, *refs),
        in_specs=[entry[2] for entry in inputs],
        out_specs=[entry[2] for entry in outputs],
        out_shape=[entry[1] for entry in outputs],
        scratch_shapes=[entry[1] for entry in scratch],
        compiler_params=pltpu.CompilerParams(collective_id=1, has_side_effects=True, vmem_limit_bytes=VMEM_LIMIT),
    )(*[entry[1] for entry in inputs])


def finish_kernel(
    a_ref, b_ref, o_ref, x_ref, early, late, fold, qkv, proj, fc1, fc2, o, x, gain, shift, qv, rel, b_proj, b_fc1, b_fc2, *scratch
):
    a, b, wide_qkv, wide_proj, wide_fc1, wide_fc2, held_o, held_x, sem_in, sem_out = scratch
    pieces = b.shape[0] // 2
    width = b.shape[1]
    part = a.shape[1]
    me = lax.axis_index("tp")
    loads = [pltpu.make_async_copy(b_ref.at[i], b.at[i], sem_in.at[i]) for i in range(2 * pieces)]
    loads += [pltpu.make_async_copy(a_ref.at[i], a.at[i], sem_in.at[2 * pieces + i]) for i in range(4)]
    loads.append(pltpu.make_async_copy(o_ref, held_o, sem_in.at[2 * pieces + 4]))
    loads.append(pltpu.make_async_copy(x_ref, held_x, sem_in.at[2 * pieces + 5]))
    for copy in loads:
        copy.start()
    stores = []

    def store(value, out):
        copy = pltpu.make_async_copy(value, out, sem_out.at[len(stores)])
        copy.start()
        stores.append(copy)

    count = 2 * WIN - 1
    gain[0:1], gain[1:2] = late[0:1], early[0:1]
    shift[0:1], shift[1:2] = late[1:2], early[1:2]
    mine = late[pl.ds(2 + me, 1), :]
    qv[0:1], qv[1:2] = mine[:, :part], mine[:, width // 2 : width // 2 + part]
    for at in range(count):
        for axis in range(2):
            rel[at, axis : axis + 1, :] = fold[count - 1 - at : count - at, axis * HALF : (axis + 1) * HALF]
    b_proj[...] = early[2]
    b_fc2[...] = early[3]
    for i in range(pieces):
        b_fc1[i * width : (i + 1) * width] = early[pl.ds(4 + me * pieces + i, 1), :].reshape(width)
    for i in range(pieces):
        loads[i].wait()
        wide_fc1[:, i * width : (i + 1) * width] = b[i].astype(f32)
    store(wide_fc1, fc1)
    for i in range(pieces):
        loads[pieces + i].wait()
        wide_fc2[i * width : (i + 1) * width, :] = b[pieces + i].astype(f32)
    store(wide_fc2, fc2)
    for t in range(3):
        loads[2 * pieces + t].wait()
        wide_qkv[t] = a[t].astype(f32)
        store(wide_qkv.at[t], qkv.at[t])
    loads[2 * pieces + 3].wait()
    wide_proj[...] = a[3].astype(f32)
    store(wide_proj, proj)
    loads[2 * pieces + 4].wait()
    store(held_o, o)
    loads[2 * pieces + 5].wait()
    store(held_x, x)
    for copy in stores:
        copy.wait()


def finish(out_a, out_b, out, grad_x, early, late, fold):
    part, width = out_a.shape[1:]
    pieces = out_b.shape[0] // 2
    units = pieces * width
    any_space = pl.BlockSpec(memory_space=pl.ANY)
    vmem = pl.BlockSpec(memory_space=pltpu.VMEM)
    large = [(3, part, width), (part, width), (width, units), (units, width)]
    small = [(2, width), (2, width), (2, part), (2 * WIN - 1, 2, HEAD_DIM), (width,), (units,), (width,)]
    shape = jax.ShapeDtypeStruct
    return pl.pallas_call(
        finish_kernel,
        in_specs=[any_space] * 4 + [vmem] * 3,
        out_specs=[any_space] * 6 + [vmem] * 7,
        out_shape=[shape(dims, f32) for dims in large]
        + [shape(out.shape, bf16), shape(grad_x.shape, f32)]
        + [shape(dims, f32) for dims in small],
        scratch_shapes=[pltpu.VMEM(out_a.shape, bf16), pltpu.VMEM(out_b.shape, bf16)]
        + [pltpu.VMEM(dims, f32) for dims in large]
        + [pltpu.VMEM(out.shape, bf16), pltpu.VMEM(grad_x.shape, f32)]
        + [pltpu.SemaphoreType.DMA((2 * pieces + 6,)), pltpu.SemaphoreType.DMA((8,))],
        compiler_params=pltpu.CompilerParams(vmem_limit_bytes=VMEM_LIMIT),
    )(out_a, out_b, out, grad_x, early, late, fold)


def body(
    tokens,
    heights,
    widths,
    norm_gain,
    norm_bias,
    w_qkv,
    b_qv,
    rel_pos,
    w_proj,
    b_proj,
    w_fc1,
    b_fc1,
    w_fc2,
    b_fc2,
    cotangent,
):
    tp, dp = lax.axis_size("tp"), lax.axis_size("dp")
    width = tokens.shape[1]
    part, units = w_qkv.shape[2], w_fc1.shape[1]
    blocks = units // width
    first = w_fc1[None] if blocks == 1 else w_fc1.reshape(width, blocks, width).transpose(1, 0, 2)
    out, grad_x, out_a, out_b, early, late, fold, _ = whole_block(
        tp,
        dp,
        tokens,
        cotangent,
        heights,
        widths,
        norm_gain,
        norm_bias,
        b_qv,
        b_proj,
        b_fc1,
        b_fc2,
        rel_pos.transpose(1, 0, 2),
        w_qkv.transpose(0, 2, 1),
        w_proj[None],
        first,
        w_fc2.reshape(blocks, width, width),
    )
    qkv, proj, fc1, fc2, out, grad_x, gain, shift, qv, rel, proj_bias, fc1_bias, fc2_bias = finish(
        out_a, out_b, out, grad_x, early, late, fold
    )
    return (
        out,
        grad_x,
        gain,
        shift,
        qkv.transpose(0, 2, 1),
        qv,
        rel.transpose(1, 0, 2),
        proj,
        proj_bias,
        fc1,
        fc1_bias,
        fc2,
        fc2_bias,
    )


def solution(mesh):
    rows = P(("dp", "tp"), None)
    return jax.shard_map(
        body,
        mesh=mesh,
        in_specs=(
            rows,
            P("dp"),
            P("dp"),
            P(),
            P(),
            P(None, None, "tp"),
            P(None, "tp"),
            P(),
            P("tp", None),
            P(),
            P(None, "tp"),
            P("tp"),
            P("tp", None),
            P(),
            rows,
        ),
        out_specs=(
            rows,
            rows,
            P(),
            P(),
            P(None, None, "tp"),
            P(None, "tp"),
            P(),
            P("tp", None),
            P(),
            P(None, "tp"),
            P("tp"),
            P("tp", None),
            P(),
        ),
        check_vma=False,
    )
```

```python
import jax
import jax.numpy as jnp
import ml_dtypes
import numpy as np
from jax import lax
from jax.experimental import pallas as pl
from jax.experimental.pallas import tpu as pltpu
from jax.sharding import PartitionSpec as P

HEAD_DIM = 64
WIN = 14
GRID = 4
SLOTS = WIN * WIN
PAD = 208
LANES = 128
HALF = 64
CHUNK = 32
ENDS = 20
PLACES = [
    ("start", 0, ("send", 0, 1)),
    ("warm", 0, ("send", 0, 2), ("first", 0, 1), ("send", 0, 3), ("second", 0, 1)),
    ("warm", 1, ("send", 1, 1), ("first", 0, 2)),
    ("project", 0, ("first", 0, 3)),
    ("unit", 0, ("send", 1, 3), ("third", 0, 1)),
    ("project", 1, ("bias_ready",), ("ready", 0, 1), ("second", 0, 2)),
    ("unit", 3, ("second", 0, 3), ("third", 0, 2)),
    ("project", 2, ("first", 1, 1), ("send", 1, 2), ("ready", 0, 2)),
    ("unit", 4, ("third", 0, 3)),
    ("project", 3, ("first", 1, 3), ("ready", 0, 3)),
    ("mid1", 0, ("second", 1, 1)),
    ("layers", 0, ("first", 1, 2)),
    ("add", 0, ("third", 1, 1)),
    ("grad", 0, ("z_sent", 1)),
    ("layer3", 0, ("second", 1, 2), ("one", 1, 0)),
    ("layers", 3, ("ready", 1, 1)),
    ("add", 4, ("second", 1, 3)),
    ("grad", 3, ("third", 1, 2), ("two", 1, 0), ("sent", 1, 1)),
    ("layer3", 1, ("ready", 1, 2)),
    ("layers", 6, ("one", 1, 1)),
    ("layers", 8, ("third", 1, 3)),
    ("add", 7, ("two", 1, 1)),
    ("grad", 6, ("sent", 1, 2)),
    ("layer3", 2, ("one", 1, 2), ("ready", 1, 3)),
    ("add", 10, ("two", 1, 2), ("three", 1, 1)),
    ("grad", 9, ("sent", 1, 3)),
    ("layer3", 3, ("one", 1, 3)),
    ("down0", 1, ("two", 1, 3)),
    ("down2", 0, ("three", 1, 2)),
    ("back", 0, ("s0", 0), ("four", 1, 1)),
    ("turn", 0, ("three", 1, 3)),
    ("shard", 0, ("one", 0, 0)),
    ("after", 0, ("four", 1, 2), ("three", 1, 0)),
    ("back", 3, ("s1", 0), ("two", 0, 0)),
    ("back", 4, ("four", 1, 3), ("one", 0, 1)),
    ("turn", 2, ("s2", 0), ("two", 0, 1)),
    ("shard", 2, ("one", 0, 2)),
    ("after", 2, ("four", 1, 0)),
    ("back", 6, ("two", 0, 2)),
    ("turn", 3, ("three", 0, 1), ("three", 0, 0)),
    ("shard", 3, ("one", 0, 3), ("three", 0, 2)),
    ("end0", 0, ("s3", 0), ("two", 0, 3), ("five", 1), ("four", 0, 1)),
    ("end1", 0, ("four", 0, 0)),
    ("end2", 0, ("s4", 0), ("four", 0, 2)),
    ("end4", 0, ("s0", 1), ("s1", 1), ("three", 0, 3), ("s2", 1), ("after_first", 1), ("s3", 1), ("four", 0, 3), ("five", 0), ("after_second", 1), ("s4", 1), ("done", 1), ("after_first", 0), ("after_second", 0), ("done", 0)),
]
TILE = 256

bf16 = jnp.bfloat16
f32 = jnp.float32
neg_fill = -30000.0
pad_fill = -1e30
root_half = 0.7071067811865476
bell = 0.3989422804014327
VMEM_LIMIT = 64 << 20
MESH = pl.DeviceIdType.MESH


def dot(a, b, dims=((1,), (0,))):
    return lax.dot_general(a, b, (dims, ((), ())), preferred_element_type=f32)


NT = ((1,), (1,))
TN = ((0,), (0,))


def window_constants():
    slot = np.arange(PAD)[:, None]
    lane = np.arange(HALF)[None, :]
    place = np.where(lane % 32 < 16, slot // WIN, slot % WIN)
    hot = ((slot < SLOTS) & (lane % 16 == place)).astype(np.float32)
    zero = np.zeros_like(hot)
    both = np.concatenate([np.concatenate([hot, zero], 1), np.concatenate([zero, hot], 1)], 0)
    pick = np.zeros((LANES, HALF), np.float32)
    for offset in range(2 * WIN - 1):
        for head in range(2):
            for axis in range(2):
                pick[HALF * head + 32 * axis + offset, 32 * axis + 2 * WIN - 2 - offset] = 8.0
    narrow = lambda values: values.astype(ml_dtypes.bfloat16)
    return narrow(both), narrow(hot[:, :32].T.copy()), narrow(pick)


def stack_heads(pair, heads):
    if heads == 1:
        return pair
    lane = lax.broadcasted_iota(jnp.int32, pair.shape, 1)
    zero = jnp.zeros_like(pair)
    return jnp.concatenate([jnp.where(lane < HALF, pair, zero), jnp.where(lane < HALF, zero, pair)], axis=0)


def merge_heads(stacked, heads):
    if heads == 1:
        return stacked
    top, bottom = stacked[:PAD], stacked[PAD:]
    lane = lax.broadcasted_iota(jnp.int32, top.shape, 1)
    return jnp.where(lane < HALF, top, bottom)


def place_of_lane():
    lane = lax.broadcasted_iota(jnp.int32, (1, PAD), 1)
    row = lax.div(lane, WIN)
    return row, lane - row * WIN


def attend_forward_unit(q_ref, k_ref, v_ref, mix_ref, p_ref, fill_ref, rel_ref, hot_ref, scr_ref, blocks):
    places = place_of_lane()
    eighth = jnp.asarray(0.125, bf16)
    firsts, scores, biases = [], [], []
    count = 0
    for window, start, heads in blocks:
        firsts.append(count)
        lanes, rows = slice(start, start + LANES), slice(window * PAD, (window + 1) * PAD)
        left = jnp.concatenate([rel_ref[: heads * HALF], stack_heads(k_ref[rows, lanes], heads)], axis=0)
        both = dot(left, q_ref[rows, lanes] * eighth, NT)
        for head in range(heads):
            scr_ref[count + head] = both[head * HALF : (head + 1) * HALF]
        scores.append(both[heads * HALF :])
        count += heads
    for b, (window, start, heads) in enumerate(blocks):
        parts = []
        for head in range(heads):
            along = []
            for base, place in ((0, places[0]), (32, places[1])):
                picked = scr_ref[firsts[b] + head, base : base + 16, :]
                for at in range(WIN - 1):
                    first = base + WIN - 1 - at
                    picked = jnp.where(place == at, scr_ref[firsts[b] + head, first : first + 16, :], picked)
                along.append(picked)
            bias = jnp.concatenate(along, axis=0)
            high = bias.astype(bf16)
            parts += [high, (bias - high.astype(f32)).astype(bf16)]
        biases.append(jnp.concatenate(parts, axis=0))
    for b, (window, start, heads) in enumerate(blocks):
        scores[b] = scores[b] + dot(hot_ref[: heads * PAD, : heads * HALF], biases[b])
    for b, (window, start, heads) in enumerate(blocks):
        fill = fill_ref[window * PAD : (window + 1) * PAD]
        fill = jnp.concatenate([fill, fill[:, : PAD - LANES]], axis=1)
        for head in range(heads):
            one = scores[b][head * PAD : (head + 1) * PAD]
            one = jnp.where(fill == 0.0, one, fill)
            weights = jnp.exp(one - jnp.max(one, axis=0, keepdims=True))
            total = jnp.sum(weights, axis=0, keepdims=True)
            p_ref[firsts[b] + head] = (weights * (1.0 / total)).astype(bf16)
    for b, (window, start, heads) in enumerate(blocks):
        lanes, rows = slice(start, start + LANES), slice(window * PAD, (window + 1) * PAD)
        turned = v_ref[rows, lanes].T
        parts = [
            dot(turned[head * HALF : (head + 1) * HALF], p_ref[firsts[b] + head]).astype(bf16) for head in range(heads)
        ]
        if heads == 1:
            parts.append(jnp.zeros_like(parts[0]))
        mix_ref[rows, lanes] = jnp.concatenate(parts, axis=0).T


def attend_backward_unit(
    q_ref, k_ref, v_ref, d_ref, p_ref, dq_ref, dk_ref, dv_ref, table_ref, relt_ref, hott_ref, scr_ref, blocks
):
    places = place_of_lane()
    eighth = jnp.asarray(0.125, bf16)
    firsts, d_attn, d_scores, sums, offsets = [], [], [], [], []
    count = 0
    for window, start, heads in blocks:
        firsts.append(count)
        lanes, rows = slice(start, start + LANES), slice(window * PAD, (window + 1) * PAD)
        d_attn.append(dot(stack_heads(v_ref[rows, lanes], heads), d_ref[rows, lanes], NT))
        count += heads
    for b, (window, start, heads) in enumerate(blocks):
        lanes, rows = slice(start, start + LANES), slice(window * PAD, (window + 1) * PAD)
        soft = p_ref[firsts[b] : firsts[b] + heads].reshape(heads * PAD, PAD)
        dv_ref[rows, lanes] = merge_heads(dot(soft, d_ref[rows, lanes]), heads).astype(bf16)
    for b, (window, start, heads) in enumerate(blocks):
        parts = []
        for head in range(heads):
            soft = p_ref[firsts[b] + head].astype(f32)
            weighted = d_attn[b][head * PAD : (head + 1) * PAD] * soft
            inner = jnp.sum(weighted, axis=0, keepdims=True)
            parts.append((weighted - soft * inner).astype(bf16))
        d_scores.append(parts)
    for b, (window, start, heads) in enumerate(blocks):
        lanes, rows = slice(start, start + LANES), slice(window * PAD, (window + 1) * PAD)
        turned_k = k_ref[rows, lanes].T * eighth
        parts = []
        for head in range(heads):
            left = jnp.concatenate([turned_k[head * HALF : (head + 1) * HALF], hott_ref[...]], axis=0)
            both = dot(left, d_scores[b][head])
            for axis in range(2):
                scr_ref[firsts[b] + head, axis, 16:32, :] = both[HALF + 16 * axis : HALF + 16 * axis + 16]
            parts.append(both[:HALF])
        sums.append(parts)
    for b, (window, start, heads) in enumerate(blocks):
        spread = []
        for head in range(heads):
            for axis in range(2):
                picked = scr_ref[firsts[b] + head, axis, 16:48, :]
                for at in range(WIN - 1):
                    picked = jnp.where(places[axis] == at, scr_ref[firsts[b] + head, axis, 3 + at : 35 + at, :], picked)
                spread.append(picked)
        offsets.append(jnp.concatenate(spread, axis=0).astype(bf16))
    for b, (window, start, heads) in enumerate(blocks):
        lanes, rows = slice(start, start + LANES), slice(window * PAD, (window + 1) * PAD)
        right = dot(jnp.concatenate(d_scores[b] + [offsets[b]], axis=0), q_ref[rows, lanes])
        dk_ref[rows, lanes] = (merge_heads(right[: heads * PAD], heads) * 0.125).astype(bf16)
        table_ref[: heads * HALF] += right[heads * PAD :]
        extra = dot(relt_ref[:, : heads * HALF], offsets[b])
        turned = jnp.concatenate(sums[b] if heads == 2 else sums[b] + [jnp.zeros_like(sums[b][0])], axis=0) + extra
        turned = turned.astype(bf16)
        dq_ref[rows, lanes] = turned.T


class Place:
    def __init__(self, tp, dp):
        self.tp, self.dp = tp, dp
        self.d, self.me = lax.axis_index("dp"), lax.axis_index("tp")
        c, x, y = self.d % 2, (self.d // 2) % 2, (self.d // 4) % 2
        self.c = c
        self.core = self.d + 1 - 2 * c
        peer_x, peer_y = self.d + 2 - 4 * x, self.d + 4 - 8 * y
        self.x, self.y = peer_x, peer_y
        self.first = peer_x * (1 - c) + peer_y * c
        self.second = peer_y * (1 - c) + peer_x * c
        self.bit_one = x * (1 - c) + y * c
        self.bit_two = y * (1 - c) + x * c
        self.extra = []
        for bit in range(3, dp.bit_length() - 1):
            step = 1 << bit
            self.extra.append(self.d + step * (1 - 2 * ((self.d // step) % 2)))

    def flips(self):
        a, b = self.bit_one, self.bit_two
        return [2 * a + b, 2 * (1 - a) + b, 2 * a + 1 - b, 2 * (1 - a) + 1 - b]

    def other(self, step):
        return (self.me + step) % self.tp

    def greet_start(self):
        barrier = pltpu.get_barrier_semaphore()
        for peer in [self.core, self.x, self.y] + self.extra:
            pl.semaphore_signal(barrier, inc=1, device_id=(peer, self.me), device_id_type=MESH)

        def signal(step, carry):
            pl.semaphore_signal(barrier, inc=1, device_id=(self.d, self.other(step)), device_id_type=MESH)
            return carry

        lax.fori_loop(1, self.tp, signal, 0)

    def greet_wait(self):
        pl.semaphore_wait(pltpu.get_barrier_semaphore(), 3 + len(self.extra) + self.tp - 1)


def piece(ref, block, c):
    rows, columns = ref.shape[-2] // 4, ref.shape[-1] // 2
    lead = (slice(None),) * (len(ref.shape) - 2)
    return ref.at[
        lead + (pl.ds(pl.multiple_of(block * rows, rows), rows), pl.ds(pl.multiple_of(c * columns, columns), columns))
    ]


def remote(src, dst, send, recv, device):
    return pltpu.make_async_remote_copy(
        src_ref=src, dst_ref=dst, send_sem=send, recv_sem=recv, device_id=device, device_id_type=MESH
    )


class Spread:
    def __init__(self, place, ref, send, recv, at):
        self.place, self.ref, self.send, self.recv, self.at = place, ref, send, recv, at

    def copy(self, k, arriving):
        place = self.place
        flips = place.flips()
        index = tuple(self.at) + (k,)
        if k == 3:
            columns = self.ref.shape[-1] // 2
            side = 1 - place.c if arriving else place.c
            lead = (slice(None),) * (len(self.ref.shape) - 1)
            view = self.ref.at[lead + (pl.ds(pl.multiple_of(side * columns, columns), columns),)]
            device = place.core
        else:
            device, block, came = (
                (place.first, flips[0], flips[1]) if k == 0 else (place.second, flips[k - 1], flips[k + 1])
            )
            view = piece(self.ref, came if arriving else block, place.c)
        return remote(view, view, self.send.at[index], self.recv.at[index], (device, place.me))

    def start_own(self):
        for k in (0, 1):
            self.copy(k, False).start()

    def after_first(self):
        self.copy(0, True).wait_recv()
        self.copy(2, False).start()

    def after_second(self):
        for k in (1, 2):
            self.copy(k, True).wait_recv()
        self.copy(3, False).start()

    def ready(self):
        self.copy(3, True).wait_recv()

    def sent(self):
        for k in range(4):
            self.copy(k, False).wait_send()


def repeat(count, fn, first=0):
    def step(i, carry):
        fn(i)
        return carry

    lax.fori_loop(first, count, step, 0)


def normal_rows(values):
    centre = jnp.mean(values, axis=-1, keepdims=True)
    centred = values - centre
    scale = lax.rsqrt(jnp.mean(centred * centred, axis=-1, keepdims=True) + 1e-06)
    return centred * scale, scale


def normal_back(gradient, normal, scale, gain):
    e = gradient * gain
    return scale * (
        e - jnp.mean(e, axis=-1, keepdims=True) - normal * jnp.mean(e * normal, axis=-1, keepdims=True)
    )


def block_kernel(tp, dp, names, *refs):
    r = dict(zip(names, refs))
    place = Place(tp, dp)
    me, c, one_bit, two_bit = place.me, place.c, place.bit_one, place.bit_two
    x, cot, fill, vec = r["x"], r["cot"], r["fill"], r["vec"]
    rel, relt = r["rel"], r["relt"]
    a, b, ga = r["a"], r["b"], r["ga"]
    normed, q, k, v, mix = r["normed"], r["q"], r["k"], r["v"], r["mix"]
    middle, total, slide = r["middle"], r["total"], r["slide"]
    normed_two, turned_two, hid, dbs = r["normed_two"], r["turned_two"], r["hid"], r["dbs"]
    early, late, bias = r["early"], r["late"], r["bias"]
    rows_all, width = x.shape
    held_units = r["p"].shape[0]
    part = a.shape[2]
    pieces = b.shape[1] // 2
    units = pieces * width
    windows = rows_all // PAD
    half_rows = rows_all // 2
    columns = width // TILE
    tiles = units // TILE
    halves_of_rows = [slice(0, half_rows), slice(half_rows, rows_all)]
    blocks = []
    for window in range(windows // 2):
        for start in range(0, part, LANES):
            blocks.append((window, start, min(2, (part - start) // HALF)))

    weights = [a, b]
    own_copy = [pltpu.make_async_copy(r["own_a"], a.at[me, 0:3], r["local"].at[0])]
    own_copy.append(pltpu.make_async_copy(r["own_p"], a.at[me, 3:4], r["local"].at[5]))
    own_copy.append(pltpu.make_async_copy(r["own_f"], b.at[me, 0:pieces], r["local"].at[1]))
    own_copy.append(pltpu.make_async_copy(r["own_g"], b.at[me, pieces:], r["local"].at[2]))
    own_copy.append(pltpu.make_async_copy(r["x_in"], hid.at[: r["x_in"].shape[0], :width], r["local"].at[3]))
    own_copy.append(pltpu.make_async_copy(r["cot_in"], dbs.at[: r["x_in"].shape[0], :width], r["local"].at[4]))

    def z_copy(w, other, arriving):
        owner = other if arriving else me
        view = piece(weights[w].at[owner], place.flips()[0], c)
        return remote(view, view, r["z_send"].at[w, other], r["z_recv"].at[w, owner], (place.d, other))

    def bias_copy(other, arriving):
        owner = other if arriving else me
        return remote(bias.at[owner], bias.at[owner], r["b_send"].at[other], r["b_recv"].at[owner], (place.d, other))

    def spread(w, s):
        return Spread(place, weights[w].at[s], r["p_send"], r["p_recv"], (w, s))

    def send(w, j):
        z_copy(w, place.other(tp - j), False).start()

    def first(w, j):
        z_copy(w, place.other(j), True).wait_recv()
        spread(w, place.other(j)).start_own()

    def second(w, j):
        spread(w, place.other(j)).after_first()

    def third(w, j):
        spread(w, place.other(j)).after_second()

    def ready(w, j):
        spread(w, place.other(j)).ready()

    def sent(w, j):
        spread(w, place.other(j)).sent()

    def z_sent(w):
        repeat(tp, lambda j: z_copy(w, place.other(j), False).wait_send(), 1)

    grads = [ga, b]
    halves, quarters, eighths, arrived, final = ([r[name + str(w)] for w in range(2)] for name in ("h", "u", "e", "t", "o"))
    outs = [r["out_a"], r["out_b"]]

    def rows_of(block, size):
        return pl.ds(pl.multiple_of(block * size, size), size)

    def lanes_of(w, side):
        count = grads[w].shape[-1] // 2
        return pl.ds(pl.multiple_of(side * count, count), count)

    def core_copy(w, s):
        return remote(
            grads[w].at[s, :, :, lanes_of(w, 1 - c)],
            halves[w].at[s],
            r["core_send"].at[w, s],
            r["core_recv"].at[w, s],
            (place.core, me),
        )

    def quarter_copy(w, s):
        size = quarters[w].shape[2]
        return remote(
            halves[w].at[s, :, rows_of(1 - one_bit, size)],
            quarters[w].at[s],
            r["one_send"].at[w, s],
            r["one_recv"].at[w, s],
            (place.first, me),
        )

    def eighth_copy(w, s):
        size = eighths[w].shape[2]
        return remote(
            quarters[w].at[s, :, rows_of(1 - two_bit, size)],
            eighths[w].at[s],
            r["two_send"].at[w, s],
            r["two_recv"].at[w, s],
            (place.second, me),
        )

    def shard_copy(w, other, arriving):
        owner = other if arriving else me
        return remote(
            eighths[w].at[other], arrived[w].at[owner], r["s_send"].at[w, other], r["s_recv"].at[w, owner], (place.d, other)
        )

    def reduce_one(w, s):
        core_copy(w, s).start()

    def reduce_two(w, s):
        core_copy(w, s).wait_recv()
        size = quarters[w].shape[2]

        def add(block):
            rows = rows_of(block, size)
            halves[w][s, :, rows] += grads[w][s, :, rows, lanes_of(w, c)]

        add(1 - one_bit)
        quarter_copy(w, s).start()
        add(one_bit)

    def reduce_three(w, s):
        size = eighths[w].shape[2]
        quarter_copy(w, s).wait_recv()

        def add(two):
            rows = rows_of(two, size)
            quarters[w][s, :, rows] += halves[w][s, :, rows_of(2 * one_bit + two, size)]

        add(1 - two_bit)
        eighth_copy(w, s).start()
        add(two_bit)

    def reduce_four(w, j):
        s = place.other(j)
        eighth_copy(w, s).wait_recv()
        eighths[w][s] += quarters[w][s, :, rows_of(two_bit, eighths[w].shape[2])]
        if j > 0:
            shard_copy(w, s, False).start()

    def out_spread(w):
        return Spread(place, outs[w], r["q_send"], r["q_recv"], (w,))

    def reduce_five(w):
        repeat(tp, lambda j: shard_copy(w, place.other(j), True).wait_recv(), 1)
        arrived[w][me] = eighths[w][me]
        value = arrived[w][0].astype(f32)
        for s in range(1, tp):
            value += arrived[w][s].astype(f32)
        final[w][...] = value.astype(bf16)
        for i, peer in enumerate(place.extra):
            copy = remote(final[w], r["x" + str(w)].at[i], r["x_send"].at[w, i], r["x_recv"].at[w, i], (peer, me))
            copy.start()
            copy.wait()
            final[w][...] += r["x" + str(w)][i]
        put = pltpu.make_async_copy(final[w], piece(outs[w], place.flips()[0], c), r["put"].at[w])
        put.start()
        put.wait()
        out_spread(w).start_own()

    def reduce_done(w):
        out_spread(w).ready()
        out_spread(w).sent()

        def one(j):
            s = place.other(j)
            core_copy(w, s).wait_send()
            quarter_copy(w, s).wait_send()
            eighth_copy(w, s).wait_send()

        repeat(tp, one)
        repeat(tp, lambda j: shard_copy(w, place.other(j), False).wait_send(), 1)

    levels = [place.core, place.x, place.y] + place.extra
    table = r["table"]
    small = [[r["early"]], [r["late"], r["fold"]]]
    small_in = [[r["early_in"]], [r["late_in"], r["fold_in"]]]
    small_z = [[r["early_z"]], [r["late_z"], r["fold_z"]]]
    small_out = [[r["early_out"]], [r["late_out"], r["fold_out"]]]

    def small_copy(group, i, level):
        at = group + i
        return remote(
            small[group][i],
            small_in[group][i].at[level],
            r["v_send"].at[at, level],
            r["v_recv"].at[at, level],
            (levels[level], me),
        )

    def small_start(group):
        for i in range(len(small[group])):
            small_copy(group, i, 0).start()

    def small_level(group, level):
        for i in range(len(small[group])):
            small_copy(group, i, level).wait()
            small[group][i][...] += small_in[group][i][level]
            if level + 1 < len(levels):
                small_copy(group, i, level + 1).start()

    def small_shard(group, i, other, arriving):
        owner = other if arriving else me
        at = group + i
        return remote(
            small[group][i], small_z[group][i].at[owner], r["vz_send"].at[at, other], r["vz_recv"].at[at, owner], (place.d, other)
        )

    def small_across(group):
        for level in range(2, len(levels)):
            small_level(group, level)
        for i in range(len(small[group])):
            repeat(tp, lambda j: small_shard(group, i, place.other(j), False).start(), 1)

    def small_finish(group):
        for i in range(len(small[group])):
            repeat(tp, lambda j: small_shard(group, i, place.other(j), True).wait_recv(), 1)
            landed = small_z[group][i]
            landed[me] = small[group][i][...]
            value = landed[0]
            for s in range(1, tp):
                value += landed[s]
            small_out[group][i][...] = value

    def small_sent():
        for group in range(2):
            for i in range(len(small[group])):
                repeat(tp, lambda j: small_shard(group, i, place.other(j), False).wait_send(), 1)

    def chunk(i):
        return pl.ds(pl.multiple_of(i * CHUNK, CHUNK), CHUNK)

    chunks = rows_all // CHUNK

    def keep_rows(rows, count):
        keep = (fill[rows] == 0.0).astype(f32)
        return jnp.concatenate([keep] * (count // LANES), axis=1)

    def fill_rows(i):
        row = i * CHUNK + lax.broadcasted_iota(jnp.int32, (CHUNK, LANES), 0)
        window = sum((row >= PAD * at).astype(jnp.int32) for at in range(1, windows))
        inside = row - PAD * window
        down = (inside * 4682) >> 16
        across = inside - WIN * down
        window = me * windows + window
        lower = window // GRID if GRID & (GRID - 1) else window >> (GRID.bit_length() - 1)
        kept = (lower * WIN + down < r["heights"][0]) & ((window - lower * GRID) * WIN + across < r["widths"][0])
        value = jnp.where(kept, 0.0, neg_fill)
        fill[chunk(i)] = jnp.where(inside < SLOTS, value, pad_fill).astype(f32)

    def norm_one(i):
        rows = chunk(i)
        normal, _ = normal_rows(x[rows].astype(f32))
        normed[rows] = (normal * vec[0:1] + vec[2:3]).astype(bf16)

    def project(s):
        for t, target in enumerate((q, k, v)):
            for rows in halves_of_rows:
                value = dot(normed[rows], a[s, t], NT)
                if t != 1:
                    value = value + bias[s, t // 2 : 1 + t // 2, :part]
                target[s, rows, :part] = value.astype(bf16)

    def unit_view(ref, s, at):
        return ref.at[s, pl.ds(pl.multiple_of(at * half_rows, half_rows), half_rows)]

    def p_out(i):
        return pltpu.make_async_copy(r["p"].at[i % held_units], r["p_hbm"].at[i], r["p_sem"].at[i % held_units])

    def p_in(i):
        return pltpu.make_async_copy(r["p_hbm"].at[i], r["p"].at[i % held_units], r["p_sem"].at[i % held_units])

    def attend(i, s, at):
        attend_forward_unit(
            unit_view(q, s, at),
            unit_view(k, s, at),
            unit_view(v, s, at),
            unit_view(mix, s, at),
            r["p"].at[i % held_units],
            fill.at[pl.ds(pl.multiple_of(at * half_rows, half_rows), half_rows)],
            rel,
            r["hot"],
            r["scr_a"],
            blocks,
        )

    def attend_back(i, s, at):
        views = [unit_view(ref, s, at) for ref in (q, k, v)]
        attend_backward_unit(
            *views, unit_view(mix, s, at), r["p"].at[i % held_units], *views, table, relt, r["hott"], r["scr_b"], blocks
        )

    def mix_out(n):
        tile = pl.ds(pl.multiple_of(n * TILE, TILE), TILE)
        for rows in halves_of_rows:
            value = dot(mix[0, rows, :part], a[0, 3, :, tile])
            for s in range(1, tp):
                value = value + dot(mix[s, rows, :part], a[s, 3, :, tile])
            middle[rows, tile] = x[rows, tile].astype(f32) + keep_rows(rows, TILE) * (value + vec[4:5, tile])

    def norm_two(i):
        rows = chunk(i)
        value = middle[rows]
        normal, _ = normal_rows(value)
        normed_two[rows] = (normal * vec[1:2] + vec[3:4]).astype(bf16)
        total[rows] = value + keep_rows(rows, width) * vec[5:6]
        slide[rows] = jnp.zeros_like(value)

    def tile_of(n):
        inner = n if pieces == 1 else n % columns
        block = 0 if pieces == 1 else n // columns
        return pl.ds(pl.multiple_of(n * TILE, TILE), TILE), block, pl.ds(pl.multiple_of(inner * TILE, TILE), TILE)

    def layers(s, j):
        def one(n):
            run("layers", j * tiles + n)
            tile, block, inner = tile_of(n)
            column = None
            for rows in halves_of_rows:
                before = dot(normed_two[rows], b[s, block, :, inner]) + bias[s, pl.ds(2 + block, 1), inner]
                keep = keep_rows(rows, TILE)
                phi = 0.5 * (1.0 + lax.erf(before * root_half))
                hid[rows, tile] = (before * phi * keep).astype(bf16)
                slope = phi + before * (jnp.exp(-0.5 * before * before) * bell)
                down = (slope * (dot(cot[rows], b[s, pieces + block, inner, :], NT) * keep)).astype(bf16)
                dbs[rows, tile] = down
                part_sum = jnp.sum(down.astype(f32), axis=0, keepdims=True)
                column = part_sum if column is None else column + part_sum
            early[pl.ds(4 + s * pieces + block, 1), inner] = column

        repeat(tiles, one)

    def layers_add(s, j):
        def one(n):
            run("add", j * columns + n)
            tile = pl.ds(pl.multiple_of(n * TILE, TILE), TILE)
            for rows in halves_of_rows:
                for i in range(pieces):
                    part_of = slice(i * width, (i + 1) * width)
                    total[rows, tile] += dot(hid[rows, part_of], b[s, pieces + i, :, tile])
                    slide[rows, tile] += dot(dbs[rows, part_of], b[s, i, tile, :], NT)

        repeat(columns, one)

    def layers_grad(s, j):
        def one(n):
            run("grad", j * tiles + n)
            tile, block, inner = tile_of(n)
            b[s, pieces + block, inner, :] = dot(hid[:, tile], cot[...], TN).astype(bf16)
            b[s, block, :, inner] = dot(turned_two[...], dbs[:, tile]).astype(bf16)

        repeat(tiles, one)

    def middle_back(i):
        rows = chunk(i)
        hid[rows, :width] = total[rows].astype(bf16)
        keep = keep_rows(rows, width)
        gradient = slide[rows]
        normal, scale = normal_rows(middle[rows])
        outer = cot[rows].astype(f32)
        down = outer + normal_back(gradient, normal, scale, vec[1:2])
        slide[rows] = down
        masked = down * keep
        dbs[rows, :width] = masked.astype(bf16)
        total[rows] = jnp.zeros_like(down)
        for at, value in enumerate((gradient * normal, gradient, masked, outer * keep)):
            early[at : at + 1] = early[at : at + 1] + jnp.sum(value, axis=0, keepdims=True)

    def mix_back(s):
        ga[s, 3] = dot(mix[s, :, :part], dbs[:, :width], TN).astype(bf16)
        for rows in halves_of_rows:
            mix[s, rows, :part] = dot(dbs[rows, :width], a[s, 3], NT).astype(bf16)

    def project_grad(s):
        turned = jnp.concatenate([source[s, :, :part].T for source in (q, k, v)], axis=0)
        for n in range(columns):
            tile = slice(n * TILE, (n + 1) * TILE)
            ga[s, 0:3, :, tile] = dot(turned, normed[:, tile]).astype(bf16).reshape(3, part, TILE)

    def project_back(s):
        for i, source in ((0, q), (1, v)):
            value = jnp.sum(source[s, :, :part].astype(f32), axis=0, keepdims=True)
            first_lane = i * (width // 2)
            late[pl.ds(2 + s, 1), first_lane : first_lane + part] = value

        def one(n):
            tile = pl.ds(pl.multiple_of(n * TILE, TILE), TILE)
            for rows in halves_of_rows:
                total[rows, tile] += (
                    dot(q[s, rows, :part], a[s, 0, :, tile])
                    + dot(k[s, rows, :part], a[s, 1, :, tile])
                    + dot(v[s, rows, :part], a[s, 2, :, tile])
                )

        repeat(columns, one)

    def input_back(i):
        rows = chunk(i)
        gradient = total[rows]
        normal, scale = normal_rows(x[rows].astype(f32))
        middle[rows] = slide[rows] + normal_back(gradient, normal, scale, vec[0:1])
        late[0:1] = late[0:1] + jnp.sum(gradient * normal, axis=0, keepdims=True)
        late[1:2] = late[1:2] + jnp.sum(gradient, axis=0, keepdims=True)

    last = tp - 1
    plan = make_plan(tp, tiles, columns)

    def run(name, index=0):
        if isinstance(index, int):
            for fn, *args in plan.get(name, {}).get(index, []):
                do[fn](*args)
            return
        for at, steps in sorted(plan.get(name, {}).items()):

            @pl.when(index == at)
            def _(steps=steps):
                for fn, *args in steps:
                    do[fn](*args)

    def bias_ready():
        repeat(tp, lambda j: bias_copy(place.other(j), True).wait_recv(), 1)

    turn_of = lambda w, j: last - j if w == 0 else j
    do = dict(
        send=send,
        first=first,
        second=second,
        third=third,
        ready=ready,
        sent=sent,
        bias_ready=bias_ready,
        one=lambda w, j: reduce_one(w, place.other(turn_of(w, j))),
        two=lambda w, j: reduce_two(w, place.other(turn_of(w, j))),
        three=lambda w, j: reduce_three(w, place.other(turn_of(w, j))),
        four=lambda w, j: reduce_four(w, turn_of(w, j)),
        z_sent=z_sent,
        five=reduce_five,
        after_first=lambda w: out_spread(w).after_first(),
        after_second=lambda w: out_spread(w).after_second(),
        s0=small_start,
        s1=lambda group: small_level(group, 0),
        s2=lambda group: small_level(group, 1),
        s3=small_across,
        s4=small_finish,
        done=reduce_done,
    )

    place.greet_start()
    for copy in own_copy:
        copy.start()
    vec[...] = jnp.zeros_like(vec)
    for at, name in ((0, "gain"), (2, "shift")):
        vec[at : at + 2] = r[name][...].astype(f32)
    vec[4] = r["b_proj"][...].astype(f32)
    vec[5] = r["b_fc2"][...].astype(f32)
    vec[8:10, :part] = r["b_qv"][...].astype(f32)
    for i in range(pieces):
        vec[10 + i] = r["b_fc1"][i * width : (i + 1) * width].astype(f32)
    bias[me] = vec[8:16]
    offsets = r["offsets"]
    offsets[...] = jnp.zeros_like(offsets)
    for at in range(2 * WIN - 1):
        pair = r["rel_pos"][at].astype(f32)
        for axis in range(2):
            offsets[32 * axis + at : 32 * axis + at + 1, :HEAD_DIM] = pair[axis : axis + 1]
    offsets[...] = offsets[...] + pltpu.roll(offsets[...], HALF, 1)
    for copy in own_copy:
        copy.wait()
    place.greet_wait()
    run("start")
    repeat(tp, lambda j: bias_copy(place.other(tp - j), False).start(), 1)
    slots = r["x_in"].shape[0] // windows

    def unpack_rows(staged, target):
        for window in range(windows):
            target[window * PAD : window * PAD + slots] = staged[window * slots : (window + 1) * slots, :width]
            target[window * PAD + slots : (window + 1) * PAD] = jnp.zeros((PAD - slots, width), bf16)

    unpack_rows(hid, x)
    run("warm", 0)
    repeat(chunks, norm_one)
    run("warm", 1)
    repeat(chunks, fill_rows)
    picked = dot(r["pick"][...], offsets[...].astype(bf16))
    lane = lax.broadcasted_iota(jnp.int32, picked.shape, 1)
    head = lax.broadcasted_iota(jnp.int32, picked.shape, 0)
    picked = jnp.where((lane < HALF) == (head < HALF), picked, 0.0)
    rel[...] = picked.astype(bf16)
    relt[...] = (picked * 0.125).T.astype(bf16)
    lead = part - part % LANES
    if lead < part:
        for ref in (q, k, v, mix):
            for s in range(tp):
                ref[s, :, lead:] = jnp.zeros((rows_all, LANES), bf16)
    for ref in (early, late, table, r["scr_b"]):
        ref[...] = jnp.zeros_like(ref)

    def forward_unit(i):
        j, at = i // 2, i % 2
        s = place.other(j)

        @pl.when(at == 0)
        def _():
            run("project", j)
            project(s)

        run("unit", i)

        @pl.when(i >= held_units)
        def _():
            p_out(i - held_units).wait()

        attend(i, s, at)

        @pl.when(i < unit_count - held_units)
        def _():
            p_out(i).start()

    unit_count = 2 * tp
    repeat(unit_count, forward_unit)
    run("mid")
    repeat(columns, mix_out)
    run("mid1")
    repeat(chunks, norm_two)
    turned_two[...] = normed_two[...].T
    unpack_rows(dbs, cot)

    def layer_step(j):
        s = place.other(j)
        layers(s, j)
        layers_add(s, j)
        layers_grad(s, j)
        run("layer3", j)

    repeat(tp, layer_step)

    for at in range(2):
        run("down0", at)
        repeat(chunks * (at + 1) // 2, middle_back, chunks * at // 2)
    for window in range(windows):
        normed_two[window * slots : (window + 1) * slots] = hid[window * PAD : window * PAD + slots, :width]
    put_out = pltpu.make_async_copy(normed_two.at[: windows * slots], r["out"], r["local"].at[1])
    put_out.start()
    run("down1")
    repeat(tp, lambda j: mix_back(place.other(j)))
    run("down2")

    def backward_unit(i):
        j, at = i // 2, i % 2
        s = place.other(last - j)
        unit = 2 * (last - j) + at
        run("back", i)

        @pl.when(unit < unit_count - held_units)
        def _():
            p_in(unit).wait()

        attend_back(unit, s, at)

        @pl.when(unit >= held_units)
        def _():
            p_in(unit - held_units).start()

        @pl.when(at == 1)
        def _():
            run("turn", j)
            project_grad(s)
            run("shard", j)
            project_back(s)
            run("after", j)

    repeat(unit_count, backward_unit)
    for at in range(4):
        run("end" + str(at))
        repeat(chunks * (at + 1) // 4, input_back, chunks * at // 4)
    for window in range(windows):
        total[window * slots : (window + 1) * slots] = middle[window * PAD : window * PAD + slots]
    put_in = pltpu.make_async_copy(total.at[: windows * slots], r["grad_x"], r["local"].at[2])
    put_in.start()
    r["fold"][:, :HALF] = table[:32, :HALF] + table[HALF : HALF + 32, HALF:]
    r["fold"][:, HALF:] = table[32:HALF, :HALF] + table[HALF + 32 :, HALF:]
    for at in range(4, ENDS):
        run("end" + str(at))
    for j in range(1, tp):
        sent(0, j)
    z_sent(0)
    small_sent()
    repeat(tp, lambda j: bias_copy(place.other(tp - j), False).wait_send(), 1)
    put_out.wait()
    put_in.wait()


def make_plan(tp, tiles, columns):
    plan = {}
    if PLACES and (tp, tiles, columns) == (4, 3, 3):
        for place, index, *steps in PLACES:
            plan.setdefault(place, {})[index] = steps
        return plan

    def at(place, index, *step):
        if place in ("layer0", "layer1", "layer2"):
            place, count = dict(layer0=("layers", tiles), layer1=("add", columns), layer2=("grad", tiles))[place]
            index *= count
        plan.setdefault(place, {}).setdefault(index, []).append(step)

    others = list(range(1, tp))
    arrivals = [(w, j) for w in (0, 1) for j in others]
    order = [("unit", 1)]
    for j in others:
        order += [("project", j), ("unit", 2 * j), ("unit", 2 * j + 1)]
    order.append(("mid", 0))
    order += [("layer" + str(stage), j) for j in range(tp) for stage in range(4)]
    slots = len(arrivals) + 2
    own_end = order.index(("layer3", 0))
    marks = [s * own_end // (slots - 1) for s in range(slots)]
    need = {0: "project", 1: "layer0"}
    limit = len(order) - 1
    for slot in reversed(range(slots)):
        if slot >= 2:
            w, j = arrivals[slot - 2]
            limit = min(limit, order.index((need[w], j)))
        limit = min(limit, marks[slot])
        marks = marks[:slot] + [limit] + marks[slot + 1 :]
    for ahead in range(min(2, len(arrivals))):
        at("start", 0, "send", *arrivals[ahead])
    for slot in range(slots):
        for name, behind in (("third", 2), ("second", 1), ("first", 0)):
            if 0 <= slot - behind < len(arrivals):
                at(*order[marks[slot]], name, *arrivals[slot - behind])
        if slot + 2 < len(arrivals):
            at(*order[marks[slot]], "send", *arrivals[slot + 2])
    if tp > 1:
        at("project", 1, "bias_ready")
        at("layer2", 0, "z_sent", 1)
    for j in others:
        at("project", j, "ready", 0, j)
        at("layer0", j, "ready", 1, j)
        at("layer2", j, "sent", 1, j)

    last = tp - 1
    for j in range(tp):
        at("layer3", j, "one", 1, j)
    for j in range(tp):
        at(*(("layer1", j + 1) if j < last else ("down1", 0)), "two", 1, j)
    for j in range(tp):
        at(*(("layer1", j + 2) if j + 2 <= last else ("down1", 0) if j < last else ("shard", 0)), "three", 1, j)
    for j in range(tp):
        where = ("layer1", j + 3) if j + 3 <= last else ("down1", 0) if j + 2 <= last else ("back", 1) if j < last else ("turn", min(1, last))
        at(*where, "four", 1, j)
    late = lambda n: ("shard", n) if n <= last else ("end0", 0)
    at(*late(1), "five", 1)
    at(*late(2), "after_first", 1)
    at(*late(3), "after_second", 1)

    for j in range(tp):
        at("shard", j, "one", 0, j)
    for j in range(tp):
        at(*(("back", 2 * j + 3) if j < last else ("end4", 0)), "two", 0, j)
    for j in range(tp):
        at(*(("shard", j + 1) if j < last else ("end6", 0)), "three", 0, j)
    for j in range(tp):
        at(*(("back", 2 * j + 5) if j + 2 <= last else ("end0", 0) if j < last else ("end7", 0)), "four", 0, j)
    for group, places in enumerate((("down2", "end0", "end1", "end2", "end3"), ("end4", "end5", "end6", "end7", "end8"))):
        for step, place in enumerate(places):
            at(place, 0, "s" + str(step), group)
    at("end9", 0, "five", 0)
    at("end9", 0, "after_first", 0)
    at("end10", 0, "after_second", 0)
    at("end11", 0, "done", 1)
    at("end11", 0, "done", 0)
    return plan


def whole_block(tp, dp, x, cot, heights, widths, gain, shift, b_qv, b_proj, b_fc1, b_fc2, rel_pos, own_a, own_p, own_f, own_g):
    width = x.shape[1]
    windows = x.shape[0] // SLOTS
    rows = windows * PAD
    part = own_a.shape[1]
    pieces = own_f.shape[0]
    units = pieces * width
    heads = (windows // 2) * (part // HEAD_DIM)
    wide = -(-part // LANES) * LANES
    unit_count = 2 * tp
    held_units = 4 if dp <= 8 else 2
    hot, hott, pick = window_constants()
    scalar = pl.BlockSpec(memory_space=pltpu.SMEM)
    any_space = pl.BlockSpec(memory_space=pl.ANY)
    vmem = pl.BlockSpec(memory_space=pltpu.VMEM)
    dma = pltpu.SemaphoreType.DMA
    inputs = [
        ("x_in", x, any_space),
        ("cot_in", cot, any_space),
        ("heights", heights, scalar),
        ("widths", widths, scalar),
        ("gain", gain, vmem),
        ("shift", shift, vmem),
        ("b_qv", b_qv, vmem),
        ("b_proj", b_proj, vmem),
        ("b_fc1", b_fc1, vmem),
        ("b_fc2", b_fc2, vmem),
        ("rel_pos", rel_pos, vmem),
        ("own_a", own_a, any_space),
        ("own_p", own_p, any_space),
        ("own_f", own_f, any_space),
        ("own_g", own_g, any_space),
        ("hot", hot, vmem),
        ("hott", hott, vmem),
        ("pick", pick, vmem),
    ]
    shape = jax.ShapeDtypeStruct
    outputs = [
        ("out", shape(x.shape, bf16), any_space),
        ("grad_x", shape(x.shape, f32), any_space),
        ("out_a", shape((4, part, width), bf16), any_space),
        ("out_b", shape((2 * pieces, width, width), bf16), any_space),
        ("early_out", shape((8, width), f32), vmem),
        ("late_out", shape((8, width), f32), vmem),
        ("fold_out", shape((32, LANES), f32), vmem),
        ("p_hbm", shape((max(unit_count - held_units, 1), heads, PAD, PAD), bf16), any_space),
    ]
    buffer = lambda dims, kind: pltpu.VMEM(tuple(dims), kind)
    scratch = [
        ("a", buffer((tp, 4, part, width), bf16)),
        ("b", buffer((tp, 2 * pieces, width, width), bf16)),
        ("ga", buffer((tp, 4, part, width), bf16)),
        ("bias", buffer((tp, 8, width), f32)),
        ("x", buffer((rows, width), bf16)),
        ("cot", buffer((rows, width), bf16)),
        ("fill", buffer((rows, LANES), f32)),
        ("vec", buffer((16, width), f32)),
        ("offsets", buffer((HALF, LANES), f32)),
        ("rel", buffer((LANES, LANES), bf16)),
        ("relt", buffer((LANES, LANES), bf16)),
        ("normed", buffer((rows, width), bf16)),
    ]
    scratch += [(name, buffer((tp, rows, wide), bf16)) for name in ("q", "k", "v", "mix")]
    scratch += [("p", buffer((held_units, heads, PAD, PAD), bf16))]
    scratch += [(name, buffer((rows, width), f32)) for name in ("middle", "total", "slide")]
    scratch += [("normed_two", buffer((rows, width), bf16)), ("turned_two", buffer((width, rows), bf16))]
    scratch += [(name, buffer((rows, units), bf16)) for name in ("hid", "dbs")]
    scratch += [
        ("early", buffer((8, width), f32)),
        ("late", buffer((8, width), f32)),
        ("table", buffer((LANES, LANES), f32)),
        ("fold", buffer((32, LANES), f32)),
        ("scr_a", buffer((heads, HALF, PAD), f32)),
        ("scr_b", buffer((heads, 2, 48, PAD), f32)),
    ]
    levels = dp.bit_length() - 1
    more = levels - 3
    for w, own in enumerate(((4, part, width), (2 * pieces, width, width))):
        n, count, lanes = own[0], own[1], own[2] // 2
        scratch += [
            ("h" + str(w), buffer((tp, n, count, lanes), bf16)),
            ("u" + str(w), buffer((tp, n, count // 2, lanes), bf16)),
            ("e" + str(w), buffer((tp, n, count // 4, lanes), bf16)),
            ("t" + str(w), buffer((tp, n, count // 4, lanes), bf16)),
            ("o" + str(w), buffer((n, count // 4, lanes), bf16)),
        ]
        if more:
            scratch += [("x" + str(w), buffer((more, n, count // 4, lanes), bf16))]
    for name, dims in (("early", (8, width)), ("late", (8, width)), ("fold", (32, LANES))):
        scratch += [(name + "_in", buffer((levels,) + dims, f32)), (name + "_z", buffer((tp,) + dims, f32))]
    semaphores = dict(local=(6,), p_sem=(held_units,), put=(2,))
    for name, dims in dict(
        z=(2, tp), p=(2, tp, 4), b=(tp,), core=(2, tp), one=(2, tp), two=(2, tp), s=(2, tp), q=(2, 4), x=(2, max(more, 1)), v=(3, levels), vz=(3, tp)
    ).items():
        semaphores[name + "_send"] = semaphores[name + "_recv"] = dims
    scratch += [(name, dma(dims)) for name, dims in semaphores.items()]
    names = [entry[0] for entry in inputs + outputs + scratch]
    return pl.pallas_call(
        lambda *refs: block_kernel(tp, dp, names, *refs),
        in_specs=[entry[2] for entry in inputs],
        out_specs=[entry[2] for entry in outputs],
        out_shape=[entry[1] for entry in outputs],
        scratch_shapes=[entry[1] for entry in scratch],
        compiler_params=pltpu.CompilerParams(collective_id=1, has_side_effects=True, vmem_limit_bytes=VMEM_LIMIT),
    )(*[entry[1] for entry in inputs])


def finish_kernel(
    a_ref, b_ref, o_ref, x_ref, early, late, fold, qkv, proj, fc1, fc2, o, x, gain, shift, qv, rel, b_proj, b_fc1, b_fc2, *scratch
):
    a, b, wide_qkv, wide_proj, wide_fc1, wide_fc2, held_o, held_x, sem_in, sem_out = scratch
    pieces = b.shape[0] // 2
    width = b.shape[1]
    part = a.shape[1]
    me = lax.axis_index("tp")
    loads = [pltpu.make_async_copy(b_ref.at[i], b.at[i], sem_in.at[i]) for i in range(2 * pieces)]
    loads += [pltpu.make_async_copy(a_ref.at[i], a.at[i], sem_in.at[2 * pieces + i]) for i in range(4)]
    loads.append(pltpu.make_async_copy(o_ref, held_o, sem_in.at[2 * pieces + 4]))
    loads.append(pltpu.make_async_copy(x_ref, held_x, sem_in.at[2 * pieces + 5]))
    for copy in loads:
        copy.start()
    stores = []

    def store(value, out):
        copy = pltpu.make_async_copy(value, out, sem_out.at[len(stores)])
        copy.start()
        stores.append(copy)

    count = 2 * WIN - 1
    gain[0:1], gain[1:2] = late[0:1], early[0:1]
    shift[0:1], shift[1:2] = late[1:2], early[1:2]
    mine = late[pl.ds(2 + me, 1), :]
    qv[0:1], qv[1:2] = mine[:, :part], mine[:, width // 2 : width // 2 + part]
    for at in range(count):
        for axis in range(2):
            rel[at, axis : axis + 1, :] = fold[count - 1 - at : count - at, axis * HALF : (axis + 1) * HALF]
    b_proj[...] = early[2]
    b_fc2[...] = early[3]
    for i in range(pieces):
        b_fc1[i * width : (i + 1) * width] = early[pl.ds(4 + me * pieces + i, 1), :].reshape(width)
    for i in range(pieces):
        loads[i].wait()
        wide_fc1[:, i * width : (i + 1) * width] = b[i].astype(f32)
    store(wide_fc1, fc1)
    for i in range(pieces):
        loads[pieces + i].wait()
        wide_fc2[i * width : (i + 1) * width, :] = b[pieces + i].astype(f32)
    store(wide_fc2, fc2)
    for t in range(3):
        loads[2 * pieces + t].wait()
        wide_qkv[t] = a[t].astype(f32)
        store(wide_qkv.at[t], qkv.at[t])
    loads[2 * pieces + 3].wait()
    wide_proj[...] = a[3].astype(f32)
    store(wide_proj, proj)
    loads[2 * pieces + 4].wait()
    store(held_o, o)
    loads[2 * pieces + 5].wait()
    store(held_x, x)
    for copy in stores:
        copy.wait()


def finish(out_a, out_b, out, grad_x, early, late, fold):
    part, width = out_a.shape[1:]
    pieces = out_b.shape[0] // 2
    units = pieces * width
    any_space = pl.BlockSpec(memory_space=pl.ANY)
    vmem = pl.BlockSpec(memory_space=pltpu.VMEM)
    large = [(3, part, width), (part, width), (width, units), (units, width)]
    small = [(2, width), (2, width), (2, part), (2 * WIN - 1, 2, HEAD_DIM), (width,), (units,), (width,)]
    shape = jax.ShapeDtypeStruct
    return pl.pallas_call(
        finish_kernel,
        in_specs=[any_space] * 4 + [vmem] * 3,
        out_specs=[any_space] * 6 + [vmem] * 7,
        out_shape=[shape(dims, f32) for dims in large]
        + [shape(out.shape, bf16), shape(grad_x.shape, f32)]
        + [shape(dims, f32) for dims in small],
        scratch_shapes=[pltpu.VMEM(out_a.shape, bf16), pltpu.VMEM(out_b.shape, bf16)]
        + [pltpu.VMEM(dims, f32) for dims in large]
        + [pltpu.VMEM(out.shape, bf16), pltpu.VMEM(grad_x.shape, f32)]
        + [pltpu.SemaphoreType.DMA((2 * pieces + 6,)), pltpu.SemaphoreType.DMA((8,))],
        compiler_params=pltpu.CompilerParams(vmem_limit_bytes=VMEM_LIMIT),
    )(out_a, out_b, out, grad_x, early, late, fold)


def body(
    tokens,
    heights,
    widths,
    norm_gain,
    norm_bias,
    w_qkv,
    b_qv,
    rel_pos,
    w_proj,
    b_proj,
    w_fc1,
    b_fc1,
    w_fc2,
    b_fc2,
    cotangent,
):
    tp, dp = lax.axis_size("tp"), lax.axis_size("dp")
    width = tokens.shape[1]
    part, units = w_qkv.shape[2], w_fc1.shape[1]
    blocks = units // width
    first = w_fc1[None] if blocks == 1 else w_fc1.reshape(width, blocks, width).transpose(1, 0, 2)
    out, grad_x, out_a, out_b, early, late, fold, _ = whole_block(
        tp,
        dp,
        tokens,
        cotangent,
        heights,
        widths,
        norm_gain,
        norm_bias,
        b_qv,
        b_proj,
        b_fc1,
        b_fc2,
        rel_pos.transpose(1, 0, 2),
        w_qkv.transpose(0, 2, 1),
        w_proj[None],
        first,
        w_fc2.reshape(blocks, width, width),
    )
    qkv, proj, fc1, fc2, out, grad_x, gain, shift, qv, rel, proj_bias, fc1_bias, fc2_bias = finish(
        out_a, out_b, out, grad_x, early, late, fold
    )
    return (
        out,
        grad_x,
        gain,
        shift,
        qkv.transpose(0, 2, 1),
        qv,
        rel.transpose(1, 0, 2),
        proj,
        proj_bias,
        fc1,
        fc1_bias,
        fc2,
        fc2_bias,
    )


def solution(mesh):
    rows = P(("dp", "tp"), None)
    return jax.shard_map(
        body,
        mesh=mesh,
        in_specs=(
            rows,
            P("dp"),
            P("dp"),
            P(),
            P(),
            P(None, None, "tp"),
            P(None, "tp"),
            P(),
            P("tp", None),
            P(),
            P(None, "tp"),
            P("tp"),
            P("tp", None),
            P(),
            rows,
        ),
        out_specs=(
            rows,
            rows,
            P(),
            P(),
            P(None, None, "tp"),
            P(None, "tp"),
            P(),
            P("tp", None),
            P(),
            P(None, "tp"),
            P("tp"),
            P("tp", None),
            P(),
        ),
        check_vma=False,
    )
```
